512 devices in a mesh: ctx: 64 (over x, z, core), dp: 8 (over y).
Axes of the slice: x: 4, y: 8, z: 8, core: 2. Of those that a mesh axis runs over, the one named last changes fastest.
Arguments:
- hidden_in: bfloat16 [8192, 2048], P('ctx'), may hold values from -6 to 6
- query_vectors: bfloat16 [8192, 1024], P('ctx', 'dp'), may hold values from -6 to 6
- key_vectors: bfloat16 [8192, 1024], P('ctx', 'dp')
- value_vectors: bfloat16 [8192, 2048], P('ctx', 'dp'), may hold values from -6 to 6
- out_cotangent: bfloat16 [8192, 2048], P('ctx', 'dp'), may hold values from -6 to 6
- w_decay: bfloat16 [2048, 16], P(None, 'dp'), may hold values from -0.125 to 0.125
- w_beta: bfloat16 [2048, 16], P(None, 'dp'), may hold values from -0.125 to 0.125
- log_decay_rate: float32 [16], P('dp')
- step_bias: float32 [16], P('dp'), may hold values from -1 to 1
- doc_start: int32 [1], replicated, may hold values from 0 to 8191
Outputs:
- query_grad: bfloat16 [8192, 1024], P('ctx', 'dp')
- key_grad: bfloat16 [8192, 1024], P('ctx', 'dp')
- value_grad: bfloat16 [8192, 2048], P('ctx', 'dp')
- hidden_grad: bfloat16 [8192, 2048], P('ctx', 'dp')
- w_decay_grad: float32 [2048, 16], P(None, 'dp')
- w_beta_grad: float32 [2048, 16], P(None, 'dp')
- rate_grad: float32 [16], P('dp')
- bias_grad: float32 [16], P('dp')
The draws below stay inside these ranges and needn't reach their ends.
Inputs may be any that keep to these rules, and one draw needn't show every extreme that they name: `doc_start`: the state is cleared at that position.
All inputs are finite; a program needn't handle non-finite values.
Results may differ from the reference program's by a relative error of at most 0.0024.
Values may be sent and summed in bfloat16 or wider, within the bound.
No kernel may reach another device: no remote copies, remote signals or barrier semaphores. Data moves between devices by JAX's collectives and lax.ppermute only.
A program may use at most 128 MiB of HBM per device.

```python
import jax
import jax.numpy as jnp
from jax import lax

D = 2048
HV = 16
HK = 8
DK = 128
DV = 128
BLOCK = 64
TOKENS = 8192


def draw_key_vectors(key, part):
    key = jax.random.fold_in(key, 11)
    direction_key, loading_key, jitter_key = jax.random.split(key, 3)
    jitter_level = (8.0 * DK / TOKENS) ** 0.5
    directions = jax.random.normal(direction_key, (4, HK, DK), jnp.float32)
    loadings = jax.random.normal(loading_key, (4, TOKENS, HK, 1), jnp.float32)
    jitter = jax.random.normal(jitter_key, (TOKENS, HK, DK), jnp.float32)
    shared = loadings[0] * directions[0]
    for position in range(1, 4):
        shared = shared + loadings[position] * directions[position]
    blended = shared + jitter_level * jitter
    return blended.reshape(TOKENS, HK * DK).astype(jnp.bfloat16)


def draw_log_decay_rate(key, part):
    key = jax.random.fold_in(key, 23)
    chooser_key, slow_key, fast_key = jax.random.split(key, 3)
    slow_share = 0.5
    slow_scale = jnp.exp(jax.random.uniform(slow_key, (HV,), jnp.float32, jnp.log(0.1), jnp.log(1.5)))
    chooser = jax.random.uniform(chooser_key, (HV,), jnp.float32)
    slow_rates = jnp.log(slow_scale / TOKENS)
    fast_rates = jax.random.uniform(fast_key, (HV,), jnp.float32, -3.6, -3.0)
    return jnp.where(chooser < slow_share, slow_rates, fast_rates).astype(jnp.float32)


def shard_levels(rng, extent, cuts, least, top_value):
    def one(dim, blocks):
        steps = jax.random.uniform(jax.random.fold_in(jax.random.fold_in(rng, 6), dim), (blocks,), jnp.float32, least / len(cuts), top_value / len(cuts))
        return jnp.repeat(jnp.exp(steps), extent[dim] // blocks).reshape((-1,) + (1,) * (len(extent) - dim - 1))

    loudness = one(*cuts[0])
    for cut in cuts[1:]:
        loudness = loudness * one(*cut)
    return loudness


def centred(key, shape, scale, bound, cuts=(), kind=jnp.bfloat16):
    entries = jax.random.normal(key, shape, jnp.float32) * scale
    if len(cuts) > 0:
        entries = shard_levels(key, shape, cuts, -0.22, 0.18) * entries
    return jnp.clip(entries, min=-bound, max=bound).astype(kind)


def setup_inputs(seed: int = 0) -> dict:
    keys = jax.random.split(jax.random.key(seed), 11)
    hidden_in = centred(keys[0], (TOKENS, D), 1.0, 6.0, ((0, 64),))
    query_vectors = centred(keys[1], (TOKENS, HK * DK), 1.0, 6.0, ((0, 64), (1, 8)))
    key_vectors = draw_key_vectors(jax.random.fold_in(keys[10], 71), 0)
    value_vectors = centred(keys[3], (TOKENS, HV * DV), 1.0, 6.0, ((0, 64), (1, 8)))
    out_cotangent = centred(keys[4], (TOKENS, HV * DV), 1.0, 6.0, ((0, 64), (1, 8)))
    w_decay = centred(keys[5], (D, HV), D ** -0.5, 0.125, ((1, 8),))
    w_beta = centred(keys[6], (D, HV), D ** -0.5, 0.125, ((1, 8),))
    log_decay_rate = draw_log_decay_rate(jax.random.fold_in(keys[10], 71), 0)
    step_bias = jnp.clip(jax.random.uniform(keys[8], (HV,), jnp.float32, -1.0, 1.0) * shard_levels(keys[8], (HV,), ((0, 8),), -0.4, 0.0), -1.0, 1.0)
    doc_start = jax.random.randint(keys[9], (1,), 0, TOKENS).astype(jnp.int32)
    return {"hidden_in": hidden_in, "query_vectors": query_vectors, "key_vectors": key_vectors, "value_vectors": value_vectors, "out_cotangent": out_cotangent, "w_decay": w_decay, "w_beta": w_beta, "log_decay_rate": log_decay_rate, "step_bias": step_bias, "doc_start": doc_start}


norm_epsilon = 1e-06

def unit_rows(source):
    return source * lax.rsqrt(lax.optimization_barrier(jnp.sum(source * source, axis=-1, keepdims=True)) + norm_epsilon)

def block_step(carried, pieces):
    query_block, key_block, value_block, decay_block, beta_block, reset_block = pieces
    length = query_block.shape[-2]
    highest = lax.Precision.HIGHEST
    cumulative = jnp.cumsum(decay_block, axis=-1)
    counted = jnp.cumsum(reset_block, axis=-1)
    places = jnp.arange(length, dtype=jnp.int32)
    lower_mask = places[:, None] >= places[None, :]
    strict_mask = places[:, None] > places[None, :]
    same_doc = (counted[:, :, None] == counted[:, None, :])[:, None]
    keep_mask = jnp.logical_and(lower_mask, same_doc)
    spread = cumulative[..., :, None] - cumulative[..., None, :]
    decay_matrix = jnp.where(keep_mask, jnp.exp(jnp.where(keep_mask, spread, 0.0)), 0.0)
    carry_in = jnp.where(counted[:, None, :] == 0, jnp.exp(cumulative), 0.0)
    key_gram = jnp.einsum('bhid,bhjd->bhij', key_block, key_block, precision=highest)
    coupling = jnp.where(strict_mask, beta_block[..., :, None] * decay_matrix * key_gram, 0.0)
    key_state = jnp.einsum('bhid,bhde->bhie', key_block, carried, precision=highest)
    target = beta_block[..., None] * (value_block - carry_in[..., None] * key_state)
    system = coupling + jnp.eye(length, dtype=jnp.float32)
    updates = lax.linalg.triangular_solve(system, target, left_side=True, lower=True, unit_diagonal=True)
    query_key = jnp.einsum('bhid,bhjd->bhij', query_block, key_block, precision=highest)
    from_state = jnp.einsum('bhid,bhde->bhie', query_block, carried, precision=highest)
    outputs = carry_in[..., None] * from_state + jnp.einsum('bhij,bhje->bhie', query_key * decay_matrix, updates, precision=highest)
    weighted_keys = key_block * decay_matrix[..., -1, :, None]
    new_state = carry_in[..., -1, None, None] * carried + jnp.einsum('bhjd,bhje->bhde', weighted_keys, updates, precision=highest)
    return (new_state, outputs)

def blocked(source, blocks):
    seq_count, tokens = (source.shape[0], source.shape[1])
    shaped = source.reshape((seq_count, blocks, tokens // blocks) + source.shape[2:])
    if source.ndim == 4:
        return shaped.transpose(1, 0, 3, 2, 4)
    if source.ndim == 3:
        return shaped.transpose(1, 0, 3, 2)
    return shaped.transpose(1, 0, 2)

def run_block(carried, queries_f, keys_f, values_f, logit_rows, rate_logs, biases, resets):
    seq_count, tokens = (logit_rows.shape[0], logit_rows.shape[1])
    head_count = rate_logs.shape[0]
    size_key = carried.shape[2]
    size_value = carried.shape[3]
    group_size = head_count // (queries_f.shape[2] // size_key)
    log_decay = -jnp.exp(rate_logs) * jax.nn.softplus(logit_rows[..., :head_count] + biases)
    beta_all = jax.nn.sigmoid(logit_rows[..., head_count:])
    query_heads = unit_rows(queries_f.reshape(seq_count, tokens, -1, size_key)) * size_key ** (-0.5)
    key_heads = unit_rows(keys_f.reshape(seq_count, tokens, -1, size_key))
    query_heads = jnp.repeat(query_heads, group_size, axis=2)
    key_heads = jnp.repeat(key_heads, group_size, axis=2)
    value_heads = values_f.reshape(seq_count, tokens, head_count, size_value)
    blocks = tokens // BLOCK
    pieces = (blocked(query_heads, blocks), blocked(key_heads, blocks), blocked(value_heads, blocks), blocked(log_decay, blocks), blocked(beta_all, blocks), blocked(resets, blocks))
    final_state, outputs = lax.scan(jax.checkpoint(block_step), carried, pieces)
    outputs = outputs.transpose(1, 0, 3, 2, 4).reshape(seq_count, tokens, head_count * size_value)
    return (outputs, final_state)

def reference(hidden_in, query_vectors, key_vectors, value_vectors, out_cotangent, w_decay, w_beta, log_decay_rate, step_bias, doc_start):
    both_weights = jnp.concatenate([w_decay, w_beta], axis=1)
    head_count = log_decay_rate.shape[0]
    positions = jnp.arange(TOKENS, dtype=jnp.int32)
    zero_state = jnp.zeros((1, head_count, DK, DV), jnp.float32)
    highest = lax.Precision.HIGHEST
    logits = jnp.dot(hidden_in.astype(jnp.float32), both_weights.astype(jnp.float32), preferred_element_type=jnp.float32)[None]
    resets = (positions == doc_start[0].astype(jnp.int32)).astype(jnp.float32)[None]

    def forward(queries_f, keys_f, values_f, logit_rows, rate_logs, biases):
        return run_block(zero_state, queries_f, keys_f, values_f, logit_rows, rate_logs, biases, resets)[0]
    result, pull_back = jax.vjp(forward, query_vectors.astype(jnp.float32)[None], key_vectors.astype(jnp.float32)[None], value_vectors.astype(jnp.float32)[None], logits, log_decay_rate, step_bias)
    gradients = pull_back(out_cotangent.astype(jnp.float32)[None])
    logit_grad = gradients[3][0]
    hidden_grad = jnp.dot(logit_grad, both_weights.astype(jnp.float32).T, precision=highest)
    weight_grad = jnp.dot(hidden_in.astype(jnp.float32).T, logit_grad, precision=highest)
    return (gradients[0][0].astype(jnp.bfloat16), gradients[1][0].astype(jnp.bfloat16), gradients[2][0].astype(jnp.bfloat16), hidden_grad.astype(jnp.bfloat16), weight_grad[:, :head_count], weight_grad[:, head_count:], gradients[4], gradients[5])
```

```python
import functools

import jax
import jax.numpy as jnp
from jax import lax
from jax.experimental import pallas as pl
from jax.experimental.pallas import tpu as pltpu
from jax.sharding import Mesh
from jax.sharding import PartitionSpec as P

F32 = jnp.float32
BF16 = jnp.bfloat16
F16 = jnp.float16
C = 128
HEADS = 2
D = 2048
NX, NZ, NC, NY = 4, 8, 2, 8
CTX = ("x", "z", "core")
norm_epsilon = 1e-06
SCALE = C**-0.5
LOG_FLOOR = -200.0
MAP_ROWS = 3 * C + 8
PACKED_ROWS = 3 * C + 16


def split(a):
    high = a.astype(BF16)
    return (high, (a - high.astype(F32)).astype(BF16))


def split3(a):
    high = a.astype(BF16)
    rest = a - high.astype(F32)
    middle = rest.astype(BF16)
    return (high, middle, (rest - middle.astype(F32)).astype(BF16))


def dot(a, b, ca, cb):
    return lax.dot_general(a, b, (((ca,), (cb,)), ((), ())), preferred_element_type=F32)


def mm(a, b, ca=1, cb=0):
    total = dot(a[0], b[0], ca, cb)
    for i in range(len(a)):
        for j in range(len(b)):
            if 0 < i + j < max(len(a), len(b)):
                total = total + dot(a[i], b[j], ca, cb)
    return total


def iotas():
    return (
        lax.broadcasted_iota(jnp.int32, (C, C), 0),
        lax.broadcasted_iota(jnp.int32, (C, C), 1),
    )


def pair_column(first, second):
    row = lax.broadcasted_iota(jnp.int32, (HEADS, C), 0)
    return jnp.where(row == 0, first, second)


def unit_rows(source):
    root = lax.rsqrt(jnp.sum(source * source, axis=-1, keepdims=True) + norm_epsilon)
    return source * root, root


def local_kernel(
    place_ref, rate_ref, bias_ref, hid_ref, q_ref, k_ref, v_ref, do_ref, wd_ref, wb_ref,
    map_ref, uhat_ref, what_ref, z0_ref, y_ref, gram_ref, qk_ref, rows_ref,
):
    reset = place_ref[0]
    ii, jj = iotas()
    keep = jnp.logical_and(ii >= jj, jnp.logical_or(jj >= reset, ii < reset))
    zd = dot(wd_ref[...], hid_ref[...], 1, 1)
    zb = dot(wb_ref[...], hid_ref[...], 1, 1)
    x = zd + pair_column(bias_ref[0], bias_ref[1])
    soft = jnp.maximum(x, 0.0) + jnp.log1p(jnp.exp(-jnp.abs(x)))
    log_decay = -jnp.exp(pair_column(rate_ref[0], rate_ref[1])) * soft
    beta = jax.nn.sigmoid(zb)
    upper = (ii <= jj).astype(BF16)
    cumulative = sum(dot(t, upper, 1, 0) for t in split3(log_decay))
    rows_ref[0:2, :] = cumulative
    rows_ref[2:4, :] = beta
    rows_ref[4:6, :] = log_decay
    rows_ref[6:8, :] = x
    cols = rows_ref[...].T
    keys, _ = unit_rows(k_ref[...].astype(F32))
    queries, _ = unit_rows(q_ref[...].astype(F32))
    queries = queries * SCALE
    ks, qs = split(keys), split(queries)
    gram = mm(ks, ks, 1, 1)
    qk = mm(qs, ks, 1, 1)
    gram_ref[...] = gram
    qk_ref[...] = qk
    ii_col = ii[:, 0:1]
    eye = jnp.where(ii == jj, 1.0, 0.0).astype(F32)
    for h in range(HEADS):
        c_col, c_row = cols[:, h : h + 1], rows_ref[h : h + 1, :]
        b_col = cols[:, 2 + h : 3 + h]
        lanes = slice(h * C, (h + 1) * C)
        decay = jnp.where(keep, jnp.exp(jnp.where(keep, c_col - c_row, 0.0)), 0.0)
        carry = jnp.where(ii_col < reset, jnp.exp(c_col), 0.0)
        c_last = c_col[C - 1 : C, :]
        late = jnp.logical_or(ii_col >= reset, reset > C - 1)
        weight = jnp.where(late, jnp.exp(jnp.where(late, c_last - c_col, 0.0)), 0.0)
        inner = jnp.where(ii > jj, decay * gram, 0.0)
        coupling = b_col * inner
        inverse = eye - jnp.where((ii & 1) * (ii - jj) == 1, coupling, 0.0)
        for level in range(1, 7):
            bi, bj = ii >> level, jj >> level
            part = jnp.where((bi & 1) * (bi - bj) == 1, coupling, 0.0)
            xs = split(inverse)
            inverse = inverse - mm(xs, split(mm(split(part), xs)))
        xs = split(inverse)
        keys_in = carry * keys
        values = v_ref[:, lanes].astype(F32)
        cotangent = (do_ref[:, lanes],)
        both = jnp.concatenate([keys_in, values], axis=1)
        wu = mm(xs, split(b_col * both))
        wus = split(wu)
        hats = both - mm(split(inner), wus)
        what_ref[h] = hats[:, :C]
        uhat_ref[h] = hats[:, C:]
        ps = split(qk * decay)
        keys_out = weight * keys
        zy = mm(xs, split(jnp.concatenate([mm(ps, cotangent, 0, 0), keys_out], axis=1)), 0, 0)
        z0_ref[h] = zy[:, :C]
        y_ref[h] = zy[:, C:]
        ml = mm(split(keys_out), wus, 0, 0)
        map_ref[h, 0:C, :] = ml[:, :C]
        map_ref[h, C : 2 * C, :] = ml[:, C:]
        effective = carry * queries - mm(ps, tuple(t[:, :C] for t in wus))
        map_ref[h, 2 * C : 3 * C, :] = mm(split(effective), cotangent, 0, 0)
        total = jnp.where(reset > C - 1, jnp.maximum(c_last, LOG_FLOOR), LOG_FLOOR)
        map_ref[h, 3 * C :, :] = jnp.broadcast_to(total, (8, C))


def read_map(ref, *at):
    m = ref[(*at, slice(0, C), slice(None))]
    state = ref[(*at, slice(C, 2 * C), slice(None))]
    adjoint = ref[(*at, slice(2 * C, 3 * C), slice(None))]
    log = ref[(*at, slice(3 * C, 3 * C + 1), slice(0, 1))]
    return m, state, adjoint, log


def pair_kernel(maps_ref, out_ref):
    m0, l0, a0, c0 = read_map(maps_ref, 0)
    m1, l1, a1, c1 = read_map(maps_ref, 1)
    g0, g1 = jnp.exp(c0), jnp.exp(c1)
    m0s, m1s = split(m0), split(m1)
    forward = mm(m1s, tuple(jnp.concatenate([a, b], axis=1) for a, b in zip(m0s, split(l0))))
    m = g1 * m0 + g0 * m1 - forward[:, :C]
    state = g1 * l0 - forward[:, C:] + l1
    adjoint = g0 * a1 - mm(m0s, split(a1), 0, 0) + a0
    log = jnp.maximum(c0 + c1, LOG_FLOOR)
    row = lax.broadcasted_iota(jnp.int32, (16, C), 0)
    meta = jnp.zeros((16, C), F32)
    for at, part in enumerate((m, state, adjoint)):
        largest = jnp.max(jnp.max(jnp.abs(part), axis=0, keepdims=True), axis=1, keepdims=True)
        power = jnp.floor(jnp.log2(jnp.maximum(largest, 1e-30)))
        out_ref[at * C : (at + 1) * C, :] = part * jnp.exp2(13.0 - power)
        meta = jnp.where(row == at, power, meta)
    quarters = jnp.floor(log * 4.0)
    fine = log * 4.0 - quarters
    coarse = jnp.floor(fine * 1024.0) * (1.0 / 1024.0)
    meta = jnp.where(row == 3, quarters * 0.25, meta)
    meta = jnp.where(row == 4, coarse, meta)
    meta = jnp.where(row == 5, (fine - coarse) * 1024.0, meta)
    out_ref[3 * C :, :] = meta


def ring_kernel(at_ref, maps_ref, out_ref, near_ref):
    here = at_ref[0]

    def fetch(z):
        meta = maps_ref[z, 3 * C :, :]
        scales = [jnp.exp2(meta[i : i + 1, 0:1] - 13.0) for i in range(3)]
        parts = [maps_ref[z, i * C : (i + 1) * C, :] * scales[i] for i in range(3)]
        log = meta[3:4, 0:1] + 0.25 * (meta[4:5, 0:1] + meta[5:6, 0:1] * (1.0 / 1024.0))
        return parts[0], parts[1], parts[2], log

    zero = jnp.zeros((C, C), F32)

    @pl.when(here == 0)
    def _():
        near_ref[0:C, :] = zero
        near_ref[C : 2 * C, :] = zero
        near_ref[4 * C : 4 * C + 8, :] = jnp.zeros((8, C), F32)

    @pl.when(here == NZ - 1)
    def _():
        near_ref[2 * C : 3 * C, :] = zero
        near_ref[3 * C : 4 * C, :] = zero
        near_ref[4 * C + 8 :, :] = jnp.zeros((8, C), F32)

    m, state, _, log = fetch(0)
    m_back, _, adjoint, log_back = fetch(NZ - 1)
    m_back = m_back.T
    for step in range(1, NZ):
        back = NZ - 1 - step

        @pl.when(here == step)
        def _():
            near_ref[0:C, :] = m
            near_ref[C : 2 * C, :] = state
            near_ref[4 * C : 4 * C + 8, :] = jnp.broadcast_to(log, (8, C))

        @pl.when(here == back)
        def _():
            near_ref[2 * C : 3 * C, :] = m_back
            near_ref[3 * C : 4 * C, :] = adjoint
            near_ref[4 * C + 8 :, :] = jnp.broadcast_to(log_back, (8, C))

        mz, lz, _, cz = fetch(step)
        moved = mm(split(mz), split(jnp.concatenate([m, state], axis=1)))
        gz, g = jnp.exp(cz), jnp.exp(log)
        m, state = gz * m + g * mz - moved[:, :C], gz * state + lz - moved[:, C:]
        log = log + cz
        mz, _, az, cz = fetch(back)
        mz = mz.T
        moved = mm(split(mz), split(jnp.concatenate([m_back, adjoint], axis=1)))
        gz, g = jnp.exp(cz), jnp.exp(log_back)
        m_back, adjoint = gz * m_back + g * mz - moved[:, :C], gz * adjoint + az - moved[:, C:]
        log_back = log_back + cz
    total = jnp.broadcast_to(jnp.maximum(log, LOG_FLOOR), (8, C))
    for slot in range(NX):
        out_ref[slot, 0:C, :] = m
        out_ref[slot, C : 2 * C, :] = state
        out_ref[slot, 2 * C : 3 * C, :] = adjoint
        out_ref[slot, 3 * C :, :] = total


def entry_kernel(at_ref, groups_ref, near_ref, maps_ref, out_ref, s_ref, a_ref):
    here = at_ref[0]
    _, first, _, _ = read_map(groups_ref, 0)
    _, _, last, _ = read_map(groups_ref, NX - 1)
    s_ref[...] = jnp.where(here > 0, first, 0.0)
    a_ref[...] = jnp.where(here < NX - 1, last, 0.0)
    for step in range(1, NX - 1):
        back = NX - 1 - step

        @pl.when(here > step)
        def _():
            m, state, _, log = read_map(groups_ref, step)
            s = s_ref[...]
            s_ref[...] = jnp.exp(log) * s - mm(split(m), split(s)) + state

        @pl.when(here < back)
        def _():
            m, _, adjoint, log = read_map(groups_ref, back)
            a = a_ref[...]
            a_ref[...] = jnp.exp(log) * a - mm(split(m), split(a), 0, 0) + adjoint

    s, a = s_ref[...], a_ref[...]
    g_in, g_out = (jnp.exp(near_ref[4 * C + 8 * i : 4 * C + 8 * i + 1, 0:1]) for i in range(2))
    s = g_in * s - mm(split(near_ref[0:C, :]), split(s)) + near_ref[C : 2 * C, :]
    a = g_out * a - mm(split(near_ref[2 * C : 3 * C, :]), split(a)) + near_ref[3 * C : 4 * C, :]
    out_ref[0, 0:C, :] = s
    out_ref[1, C : 2 * C, :] = a
    m, state, _, log = read_map(maps_ref, 0)
    out_ref[1, 0:C, :] = jnp.exp(log) * s - mm(split(m), split(s)) + state
    m, _, adjoint, log = read_map(maps_ref, 1)
    out_ref[0, C : 2 * C, :] = jnp.exp(log) * a - mm(split(m), split(a), 0, 0) + adjoint


def grad_kernel(
    place_ref, rate_ref, bias_ref, ends_ref, hid_ref, q_ref, k_ref, v_ref, do_ref, wd_ref, wb_ref,
    uhat_ref, what_ref, z0_ref, y_ref, gram_ref, qk_ref, rows_ref,
    dq_ref, dk_ref, dv_ref, share_ref, weight_ref, sums_ref,
):
    reset = place_ref[0]
    ii, jj = iotas()
    keep = jnp.logical_and(ii >= jj, jnp.logical_or(jj >= reset, ii < reset))
    rows = rows_ref[...]
    cols = rows.T
    keys, key_root = unit_rows(k_ref[...].astype(F32))
    unit_queries, query_root = unit_rows(q_ref[...].astype(F32))
    queries = unit_queries * SCALE
    ks, qs = split(keys), split(queries)
    gram, qk = gram_ref[...], qk_ref[...]
    ii_col = ii[:, 0:1]
    ones = jnp.ones((8, C), BF16)
    lower = (ii >= jj).astype(BF16)
    dq = dk = e_sum = f_sum = None
    for h in range(HEADS):
        c_col, c_row = cols[:, h : h + 1], rows[h : h + 1, :]
        b_col = cols[:, 2 + h : 3 + h]
        lanes = slice(h * C, (h + 1) * C)
        decay = jnp.where(keep, jnp.exp(jnp.where(keep, c_col - c_row, 0.0)), 0.0)
        carry = jnp.where(ii_col < reset, jnp.exp(c_col), 0.0)
        c_last = c_col[C - 1 : C, :]
        late = jnp.logical_or(ii_col >= reset, reset > C - 1)
        weight = jnp.where(late, jnp.exp(jnp.where(late, c_last - c_col, 0.0)), 0.0)
        s, a = ends_ref[h, 0:C, :], ends_ref[h, C : 2 * C, :]
        ss, as_ = split(s), split(a)
        uhat = uhat_ref[h] - mm(split(what_ref[h]), ss)
        z = z0_ref[h] + mm(split(y_ref[h]), as_)
        bz = b_col * z
        dv_ref[:, lanes] = bz.astype(BF16)
        us = split(b_col * uhat)
        cotangent = (do_ref[:, lanes],)
        e = jnp.where(keep, mm(cotangent, us, 1, 1) * decay, 0.0)
        f = jnp.where(ii > jj, mm(split(z), us, 1, 1) * decay * -b_col, 0.0)
        from_out = carry * mm(cotangent, ss, 1, 1)
        from_keys = weight * mm(us, as_, 1, 1)
        key_side = from_keys - carry * mm(split(bz), ss, 1, 1)
        h_mat = e * qk + f * gram
        by_row = h_mat + queries * from_out + keys * (key_side - 2.0 * from_keys)
        dc = sum(dot(ones, t, 1, 1) for t in split3(by_row))
        dc = dc[0:1, :] - jnp.sum(h_mat, axis=0, keepdims=True)
        tail = jnp.sum(jnp.sum(keys * from_keys, axis=0, keepdims=True), axis=1, keepdims=True)
        tail = tail + carry[C - 1 : C, :] * jnp.sum(
            jnp.sum(s * a, axis=0, keepdims=True), axis=1, keepdims=True
        )
        db = sum(dot(ones, t, 1, 1) for t in split3(z * uhat))
        sums_ref[h : h + 1, :] = dc
        sums_ref[2 + h : 3 + h, :] = db[0:1, :]
        sums_ref[4 + h : 5 + h, :] = jnp.broadcast_to(tail, (1, C))
        if h == 0:
            dq, dk, e_sum, f_sum = from_out, key_side, e, f
        else:
            dq, dk, e_sum, f_sum = dq + from_out, dk + key_side, e_sum + e, f_sum + f
    es = split(e_sum)
    dq = dq + mm(es, ks)
    dk = dk + mm(es, qs, 0, 0) + mm(split(f_sum + f_sum.T), ks)
    dq = dq - unit_queries * jnp.sum(unit_queries * dq, axis=-1, keepdims=True)
    dk = dk - keys * jnp.sum(keys * dk, axis=-1, keepdims=True)
    dq_ref[...] = (dq * (query_root * SCALE)).astype(BF16)
    dk_ref[...] = (dk * key_root).astype(BF16)
    dc, db, tail = sums_ref[0:2, :], sums_ref[2:4, :], sums_ref[4:6, :]
    dg = sum(dot(t, lower, 1, 0) for t in split3(dc)) + tail
    beta, log_decay, x = rows_ref[2:4, :], rows_ref[4:6, :], rows_ref[6:8, :]
    dz = dg * -jnp.exp(pair_column(rate_ref[0], rate_ref[1])) * jax.nn.sigmoid(x)
    dzb = db * beta * (1.0 - beta)
    rate_part = jnp.sum(dg * log_decay, axis=1, keepdims=True)
    bias_part = jnp.sum(dz, axis=1, keepdims=True)
    sums_ref[0:2, :] = dz
    sums_ref[2:4, :] = dzb
    sums_ref[4:6, :] = jnp.broadcast_to(rate_part, (2, C))
    sums_ref[6:8, :] = jnp.broadcast_to(bias_part, (2, C))
    for slot in range(NY):
        share_ref[slot, 0:4, :] = sums_ref[0:4, :]
        for half in range(2):
            at = slice((2 * slot + half) * C, (2 * slot + half + 1) * C)
            share_ref[slot, 4 + 4 * half : 6 + 4 * half, :] = wd_ref[:, at].astype(F32)
            share_ref[slot, 6 + 4 * half : 8 + 4 * half, :] = wb_ref[:, at].astype(F32)
        share_ref[slot, 12:16, :] = jnp.zeros((4, C), F32)
    grad = sum(dot(t, hid_ref[...], 1, 0) for t in split3(sums_ref[...]))
    for slot in range(NZ * NC):
        weight_ref[slot, 0:4, :] = grad[0:4, slot * C : (slot + 1) * C]
        weight_ref[slot, 4:8, :] = sums_ref[4:8, :]


def add_kernel(parts_ref, out_ref):
    total = parts_ref[0]
    for i in range(1, NZ * NC):
        total = total + parts_ref[i]
    for slot in range(NX * NZ * NC):
        out_ref[slot] = total


def finish_kernel(share_ref, parts_ref, hidden_ref, wd_ref, wb_ref, stat_ref):
    logit_rows = jnp.concatenate(
        [jnp.concatenate([share_ref[2 * i, 0:4, :], share_ref[2 * i + 1, 0:4, :]], axis=0) for i in range(NY // 2)],
        axis=0,
    )
    terms = split3(logit_rows)
    for half in range(2):
        at = slice(4 + 4 * half, 8 + 4 * half)
        weights = jnp.concatenate(
            [jnp.concatenate([share_ref[2 * i, at, :], share_ref[2 * i + 1, at, :]], axis=0) for i in range(NY // 2)],
            axis=0,
        ).astype(BF16)
        hidden_ref[:, half * C : (half + 1) * C] = sum(dot(t, weights, 0, 0) for t in terms).astype(BF16)
    per = NZ * NC
    for slot in range(per):
        total = parts_ref[slot]
        for group in range(1, NX):
            total = total + parts_ref[group * per + slot]
        wd_ref[:, slot * C : (slot + 1) * C] = total[0:2, :]
        wb_ref[:, slot * C : (slot + 1) * C] = total[2:4, :]
        if slot == 0:
            stat_ref[...] = total


VMEM = pl.BlockSpec(memory_space=pltpu.VMEM)
SMEM = pl.BlockSpec(memory_space=pltpu.SMEM)


def call(kernel, scalars, arrays, outs, scratch=()):
    return pl.pallas_call(
        kernel,
        out_shape=tuple(jax.ShapeDtypeStruct(s, t) for s, t in outs),
        in_specs=[SMEM] * len(scalars) + [VMEM] * len(arrays),
        out_specs=tuple([VMEM] * len(outs)),
        scratch_shapes=list(scratch),
        compiler_params=pltpu.CompilerParams(vmem_limit_bytes=40 * 1024 * 1024),
    )(*scalars, *arrays)


def exchange(a, axes):
    return lax.all_to_all(a, axes, 0, 0, tiled=True)


def on_device(hidden, queries, keys, values, cotangent, w_decay, w_beta, rate, bias, doc_start):
    at_x = lax.axis_index("x").astype(jnp.int32)
    at_z = lax.axis_index("z").astype(jnp.int32)
    at_core = lax.axis_index("core").astype(jnp.int32)
    place = doc_start - ((at_x * NZ + at_z) * NC + at_core) * C
    place = jnp.where(place < 0, C, place)
    wd, wb = w_decay.T, w_beta.T
    square, heads = (C, C), (HEADS, C, C)
    maps, uhat, what, z0, y, gram, qk, rows = call(
        local_kernel,
        (place, rate, bias),
        (hidden, queries, keys, values, cotangent, wd, wb),
        [((HEADS, MAP_ROWS, C), F32)] + [(heads, F32)] * 4 + [(square, F32)] * 2 + [((8, C), F32)],
    )
    maps = exchange(maps, "core")
    (packed,) = call(pair_kernel, (), (maps,), [((PACKED_ROWS, C), F32)])
    packed = jnp.broadcast_to(packed.astype(F16), (NZ, PACKED_ROWS, C))
    ring = exchange(packed, "z").astype(F32)
    groups, near = call(
        ring_kernel,
        (at_z[None],),
        (ring,),
        [((NX, MAP_ROWS, C), F32), ((4 * C + 16, C), F32)],
    )
    groups = exchange(groups, "x")
    (ends,) = call(
        entry_kernel,
        (at_x[None],),
        (groups, near, maps),
        [((NC, 2 * C, C), F32)],
        [pltpu.VMEM(square, F32), pltpu.VMEM(square, F32)],
    )
    ends = exchange(ends, "core")
    dq, dk, dv, share, weights = call(
        grad_kernel,
        (place, rate, bias),
        (ends, hidden, queries, keys, values, cotangent, wd, wb, uhat, what, z0, y, gram, qk, rows),
        [
            (square, BF16),
            (square, BF16),
            ((C, HEADS * C), BF16),
            ((NY, 16, C), F32),
            ((NZ * NC, 8, C), F32),
        ],
        [pltpu.VMEM((8, C), F32)],
    )
    share = exchange(share, "dp")
    weights = exchange(weights, ("z", "core"))
    (weights,) = call(add_kernel, (), (weights,), [((NX * NZ * NC, 8, C), F32)])
    weights = exchange(weights, CTX)
    hidden_grad, wd_grad, wb_grad, stats = call(
        finish_kernel,
        (),
        (share, weights),
        [((C, 2 * C), BF16), ((2, D), F32), ((2, D), F32), ((8, C), F32)],
    )
    return (dq, dk, dv, hidden_grad, wd_grad.T, wb_grad.T, stats[4:6, 0], stats[6:8, 0])


def solution(mesh):
    fine = Mesh(mesh.devices.reshape(NX, NZ, NC, NY), ("x", "z", "core", "dp"))
    rows, both, cols = P(CTX, None), P(CTX, "dp"), P(None, "dp")
    return jax.shard_map(
        on_device,
        mesh=fine,
        in_specs=(rows, both, both, both, both, cols, cols, P("dp"), P("dp"), P()),
        out_specs=(both, both, both, both, cols, cols, P("dp"), P("dp")),
        check_vma=False,
    )
```

```python
import functools

import jax
import jax.numpy as jnp
from jax import lax
from jax.experimental import pallas as pl
from jax.experimental.pallas import tpu as pltpu
from jax.sharding import Mesh
from jax.sharding import PartitionSpec as P

F32 = jnp.float32
BF16 = jnp.bfloat16
F16 = jnp.float16
C = 128
HEADS = 2
D = 2048
NX, NZ, NC, NY = 4, 8, 2, 8
CTX = ("x", "z", "core")
norm_epsilon = 1e-06
SCALE = C**-0.5
FULL_VMEM = 64 << 20
LOG_FLOOR = -200.0
MAP_ROWS = 3 * C + 8
PACKED_ROWS = 3 * C + 16


def split(a):
    high = a.astype(BF16)
    return (high, (a - high.astype(F32)).astype(BF16))


def split3(a):
    high = a.astype(BF16)
    rest = a - high.astype(F32)
    middle = rest.astype(BF16)
    return (high, middle, (rest - middle.astype(F32)).astype(BF16))


def dot(a, b, ca, cb):
    return lax.dot_general(a, b, (((ca,), (cb,)), ((), ())), preferred_element_type=F32)


def mm(a, b, ca=1, cb=0):
    total = dot(a[0], b[0], ca, cb)
    for i in range(len(a)):
        for j in range(len(b)):
            if 0 < i + j < max(len(a), len(b)):
                total = total + dot(a[i], b[j], ca, cb)
    return total


def iotas():
    return (
        lax.broadcasted_iota(jnp.int32, (C, C), 0),
        lax.broadcasted_iota(jnp.int32, (C, C), 1),
    )


def pair_column(first, second):
    row = lax.broadcasted_iota(jnp.int32, (HEADS, C), 0)
    return jnp.where(row == 0, first, second)


def unit_rows(source):
    root = lax.rsqrt(jnp.sum(source * source, axis=-1, keepdims=True) + norm_epsilon)
    return source * root, root


def gate_matrices(rows_ref, cols, h, ii, jj, reset):
    keep = jnp.logical_and(ii >= jj, jnp.logical_or(jj >= reset, ii < reset))
    ii_col = ii[:, 0:1]
    c_col, c_row = cols[:, h : h + 1], rows_ref[h : h + 1, :]
    decay = jnp.where(keep, jnp.exp(jnp.where(keep, c_col - c_row, 0.0)), 0.0)
    carry = jnp.where(ii_col < reset, jnp.exp(c_col), 0.0)
    c_last = c_col[C - 1 : C, :]
    late = jnp.logical_or(ii_col >= reset, reset > C - 1)
    weight = jnp.where(late, jnp.exp(jnp.where(late, c_last - c_col, 0.0)), 0.0)
    return keep, decay, carry, weight, cols[:, 2 + h : 3 + h], c_last


def local_kernel(
    at_ref, doc_hbm, rate_hbm, bias_hbm, k_hbm, hid_hbm, wd_hbm, wb_hbm, q_hbm, v_hbm, do_hbm,
    map_ref, wu_ref, inverse_ref, pdo_ref, gram_ref, qk_ref, rows_ref,
    doc_ref, rate_ref, bias_ref, k_ref, hid_ref, wd_ref, wb_ref, q_ref, v_ref, do_ref, sems,
):
    pairs = (
        (hid_hbm, hid_ref), (wd_hbm, wd_ref), (wb_hbm, wb_ref), (rate_hbm, rate_ref), (bias_hbm, bias_ref),
        (doc_hbm, doc_ref), (k_hbm, k_ref), (q_hbm, q_ref), (v_hbm, v_ref), (do_hbm, do_ref),
    )
    copies = [pltpu.make_async_copy(a, b, sems.at[i]) for i, (a, b) in enumerate(pairs)]
    for copy in copies:
        copy.start()
    ii, jj = iotas()
    copies[6].wait()
    copies[7].wait()
    keys, _ = unit_rows(k_ref[...].astype(F32))
    queries, _ = unit_rows(q_ref[...].astype(F32))
    queries = queries * SCALE
    ks, qs = split(keys), split(queries)
    gram = mm(ks, ks, 1, 1)
    qk = mm(qs, ks, 1, 1)
    gram_ref[...] = gram
    qk_ref[...] = qk
    for copy in copies[:6]:
        copy.wait()
    reset = doc_ref[0] - at_ref[0]
    reset = jnp.where(reset < 0, C, jnp.minimum(reset, C))
    zd = dot(wd_ref[...], hid_ref[...], 1, 1)
    zb = dot(wb_ref[...], hid_ref[...], 1, 1)
    x = zd + pair_column(bias_ref[0], bias_ref[1])
    soft = jnp.maximum(x, 0.0) + jnp.log1p(jnp.exp(-jnp.abs(x)))
    slope = -jnp.exp(pair_column(rate_ref[0], rate_ref[1]))
    log_decay = slope * soft
    upper = (ii <= jj).astype(BF16)
    rows_ref[0:2, :] = sum(dot(t, upper, 1, 0) for t in split3(log_decay))
    rows_ref[2:4, :] = jax.nn.sigmoid(zb)
    rows_ref[4:6, :] = log_decay
    rows_ref[6:8, :] = x
    rows_ref[8:10, :] = slope
    rows_ref[10:16, :] = jnp.broadcast_to(reset.astype(F32), (6, C))
    cols = rows_ref[0:8, :].T
    copies[8].wait()
    copies[9].wait()
    eye = jnp.where(ii == jj, 1.0, 0.0).astype(F32)
    both_heads = range(HEADS)
    gates = [gate_matrices(rows_ref, cols, h, ii, jj, reset) for h in both_heads]
    coupling = [g[4] * jnp.where(ii > jj, g[1] * gram, 0.0) for g in gates]
    inverse = [eye - jnp.where((ii & 1) * (ii - jj) == 1, c, 0.0) for c in coupling]
    for level in range(1, 7):
        bi, bj = ii >> level, jj >> level
        here = (bi & 1) * (bi - bj) == 1
        part = [split(jnp.where(here, c, 0.0)) for c in coupling]
        xs = [split(x) for x in inverse]
        step = [split(mm(part[h], xs[h])) for h in both_heads]
        inverse = [inverse[h] - mm(xs[h], step[h]) for h in both_heads]
    xs = [split(x) for x in inverse]
    cotangent = [(do_ref[:, h * C : (h + 1) * C],) for h in both_heads]
    ps = [split(qk * g[1]) for g in gates]
    right = [
        split(g[4] * jnp.concatenate([g[2] * keys, v_ref[:, h * C : (h + 1) * C].astype(F32)], axis=1))
        for h, g in enumerate(gates)
    ]
    wu = [mm(xs[h], right[h]) for h in both_heads]
    wus = [split(w) for w in wu]
    ml = [mm(split(gates[h][3] * keys), wus[h], 0, 0) for h in both_heads]
    reach = [mm(ps[h], tuple(t[:, :C] for t in wus[h])) for h in both_heads]
    effective = [split(gates[h][2] * queries - reach[h]) for h in both_heads]
    adjoint = [mm(effective[h], cotangent[h], 0, 0) for h in both_heads]
    pdo = [mm(ps[h], cotangent[h], 0, 0) for h in both_heads]
    for h in both_heads:
        inverse_ref[h] = inverse[h]
        wu_ref[h] = wu[h]
        pdo_ref[h] = pdo[h]
        map_ref[h, 0:C, :] = ml[h][:, :C]
        map_ref[h, C : 2 * C, :] = ml[h][:, C:]
        map_ref[h, 2 * C : 3 * C, :] = adjoint[h]
        total = jnp.where(reset > C - 1, jnp.maximum(gates[h][5], LOG_FLOOR), LOG_FLOOR)
        map_ref[h, 3 * C :, :] = jnp.broadcast_to(total, (8, C))


def own_rest(h, ii, jj, k_ref, v_ref, wu_ref, inverse_ref, pdo_ref, gram_ref, rows_ref, uhat_ref, what_ref, z0_ref, y_ref):
    reset = rows_ref[10:11, 0:1].astype(jnp.int32)
    keys, _ = unit_rows(k_ref[...].astype(F32))
    _, decay, carry, weight, _, _ = gate_matrices(rows_ref, rows_ref[0:8, :].T, h, ii, jj, reset)
    inner = jnp.where(ii > jj, decay * gram_ref[...], 0.0)
    both = jnp.concatenate([carry * keys, v_ref[:, h * C : (h + 1) * C].astype(F32)], axis=1)
    hats = both - mm(split(inner), split(wu_ref[h]))
    what_ref[h] = hats[:, :C]
    uhat_ref[h] = hats[:, C:]
    sides = jnp.concatenate([pdo_ref[h], weight * keys], axis=1)
    zy = mm(split(inverse_ref[h]), split(sides), 0, 0)
    z0_ref[h] = zy[:, :C]
    y_ref[h] = zy[:, C:]


def read_map(ref, *at):
    m = ref[(*at, slice(0, C), slice(None))]
    state = ref[(*at, slice(C, 2 * C), slice(None))]
    adjoint = ref[(*at, slice(2 * C, 3 * C), slice(None))]
    log = ref[(*at, slice(3 * C, 3 * C + 1), slice(0, 1))]
    return m, state, adjoint, log


def power_of_two(a):
    largest = jnp.max(jnp.max(jnp.abs(a), axis=0, keepdims=True), axis=1, keepdims=True)
    return jnp.floor(jnp.log2(jnp.maximum(largest, 1e-30)))


def pack(out_ref, parts, log):
    row = lax.broadcasted_iota(jnp.int32, (16, C), 0)
    meta = jnp.zeros((16, C), F32)
    for at, part in enumerate(parts):
        power = power_of_two(part)
        out_ref[at * C : (at + 1) * C, :] = part * jnp.exp2(13.0 - power)
        meta = jnp.where(row == at, power, meta)
    log = jnp.maximum(log, LOG_FLOOR)
    quarters = jnp.floor(log * 4.0)
    fine = log * 4.0 - quarters
    coarse = jnp.floor(fine * 1024.0) * (1.0 / 1024.0)
    meta = jnp.where(row == 3, quarters * 0.25, meta)
    meta = jnp.where(row == 4, coarse, meta)
    meta = jnp.where(row == 5, (fine - coarse) * 1024.0, meta)
    out_ref[3 * C :, :] = meta


def unpack(ref, at):
    meta = ref[at, 3 * C :, :]
    scales = [jnp.exp2(meta[i : i + 1, 0:1] - 13.0) for i in range(3)]
    parts = [ref[at, i * C : (i + 1) * C, :] * scales[i] for i in range(3)]
    log = meta[3:4, 0:1] + 0.25 * (meta[4:5, 0:1] + meta[5:6, 0:1] * (1.0 / 1024.0))
    return parts[0], parts[1], parts[2], log


def pair_kernel(maps_ref, out_ref):
    m0, l0, a0, c0 = read_map(maps_ref, 0)
    m1, l1, a1, c1 = read_map(maps_ref, 1)
    g0, g1 = jnp.exp(c0), jnp.exp(c1)
    m0s, m1s = split(m0), split(m1)
    forward = mm(m1s, tuple(jnp.concatenate([a, b], axis=1) for a, b in zip(m0s, split(l0))))
    m = g1 * m0 + g0 * m1 - forward[:, :C]
    state = g1 * l0 - forward[:, C:] + l1
    adjoint = g0 * a1 - mm(m0s, split(a1), 0, 0) + a0
    pack(out_ref, (m, state, adjoint), c0 + c1)


def ring_kernel(
    at_ref, maps_ref, k_ref, v_ref, wu_ref, inverse_ref, pdo_ref, gram_ref, rows_ref,
    out_ref, near_ref, uhat_ref, what_ref, z0_ref, y_ref,
):
    here = at_ref[0]
    ii, jj = iotas()

    fetch = functools.partial(unpack, maps_ref)
    zero = jnp.zeros((C, C), F32)

    @pl.when(here == 0)
    def _():
        near_ref[0:C, :] = zero
        near_ref[C : 2 * C, :] = zero
        near_ref[4 * C : 4 * C + 8, :] = jnp.zeros((8, C), F32)

    @pl.when(here == NZ - 1)
    def _():
        near_ref[2 * C : 3 * C, :] = zero
        near_ref[3 * C : 4 * C, :] = zero
        near_ref[4 * C + 8 :, :] = jnp.zeros((8, C), F32)

    m, state, _, log = fetch(0)
    m_back, _, adjoint, log_back = fetch(NZ - 1)
    m_back = m_back.T
    for step in range(1, NZ):
        back = NZ - 1 - step
        if step in (2, 5):
            own_rest(
                step // 4, ii, jj, k_ref, v_ref, wu_ref, inverse_ref, pdo_ref, gram_ref, rows_ref,
                uhat_ref, what_ref, z0_ref, y_ref,
            )

        @pl.when(here == step)
        def _():
            near_ref[0:C, :] = m
            near_ref[C : 2 * C, :] = state
            near_ref[4 * C : 4 * C + 8, :] = jnp.broadcast_to(log, (8, C))

        @pl.when(here == back)
        def _():
            near_ref[2 * C : 3 * C, :] = m_back
            near_ref[3 * C : 4 * C, :] = adjoint
            near_ref[4 * C + 8 :, :] = jnp.broadcast_to(log_back, (8, C))

        mz, lz, _, cz = fetch(step)
        moved = mm(split(mz), split(jnp.concatenate([m, state], axis=1)))
        gz, g = jnp.exp(cz), jnp.exp(log)
        m, state = gz * m + g * mz - moved[:, :C], gz * state + lz - moved[:, C:]
        log = log + cz
        mz, _, az, cz = fetch(back)
        mz = mz.T
        moved = mm(split(mz), split(jnp.concatenate([m_back, adjoint], axis=1)))
        gz, g = jnp.exp(cz), jnp.exp(log_back)
        m_back, adjoint = gz * m_back + g * mz - moved[:, :C], gz * adjoint + az - moved[:, C:]
        log_back = log_back + cz
    pack(out_ref, (m, state, adjoint), log)


def entry_kernel(at_ref, groups_ref, near_ref, maps_ref, out_ref, s_ref, a_ref):
    here = at_ref[0]
    _, first, _, _ = unpack(groups_ref, 0)
    _, _, last, _ = unpack(groups_ref, NX - 1)
    s_ref[...] = jnp.where(here > 0, first, 0.0)
    a_ref[...] = jnp.where(here < NX - 1, last, 0.0)
    for step in range(1, NX - 1):
        back = NX - 1 - step

        @pl.when(here > step)
        def _():
            m, state, _, log = unpack(groups_ref, step)
            s = s_ref[...]
            s_ref[...] = jnp.exp(log) * s - mm(split(m), split(s)) + state

        @pl.when(here < back)
        def _():
            m, _, adjoint, log = unpack(groups_ref, back)
            a = a_ref[...]
            a_ref[...] = jnp.exp(log) * a - mm(split(m), split(a), 0, 0) + adjoint

    s, a = s_ref[...], a_ref[...]
    g_in, g_out = (jnp.exp(near_ref[4 * C + 8 * i : 4 * C + 8 * i + 1, 0:1]) for i in range(2))
    s = g_in * s - mm(split(near_ref[0:C, :]), split(s)) + near_ref[C : 2 * C, :]
    a = g_out * a - mm(split(near_ref[2 * C : 3 * C, :]), split(a)) + near_ref[3 * C : 4 * C, :]
    out_ref[0, 0:C, :] = s
    out_ref[1, C : 2 * C, :] = a
    m, state, _, log = read_map(maps_ref, 0)
    out_ref[1, 0:C, :] = jnp.exp(log) * s - mm(split(m), split(s)) + state
    m, _, adjoint, log = read_map(maps_ref, 1)
    out_ref[0, C : 2 * C, :] = jnp.exp(log) * a - mm(split(m), split(a), 0, 0) + adjoint


def grad_kernel(
    at_z_ref, at_y_ref,
    ends_ref, hid_ref, k_ref, q_ref, do_ref, wd_ref, wb_ref,
    uhat_ref, what_ref, z0_ref, y_ref, gram_ref, qk_ref, rows_ref,
    dv_ref, e_ref, f_ref, query_side_ref, key_side_ref, share_ref, own_ref,
    sums_ref,
):
    here, mine = at_z_ref[0], at_y_ref[0]
    ii, jj = iotas()
    reset = rows_ref[10:11, 0:1].astype(jnp.int32)
    cols = rows_ref[0:8, :].T
    keys, _ = unit_rows(k_ref[...].astype(F32))
    queries = unit_rows(q_ref[...].astype(F32))[0] * SCALE
    gram, qk = gram_ref[...], qk_ref[...]
    ones = jnp.ones((8, C), BF16)
    lower = (ii >= jj).astype(BF16)
    both_heads = range(HEADS)
    gates = [gate_matrices(rows_ref, cols, h, ii, jj, reset) for h in both_heads]
    states = [ends_ref[h, 0:C, :] for h in both_heads]
    adjoints = [ends_ref[h, C : 2 * C, :] for h in both_heads]
    ss, as_ = [split(s) for s in states], [split(a) for a in adjoints]
    cotangent = [(do_ref[:, h * C : (h + 1) * C],) for h in both_heads]
    uhat = [uhat_ref[h] - mm(split(what_ref[h]), ss[h]) for h in both_heads]
    z = [z0_ref[h] + mm(split(y_ref[h]), as_[h]) for h in both_heads]
    from_out = [gates[h][2] * mm(cotangent[h], ss[h], 1, 1) for h in both_heads]
    bz = [gates[h][4] * z[h] for h in both_heads]
    us = [split(gates[h][4] * uhat[h]) for h in both_heads]
    zs, bzs = [split(a) for a in z], [split(a) for a in bz]
    from_keys = [gates[h][3] * mm(us[h], as_[h], 1, 1) for h in both_heads]
    through = [mm(bzs[h], ss[h], 1, 1) for h in both_heads]
    e = [mm(cotangent[h], us[h], 1, 1) for h in both_heads]
    f = [mm(zs[h], us[h], 1, 1) for h in both_heads]
    e = [jnp.where(gates[h][0], e[h] * gates[h][1], 0.0) for h in both_heads]
    f = [jnp.where(ii > jj, f[h] * gates[h][1] * -gates[h][4], 0.0) for h in both_heads]
    key_side = [from_keys[h] - gates[h][2] * through[h] for h in both_heads]
    h_mat = [e[h] * qk + f[h] * gram for h in both_heads]
    by_row = [
        split3(h_mat[h] + queries * from_out[h] + keys * (key_side[h] - 2.0 * from_keys[h]))
        for h in both_heads
    ]
    zu = [split3(z[h] * uhat[h]) for h in both_heads]
    dc = [sum(dot(ones, t, 1, 1) for t in by_row[h]) for h in both_heads]
    db = [sum(dot(ones, t, 1, 1) for t in zu[h]) for h in both_heads]
    for h in both_heads:
        carry = gates[h][2]
        ends = keys * from_keys[h] + carry[C - 1 : C, :] * states[h] * adjoints[h]
        tail = jnp.sum(jnp.sum(ends, axis=0, keepdims=True), axis=1, keepdims=True)
        sums_ref[h : h + 1, :] = dc[h][0:1, :] - jnp.sum(h_mat[h], axis=0, keepdims=True)
        sums_ref[2 + h : 3 + h, :] = db[h][0:1, :]
        sums_ref[4 + h : 5 + h, :] = jnp.broadcast_to(tail, (1, C))
        dv_ref[:, h * C : (h + 1) * C] = bz[h].astype(BF16)
    e_ref[...] = e[0] + e[1]
    f_ref[...] = f[0] + f[1]
    query_side_ref[...] = from_out[0] + from_out[1]
    key_side_ref[...] = key_side[0] + key_side[1]
    dc, db, tail = sums_ref[0:2, :], sums_ref[2:4, :], sums_ref[4:6, :]
    dg = sum(dot(t, lower, 1, 0) for t in split3(dc)) + tail
    beta, log_decay = rows_ref[2:4, :], rows_ref[4:6, :]
    dz = dg * rows_ref[8:10, :] * jax.nn.sigmoid(rows_ref[6:8, :])
    own_ref[0:2, :] = dz
    own_ref[2:4, :] = db * beta * (1.0 - beta)
    own_ref[4:6, :] = jnp.broadcast_to(jnp.sum(dg * log_decay, axis=1, keepdims=True), (2, C))
    own_ref[6:8, :] = jnp.broadcast_to(jnp.sum(dz, axis=1, keepdims=True), (2, C))
    grad = sum(dot(t, hid_ref[...], 1, 0) for t in split3(own_ref[0:4, :]))
    share_ref[...] = jnp.zeros_like(share_ref)
    after = lax.rem(here + 1, NZ)
    for other in range(NY):
        share_ref[here * NY + other, 0:4, :] = own_ref[0:4, :]
        for half in range(2):
            at = slice((2 * other + half) * C, (2 * other + half + 1) * C)
            share_ref[after * NY + other, 4 * half : 4 * half + 2, :] = wd_ref[:, at].astype(F32)
            share_ref[after * NY + other, 4 * half + 2 : 4 * half + 4, :] = wb_ref[:, at].astype(F32)
    for z in range(NZ):
        for half in range(2):
            at = slice((2 * z + half) * C, (2 * z + half + 1) * C)
            share_ref[z * NY + mine, 4 * half : 4 * half + 4, :] = grad[:, at]


def vector_kernel(k_ref, q_ref, e_ref, f_ref, query_side_ref, key_side_ref, dq_ref, dk_ref):
    keys, key_root = unit_rows(k_ref[...].astype(F32))
    unit_queries, query_root = unit_rows(q_ref[...].astype(F32))
    ks, qs = split(keys), split(unit_queries * SCALE)
    es, f = split(e_ref[...]), f_ref[...]
    dq = query_side_ref[...] + mm(es, ks)
    dk = key_side_ref[...] + mm(es, qs, 0, 0) + mm(split(f + f.T), ks)
    dq = dq - unit_queries * jnp.sum(unit_queries * dq, axis=-1, keepdims=True)
    dk = dk - keys * jnp.sum(keys * dk, axis=-1, keepdims=True)
    dq_ref[...] = (dq * (query_root * SCALE)).astype(BF16)
    dk_ref[...] = (dk * key_root).astype(BF16)


def sum_kernel(at_y_ref, share_ref, own_ref, out_ref):
    mine = at_y_ref[0]
    total = share_ref[mine]
    for z in range(1, NZ):
        total = total + share_ref[z * NY + mine]
    power = power_of_two(total)
    out_ref[0:8, :] = total * jnp.exp2(13.0 - power)
    lane = lax.broadcasted_iota(jnp.int32, (1, C), 1) >> 5
    sums = own_ref[4:5, :]
    for i in range(1, 4):
        sums = jnp.where(lane == i, own_ref[4 + i : 5 + i, :], sums)
    powers = jnp.floor(jnp.log2(jnp.maximum(jnp.abs(sums), 1e-30)))
    scaled = sums * jnp.exp2(-powers)
    high = jnp.floor(scaled * 256.0) * (1.0 / 256.0)
    out_ref[8:9, :] = jnp.broadcast_to(power, (1, C))
    out_ref[9:10, :] = powers
    out_ref[10:11, :] = high
    out_ref[11:12, :] = (scaled - high) * 256.0
    out_ref[12:16, :] = jnp.zeros((4, C), F32)


def hidden_kernel(at_z_ref, at_y_ref, share_ref, own_ref, wd_ref, wb_ref, hidden_ref, lg_ref, w_ref):
    here, mine = at_z_ref[0], at_y_ref[0]
    before = lax.rem(here + NZ - 1, NZ)
    for y in range(NY):
        rows = slice(4 * y, 4 * y + 4)

        @pl.when(mine == y)
        def _():
            lg_ref[rows, :] = own_ref[0:4, :]
            w_ref[4 * y : 4 * y + 2, :] = wd_ref[:, 2 * y * C : 2 * (y + 1) * C].astype(F32)
            w_ref[4 * y + 2 : 4 * y + 4, :] = wb_ref[:, 2 * y * C : 2 * (y + 1) * C].astype(F32)

        @pl.when(mine != y)
        def _():
            lg_ref[rows, :] = share_ref[here * NY + y, 0:4, :]
            w_ref[rows, 0:C] = share_ref[before * NY + y, 0:4, :]
            w_ref[rows, C : 2 * C] = share_ref[before * NY + y, 4:8, :]

    weights = w_ref[...].astype(BF16)
    hidden = sum(dot(t, weights, 0, 0) for t in split3(lg_ref[...]))
    hidden_ref[...] = hidden.astype(BF16)


def finish_kernel(parts_ref, wd_ref, wb_ref, rate_ref, bias_ref):
    per = NZ * NC
    sums = jnp.zeros((1, C), F32)
    for z in range(NZ):
        total = jnp.zeros((8, C), F32)
        for x in range(NX):
            for core in range(NC):
                part = parts_ref[x * per + z * NC + core]
                total = total + part[0:8, :] * jnp.exp2(part[8:9, :] - 13.0)
                sums = sums + (part[10:11, :] + part[11:12, :] * (1.0 / 256.0)) * jnp.exp2(part[9:10, :])
        for half in range(2):
            at = slice((2 * z + half) * C, (2 * z + half + 1) * C)
            wd_ref[:, at] = total[4 * half : 4 * half + 2, :]
            wb_ref[:, at] = total[4 * half + 2 : 4 * half + 4, :]
    lane = lax.broadcasted_iota(jnp.int32, (1, C), 1)
    for i in range(2):
        rate_ref[i] = jnp.sum(jnp.where(lane == 32 * i, sums, 0.0))
        bias_ref[i] = jnp.sum(jnp.where(lane == 64 + 32 * i, sums, 0.0))


VMEM = pl.BlockSpec(memory_space=pltpu.VMEM)
SMEM = pl.BlockSpec(memory_space=pltpu.SMEM)
HBM = pl.BlockSpec(memory_space=pltpu.HBM)


def call(kernel, scalars, arrays, outs, scratch=(), space=VMEM, small=0, flops=0, vmem=40 << 20):
    return pl.pallas_call(
        kernel,
        out_shape=tuple(jax.ShapeDtypeStruct(s, t) for s, t in outs),
        in_specs=[SMEM] * len(scalars) + [space] * len(arrays),
        out_specs=tuple([VMEM] * (len(outs) - small) + [SMEM] * small),
        scratch_shapes=list(scratch),
        compiler_params=pltpu.CompilerParams(vmem_limit_bytes=vmem),
        cost_estimate=pl.CostEstimate(flops=flops, bytes_accessed=1 << 20, transcendentals=0) if flops else None,
    )(*scalars, *arrays)


def exchange(a, axes):
    return lax.all_to_all(a, axes, 0, 0, tiled=True)


def spread(a, count, axes):
    a = jnp.broadcast_to(a.astype(F16), (count, *a.shape))
    return exchange(a, axes).astype(F32)


def on_device(hidden, queries, keys, values, cotangent, w_decay, w_beta, rate, bias, doc_start):
    at_x = lax.axis_index("x").astype(jnp.int32)
    at_z = lax.axis_index("z").astype(jnp.int32)
    at_core = lax.axis_index("core").astype(jnp.int32)
    at_y = lax.axis_index("dp").astype(jnp.int32)
    first = ((at_x * NZ + at_z) * NC + at_core) * C
    at_x, at_y, at_z, first = (a[None] for a in (at_x, at_y, at_z, first))
    wd, wb = w_decay.T, w_beta.T
    square, heads, wide = (C, C), (HEADS, C, C), (C, HEADS * C)
    maps, wu, inverse, pdo, gram, qk, rows = call(
        local_kernel,
        (first,),
        (doc_start, rate, bias, keys, hidden, wd, wb, queries, values, cotangent),
        [
            ((HEADS, MAP_ROWS, C), F32),
            ((HEADS, C, 2 * C), F32),
            (heads, F32),
            (heads, F32),
            (square, F32),
            (square, F32),
            ((16, C), F32),
        ],
        [
            pltpu.SMEM((1,), jnp.int32),
            pltpu.SMEM((2,), F32),
            pltpu.SMEM((2,), F32),
            pltpu.VMEM(square, BF16),
            pltpu.VMEM((C, D), BF16),
            pltpu.VMEM((2, D), BF16),
            pltpu.VMEM((2, D), BF16),
            pltpu.VMEM(square, BF16),
            pltpu.VMEM(wide, BF16),
            pltpu.VMEM(wide, BF16),
            pltpu.SemaphoreType.DMA((10,)),
        ],
        HBM,
        vmem=FULL_VMEM,
    )
    maps = exchange(maps, "core")
    (packed,) = call(pair_kernel, (), (maps,), [((PACKED_ROWS, C), F32)])
    ring = spread(packed, NZ, "z")
    packed, near, uhat, what, z0, y = call(
        ring_kernel,
        (at_z,),
        (ring, keys, values, wu, inverse, pdo, gram, rows),
        [((PACKED_ROWS, C), F32), ((4 * C + 16, C), F32)] + [(heads, F32)] * 4,
    )
    groups = spread(packed, NX, "x")
    (ends,) = call(
        entry_kernel,
        (at_x,),
        (groups, near, maps),
        [((NC, 2 * C, C), F32)],
        [pltpu.VMEM(square, F32), pltpu.VMEM(square, F32)],
    )
    ends = exchange(ends, "core")
    dv, e, f, query_side, key_side, share, own = call(
        grad_kernel,
        (at_z, at_y),
        (ends, hidden, keys, queries, cotangent, wd, wb, uhat, what, z0, y, gram, qk, rows),
        [(wide, BF16)] + [(square, F32)] * 4 + [((NZ * NY, 8, C), F32), ((8, C), F32)],
        [pltpu.VMEM((8, C), F32)],
    )
    share = exchange(share, ("z", "dp"))
    dq, dk = call(
        vector_kernel,
        (),
        (keys, queries, e, f, query_side, key_side),
        [(square, BF16), (square, BF16)],
        flops=1 << 28,
    )
    (sums,) = call(sum_kernel, (at_y,), (share, own), [((16, C), F32)])
    parts = spread(sums, NX * NZ * NC, CTX)
    (hidden_grad,) = call(
        hidden_kernel,
        (at_z, at_y),
        (share, own, wd, wb),
        [(wide, BF16)],
        [pltpu.VMEM((4 * NY, C), F32), pltpu.VMEM((4 * NY, 2 * C), F32)],
        flops=1 << 28,
    )
    wd_grad, wb_grad, rate_grad, bias_grad = call(
        finish_kernel,
        (),
        (parts,),
        [((2, D), F32), ((2, D), F32), ((HEADS,), F32), ((HEADS,), F32)],
        small=2,
    )
    return (dq, dk, dv, hidden_grad, wd_grad.T, wb_grad.T, rate_grad, bias_grad)


def solution(mesh):
    fine = Mesh(mesh.devices.reshape(NX, NZ, NC, NY), ("x", "z", "core", "dp"))
    rows, both, cols = P(CTX, None), P(CTX, "dp"), P(None, "dp")
    return jax.shard_map(
        on_device,
        mesh=fine,
        in_specs=(rows, both, both, both, both, cols, cols, P("dp"), P("dp"), P()),
        out_specs=(both, both, both, both, cols, cols, P("dp"), P("dp")),
        check_vma=False,
    )
```

```python
import functools

import jax
import jax.numpy as jnp
from jax import lax
from jax.experimental import pallas as pl
from jax.experimental.pallas import tpu as pltpu
from jax.sharding import Mesh
from jax.sharding import PartitionSpec as P

F32 = jnp.float32
BF16 = jnp.bfloat16
F16 = jnp.float16
C = 128
HEADS = 2
D = 2048
NX, NZ, NC, NY = 4, 8, 2, 8
CTX = ("x", "z", "core")
norm_epsilon = 1e-06
SCALE = C**-0.5
MAP_ROWS = 3 * C


def split(a):
    high = a.astype(BF16)
    return (high, (a - high.astype(F32)).astype(BF16))


def split3(a):
    high = a.astype(BF16)
    rest = a - high.astype(F32)
    middle = rest.astype(BF16)
    return (high, middle, (rest - middle.astype(F32)).astype(BF16))


def dot(a, b, ca, cb):
    return lax.dot_general(a, b, (((ca,), (cb,)), ((), ())), preferred_element_type=F32)


def mm(a, b, ca=1, cb=0):
    if len(a) == len(b) == 2 and (ca, cb) != (0, 1):
        return dot(jnp.concatenate([a[0], a[0], a[1]], axis=ca), jnp.concatenate([b[0], b[1], b[0]], axis=cb), ca, cb)
    total = dot(a[0], b[0], ca, cb)
    for i in range(len(a)):
        for j in range(len(b)):
            if 0 < i + j < max(len(a), len(b)):
                total = total + dot(a[i], b[j], ca, cb)
    return total


def iotas():
    return (
        lax.broadcasted_iota(jnp.int32, (C, C), 0),
        lax.broadcasted_iota(jnp.int32, (C, C), 1),
    )


def pair_column(first, second):
    row = lax.broadcasted_iota(jnp.int32, (HEADS, C), 0)
    return jnp.where(row == 0, first, second)


def unit_rows(source):
    root = lax.rsqrt(jnp.sum(source * source, axis=-1, keepdims=True) + norm_epsilon)
    return source * root, root


def gate_matrices(rows_ref, cols, h, ii, jj, reset):
    keep = jnp.logical_and(ii >= jj, jnp.logical_or(jj >= reset, ii < reset))
    ii_col = ii[:, 0:1]
    c_col, c_row = cols[:, h : h + 1], rows_ref[h : h + 1, :]
    decay = jnp.where(keep, jnp.exp(jnp.where(keep, c_col - c_row, 0.0)), 0.0)
    carry = jnp.where(ii_col < reset, jnp.exp(c_col), 0.0)
    c_last = c_col[C - 1 : C, :]
    late = jnp.logical_or(ii_col >= reset, reset > C - 1)
    weight = jnp.where(late, jnp.exp(jnp.where(late, c_last - c_col, 0.0)), 0.0)
    return keep, decay, carry, weight, cols[:, 2 + h : 3 + h], c_last


def local_kernel(
    at_ref, _x_ref, _y_ref, _z_ref, doc_ref, rate_hbm, bias_hbm, k_hbm, hid_hbm, wd_hbm, wb_hbm, q_hbm, v_hbm, do_hbm,
    map_ref, uhat_ref, what_ref, z0_ref, y_ref, gram_ref, qk_ref, rows_ref,
    rate_ref, bias_ref, k_ref, hid_ref, wd_ref, wb_ref, q_ref, v_ref, do_ref, sems,
):
    pairs = (
        (hid_hbm, hid_ref), (wd_hbm, wd_ref), (wb_hbm, wb_ref), (rate_hbm, rate_ref), (bias_hbm, bias_ref),
        (k_hbm, k_ref), (q_hbm, q_ref), (v_hbm, v_ref), (do_hbm, do_ref),
    )
    copies = [pltpu.make_async_copy(a, b, sems.at[i]) for i, (a, b) in enumerate(pairs)]
    for copy in copies:
        copy.start()
    ii, jj = iotas()
    copies[5].wait()
    copies[6].wait()
    keys, _ = unit_rows(k_ref[...].astype(F32))
    queries, _ = unit_rows(q_ref[...].astype(F32))
    queries = queries * SCALE
    ks, qs = split(keys), split(queries)
    gram = mm(ks, ks, 1, 1)
    qk = mm(qs, ks, 1, 1)
    gram_ref[...] = gram
    qk_ref[...] = qk
    for copy in copies[:5]:
        copy.wait()
    reset = doc_ref[0] - at_ref[0]
    reset = jnp.where(reset < 0, C, jnp.minimum(reset, C))
    zd = dot(wd_ref[...], hid_ref[...], 1, 1)
    zb = dot(wb_ref[...], hid_ref[...], 1, 1)
    x = zd + pair_column(bias_ref[0], bias_ref[1])
    soft = jnp.maximum(x, 0.0) + jnp.log1p(jnp.exp(-jnp.abs(x)))
    slope = -jnp.exp(pair_column(rate_ref[0], rate_ref[1]))
    log_decay = slope * soft
    upper = (ii <= jj).astype(BF16)
    rows_ref[0:2, :] = sum(dot(t, upper, 1, 0) for t in split3(log_decay))
    rows_ref[2:4, :] = jax.nn.sigmoid(zb)
    rows_ref[4:6, :] = log_decay
    rows_ref[6:8, :] = x
    rows_ref[8:10, :] = slope
    rows_ref[10:16, :] = jnp.broadcast_to(reset.astype(F32), (6, C))
    cols = rows_ref[0:8, :].T
    copies[7].wait()
    copies[8].wait()
    eye = jnp.where(ii == jj, 1.0, 0.0).astype(F32)
    both_heads = range(HEADS)
    gates = [gate_matrices(rows_ref, cols, h, ii, jj, reset) for h in both_heads]
    inner = [jnp.where(ii > jj, g[1] * gram, 0.0) for g in gates]
    coupling = [g[4] * i for g, i in zip(gates, inner)]
    inverse = [eye - jnp.where((ii & 1) * (ii - jj) == 1, c, 0.0) for c in coupling]
    for level in (1, 3, 5):
        same = (ii >> (level + 2)) == (jj >> (level + 2))
        between = jnp.logical_and(same, (ii >> level) > (jj >> level))
        part = [split(jnp.where(between, c, 0.0)) for c in coupling]
        xs = [split(x) for x in inverse]
        links = [split(mm(xs[h], part[h])) for h in both_heads]
        twice = [split(mm(p, p)) for p in links]
        inverse = [inverse[h] - mm(links[h], xs[h]) for h in both_heads]
        inverse = [inverse[h] + mm(twice[h], split(inverse[h])) for h in both_heads]
    xs = [split(x) for x in inverse]
    cotangent = [(do_ref[:, h * C : (h + 1) * C],) for h in both_heads]
    ps = [split(qk * g[1]) for g in gates]
    both = [
        jnp.concatenate([g[2] * keys, v_ref[:, h * C : (h + 1) * C].astype(F32)], axis=1)
        for h, g in enumerate(gates)
    ]
    right = [split(g[4] * b) for g, b in zip(gates, both)]
    wu = [split(mm(xs[h], right[h])) for h in both_heads]
    pdo = [mm(ps[h], cotangent[h], 0, 0) for h in both_heads]
    keys_out = [g[3] * keys for g in gates]
    ml = [mm(split(keys_out[h]), wu[h], 0, 0) for h in both_heads]
    reach = [mm(ps[h], tuple(t[:, :C] for t in wu[h])) for h in both_heads]
    sides = [split(jnp.concatenate([pdo[h], keys_out[h]], axis=1)) for h in both_heads]
    zy = [mm(xs[h], sides[h], 0, 0) for h in both_heads]
    hats = [both[h] - mm(split(inner[h]), wu[h]) for h in both_heads]
    effective = [split(gates[h][2] * queries - reach[h]) for h in both_heads]
    adjoint = [mm(effective[h], cotangent[h], 0, 0) for h in both_heads]
    for h in both_heads:
        left = jnp.where(reset > C - 1, 1.0 - jnp.exp(gates[h][5]), 1.0)
        map_ref[h, 0:C, :] = ml[h][:, :C] + eye * left
        map_ref[h, C : 2 * C, :] = ml[h][:, C:]
        map_ref[h, 2 * C : 3 * C, :] = adjoint[h]
        what_ref[h], uhat_ref[h] = hats[h][:, :C], hats[h][:, C:]
        z0_ref[h], y_ref[h] = zy[h][:, :C], zy[h][:, C:]


def read_map(ref, *at):
    return tuple(ref[(*at, slice(i * C, (i + 1) * C), slice(None))] for i in range(3))


def pack(out_ref, parts):
    ii, jj = iotas()
    bits = jnp.zeros((C, C), jnp.int32)
    for at, part in enumerate(parts[1:]):
        largest = jnp.max(jnp.max(jnp.abs(part), axis=0, keepdims=True), axis=1, keepdims=True)
        power = jnp.floor(jnp.log2(jnp.maximum(largest, 1e-30)))
        out_ref[(at + 1) * C : (at + 2) * C, :] = part * jnp.exp2(13.0 - power)
        code = power.astype(jnp.int32) + 256
        place = jj - 16 * at
        bits = jnp.where(jnp.logical_and(place >= 0, place < 16), (code >> (place & 15)) & 1, bits)
    n = parts[0] * 8192.0
    diagonal = jnp.maximum(n, 2.0**-13) * (1 - 2 * bits).astype(F32)
    out_ref[0:C, :] = jnp.where(ii == jj, diagonal, n)


def unpack(ref, at):
    ii, jj = iotas()
    n = ref[at, 0:C, :]
    head = jnp.logical_and(ii == jj, n < 0.0)[0:32, :]
    place = jj[0:32, :]
    weight = jnp.where(head, 1 << (place & 15), 0)
    parts = []
    for i in range(2):
        code = jnp.where((place >> 4) == i, weight, 0).astype(F32)
        code = jnp.sum(jnp.sum(code, axis=0, keepdims=True), axis=1, keepdims=True)
        parts.append(ref[at, (i + 1) * C : (i + 2) * C, :] * jnp.exp2(code - (256.0 + 13.0)))
    return jnp.where(ii == jj, jnp.abs(n), n) * (1.0 / 8192.0), *parts


def pair_kernel(maps_ref, out_ref):
    n0, l0, a0 = read_map(maps_ref, 0)
    n1, l1, a1 = read_map(maps_ref, 1)
    n0s = split(n0)
    forward = mm(split(n1), tuple(jnp.concatenate([a, b], axis=1) for a, b in zip(n0s, split(l0))))
    backward = mm(n0s, split(a1), 0, 0)
    pack(out_ref, (n0 + n1 - forward[:, :C], l0 + l1 - forward[:, C:], a0 + a1 - backward))


def ring_kernel(at_ref, maps_ref, out_ref, near_ref):
    here = at_ref[0]
    zero = jnp.zeros((C, C), F32)

    @pl.when(here == 0)
    def _():
        near_ref[0:C, :] = zero
        near_ref[C : 2 * C, :] = zero

    @pl.when(here == NZ - 1)
    def _():
        near_ref[2 * C : 3 * C, :] = zero
        near_ref[3 * C : 4 * C, :] = zero

    maps = [unpack(maps_ref, z) for z in range(NZ)]
    n, state, _ = maps[0]
    n_back, _, adjoint = maps[NZ - 1]
    n_back = n_back.T
    for step in range(1, NZ):
        back = NZ - 1 - step

        @pl.when(here == step)
        def _():
            near_ref[0:C, :] = n
            near_ref[C : 2 * C, :] = state

        @pl.when(here == back)
        def _():
            near_ref[2 * C : 3 * C, :] = n_back
            near_ref[3 * C : 4 * C, :] = adjoint

        nz, lz, _ = maps[step]
        ahead = jnp.concatenate([n, state], axis=1)
        nb, _, az = maps[back]
        nb = nb.T
        behind = jnp.concatenate([n_back, adjoint], axis=1)
        ahead = ahead - mm(split(nz), split(ahead))
        behind = behind - mm(split(nb), split(behind))
        n, state = ahead[:, :C] + nz, ahead[:, C:] + lz
        n_back, adjoint = behind[:, :C] + nb, behind[:, C:] + az
    pack(out_ref, (n, state, adjoint))


def entry_kernel(at_ref, groups_ref, near_ref, maps_ref, out_ref, s_ref, a_ref):
    here = at_ref[0]
    s_ref[...] = jnp.where(here > 0, unpack(groups_ref, 0)[1], 0.0)
    a_ref[...] = jnp.where(here < NX - 1, unpack(groups_ref, NX - 1)[2], 0.0)
    for step in range(1, NX - 1):
        back = NX - 1 - step

        @pl.when(here > step)
        def _():
            n, state, _ = unpack(groups_ref, step)
            s = s_ref[...]
            s_ref[...] = s - mm(split(n), split(s)) + state

        @pl.when(here < back)
        def _():
            n, _, adjoint = unpack(groups_ref, back)
            a = a_ref[...]
            a_ref[...] = a - mm(split(n), split(a), 0, 0) + adjoint

    s, a = s_ref[...], a_ref[...]
    s = s - mm(split(near_ref[0:C, :]), split(s)) + near_ref[C : 2 * C, :]
    a = a - mm(split(near_ref[2 * C : 3 * C, :]), split(a)) + near_ref[3 * C : 4 * C, :]
    out_ref[0, 0:C, :] = s
    out_ref[1, C : 2 * C, :] = a
    n, state, _ = read_map(maps_ref, 0)
    out_ref[1, 0:C, :] = s - mm(split(n), split(s)) + state
    n, _, adjoint = read_map(maps_ref, 1)
    out_ref[0, C : 2 * C, :] = a - mm(split(n), split(a), 0, 0) + adjoint


def grad_kernel(
    at_z_ref, at_y_ref,
    ends_ref, hid_ref, k_ref, q_ref, do_ref, wd_ref, wb_ref,
    uhat_ref, what_ref, z0_ref, y_ref, gram_ref, qk_ref, rows_ref,
    dv_ref, e_ref, f_ref, query_side_ref, key_side_ref, share_ref, own_ref,
    sums_ref,
):
    here, mine = at_z_ref[0], at_y_ref[0]
    ii, jj = iotas()
    reset = rows_ref[10:11, 0:1].astype(jnp.int32)
    cols = rows_ref[0:8, :].T
    keys, _ = unit_rows(k_ref[...].astype(F32))
    queries = unit_rows(q_ref[...].astype(F32))[0] * SCALE
    gram, qk = gram_ref[...], qk_ref[...]
    ones = jnp.ones((8, C), BF16)
    lower = (ii >= jj).astype(BF16)
    both_heads = range(HEADS)
    gates = [gate_matrices(rows_ref, cols, h, ii, jj, reset) for h in both_heads]
    states = [ends_ref[h, 0:C, :] for h in both_heads]
    adjoints = [ends_ref[h, C : 2 * C, :] for h in both_heads]
    ss, as_ = [split(s) for s in states], [split(a) for a in adjoints]
    cotangent = [(do_ref[:, h * C : (h + 1) * C],) for h in both_heads]
    uhat = [uhat_ref[h] - mm(split(what_ref[h]), ss[h]) for h in both_heads]
    z = [z0_ref[h] + mm(split(y_ref[h]), as_[h]) for h in both_heads]
    from_out = [gates[h][2] * mm(cotangent[h], ss[h], 1, 1) for h in both_heads]
    bz = [gates[h][4] * z[h] for h in both_heads]
    us = [split(gates[h][4] * uhat[h]) for h in both_heads]
    zs, bzs = [split(a) for a in z], [split(a) for a in bz]
    from_keys = [gates[h][3] * mm(us[h], as_[h], 1, 1) for h in both_heads]
    through = [mm(bzs[h], ss[h], 1, 1) for h in both_heads]
    e = [mm(cotangent[h], us[h], 1, 1) for h in both_heads]
    f = [mm(zs[h], us[h], 1, 1) for h in both_heads]
    e = [jnp.where(gates[h][0], e[h] * gates[h][1], 0.0) for h in both_heads]
    f = [jnp.where(ii > jj, f[h] * gates[h][1] * -gates[h][4], 0.0) for h in both_heads]
    key_side = [from_keys[h] - gates[h][2] * through[h] for h in both_heads]
    h_mat = [e[h] * qk + f[h] * gram for h in both_heads]
    by_row = [
        split3(h_mat[h] + queries * from_out[h] + keys * (key_side[h] - 2.0 * from_keys[h]))
        for h in both_heads
    ]
    zu = [split3(z[h] * uhat[h]) for h in both_heads]
    dc = [sum(dot(ones, t, 1, 1) for t in by_row[h]) for h in both_heads]
    db = [sum(dot(ones, t, 1, 1) for t in zu[h]) for h in both_heads]
    for h in both_heads:
        carry = gates[h][2]
        ends = keys * from_keys[h] + carry[C - 1 : C, :] * states[h] * adjoints[h]
        tail = jnp.sum(jnp.sum(ends, axis=0, keepdims=True), axis=1, keepdims=True)
        sums_ref[h : h + 1, :] = dc[h][0:1, :] - jnp.sum(h_mat[h], axis=0, keepdims=True)
        sums_ref[2 + h : 3 + h, :] = db[h][0:1, :]
        sums_ref[4 + h : 5 + h, :] = jnp.broadcast_to(tail, (1, C))
        dv_ref[:, h * C : (h + 1) * C] = bz[h].astype(BF16)
    e_ref[...] = e[0] + e[1]
    f_ref[...] = f[0] + f[1]
    query_side_ref[...] = from_out[0] + from_out[1]
    key_side_ref[...] = key_side[0] + key_side[1]
    dc, db, tail = sums_ref[0:2, :], sums_ref[2:4, :], sums_ref[4:6, :]
    dg = sum(dot(t, lower, 1, 0) for t in split3(dc)) + tail
    beta, log_decay = rows_ref[2:4, :], rows_ref[4:6, :]
    dz = dg * rows_ref[8:10, :] * jax.nn.sigmoid(rows_ref[6:8, :])
    own_ref[0:2, :] = dz
    own_ref[2:4, :] = db * beta * (1.0 - beta)
    own_ref[4:6, :] = jnp.broadcast_to(jnp.sum(dg * log_decay, axis=1, keepdims=True), (2, C))
    own_ref[6:8, :] = jnp.broadcast_to(jnp.sum(dz, axis=1, keepdims=True), (2, C))
    grad = sum(dot(t, hid_ref[...], 1, 0) for t in split3(own_ref[0:4, :]))
    share_ref[...] = jnp.zeros_like(share_ref)
    after = lax.rem(here + 1, NZ)
    for other in range(NY):
        share_ref[here * NY + other, 0:4, :] = own_ref[0:4, :]
        for half in range(2):
            at = slice((2 * other + half) * C, (2 * other + half + 1) * C)
            share_ref[after * NY + other, 4 * half : 4 * half + 2, :] = wd_ref[:, at].astype(F32)
            share_ref[after * NY + other, 4 * half + 2 : 4 * half + 4, :] = wb_ref[:, at].astype(F32)
    for z in range(NZ):
        for half in range(2):
            at = slice((2 * z + half) * C, (2 * z + half + 1) * C)
            share_ref[z * NY + mine, 4 * half : 4 * half + 4, :] = grad[:, at]


def vector_kernel(k_ref, q_ref, e_ref, f_ref, query_side_ref, key_side_ref, dq_ref, dk_ref):
    keys, key_root = unit_rows(k_ref[...].astype(F32))
    unit_queries, query_root = unit_rows(q_ref[...].astype(F32))
    ks, qs = split(keys), split(unit_queries * SCALE)
    es, f = split(e_ref[...]), f_ref[...]
    dq = query_side_ref[...] + mm(es, ks)
    dk = key_side_ref[...] + mm(es, qs, 0, 0) + mm(split(f + f.T), ks)
    dq = dq - unit_queries * jnp.sum(unit_queries * dq, axis=-1, keepdims=True)
    dk = dk - keys * jnp.sum(keys * dk, axis=-1, keepdims=True)
    dq_ref[...] = (dq * (query_root * SCALE)).astype(BF16)
    dk_ref[...] = (dk * key_root).astype(BF16)


def sum_kernel(at_y_ref, share_ref, own_ref, out_ref):
    mine = at_y_ref[0]
    total = share_ref[mine]
    for z in range(1, NZ):
        total = total + share_ref[z * NY + mine]
    largest = jnp.max(jnp.max(jnp.abs(total), axis=0, keepdims=True), axis=1, keepdims=True)
    power = jnp.floor(jnp.log2(jnp.maximum(largest, 1e-30)))
    out_ref[0:8, :] = total * jnp.exp2(13.0 - power)
    lane = lax.broadcasted_iota(jnp.int32, (1, C), 1) >> 5
    sums = own_ref[4:5, :]
    for i in range(1, 4):
        sums = jnp.where(lane == i, own_ref[4 + i : 5 + i, :], sums)
    powers = jnp.floor(jnp.log2(jnp.maximum(jnp.abs(sums), 1e-30)))
    scaled = sums * jnp.exp2(-powers)
    high = jnp.floor(scaled * 256.0) * (1.0 / 256.0)
    out_ref[8:9, :] = jnp.broadcast_to(power, (1, C))
    out_ref[9:10, :] = powers
    out_ref[10:11, :] = high
    out_ref[11:12, :] = (scaled - high) * 256.0
    out_ref[12:16, :] = jnp.zeros((4, C), F32)


def hidden_kernel(at_z_ref, at_y_ref, share_ref, own_ref, wd_ref, wb_ref, hidden_ref, lg_ref, w_ref):
    here, mine = at_z_ref[0], at_y_ref[0]
    before = lax.rem(here + NZ - 1, NZ)
    for y in range(NY):
        rows = slice(4 * y, 4 * y + 4)

        @pl.when(mine == y)
        def _():
            lg_ref[rows, :] = own_ref[0:4, :]
            w_ref[4 * y : 4 * y + 2, :] = wd_ref[:, 2 * y * C : 2 * (y + 1) * C].astype(F32)
            w_ref[4 * y + 2 : 4 * y + 4, :] = wb_ref[:, 2 * y * C : 2 * (y + 1) * C].astype(F32)

        @pl.when(mine != y)
        def _():
            lg_ref[rows, :] = share_ref[here * NY + y, 0:4, :]
            w_ref[rows, 0:C] = share_ref[before * NY + y, 0:4, :]
            w_ref[rows, C : 2 * C] = share_ref[before * NY + y, 4:8, :]

    weights = w_ref[...].astype(BF16)
    hidden = sum(dot(t, weights, 0, 0) for t in split3(lg_ref[...]))
    hidden_ref[...] = hidden.astype(BF16)


def finish_kernel(parts_ref, wd_ref, wb_ref, rate_ref, bias_ref):
    per = NZ * NC
    sums = jnp.zeros((1, C), F32)
    for z in range(NZ):
        total = jnp.zeros((8, C), F32)
        for x in range(NX):
            for core in range(NC):
                part = parts_ref[x * per + z * NC + core]
                total = total + part[0:8, :] * jnp.exp2(part[8:9, :] - 13.0)
                sums = sums + (part[10:11, :] + part[11:12, :] * (1.0 / 256.0)) * jnp.exp2(part[9:10, :])
        for half in range(2):
            at = slice((2 * z + half) * C, (2 * z + half + 1) * C)
            wd_ref[:, at] = total[4 * half : 4 * half + 2, :]
            wb_ref[:, at] = total[4 * half + 2 : 4 * half + 4, :]
    lane = lax.broadcasted_iota(jnp.int32, (1, C), 1)
    for i in range(2):
        rate_ref[i] = jnp.sum(jnp.where(lane == 32 * i, sums, 0.0))
        bias_ref[i] = jnp.sum(jnp.where(lane == 64 + 32 * i, sums, 0.0))


VMEM = pl.BlockSpec(memory_space=pltpu.VMEM)
SMEM = pl.BlockSpec(memory_space=pltpu.SMEM)
HBM = pl.BlockSpec(memory_space=pltpu.HBM)


def call(kernel, scalars, arrays, outs, scratch=(), space=VMEM, small=0, flops=0):
    if space is HBM:
        arrays = tuple(pltpu.with_memory_space_constraint(a, pltpu.HBM) for a in arrays)
    return pl.pallas_call(
        kernel,
        out_shape=tuple(jax.ShapeDtypeStruct(s, t) for s, t in outs),
        in_specs=[SMEM] * len(scalars) + [space] * len(arrays),
        out_specs=tuple([VMEM] * (len(outs) - small) + [SMEM] * small),
        scratch_shapes=list(scratch),
        compiler_params=pltpu.CompilerParams(vmem_limit_bytes=40 << 20),
        cost_estimate=pl.CostEstimate(flops=flops, bytes_accessed=1 << 20, transcendentals=0) if flops else None,
    )(*scalars, *arrays)


def exchange(a, axes):
    return lax.all_to_all(a, axes, 0, 0, tiled=True)


def spread(a, count, axes):
    a = jnp.broadcast_to(a.astype(F16), (count, *a.shape))
    return exchange(a, axes).astype(F32)


def on_device(hidden, queries, keys, values, cotangent, w_decay, w_beta, rate, bias, doc_start):
    at_x = lax.axis_index("x").astype(jnp.int32)
    at_z = lax.axis_index("z").astype(jnp.int32)
    at_core = lax.axis_index("core").astype(jnp.int32)
    at_y = lax.axis_index("dp").astype(jnp.int32)
    first = ((at_x * NZ + at_z) * NC + at_core) * C
    at_x, at_y, at_z, first = (a[None] for a in (at_x, at_y, at_z, first))
    wd, wb = w_decay.T, w_beta.T
    square, heads, wide = (C, C), (HEADS, C, C), (C, HEADS * C)
    maps, uhat, what, z0, y, gram, qk, rows = call(
        local_kernel,
        (first, at_x, at_y, at_z, doc_start),
        (rate, bias, keys, hidden, wd, wb, queries, values, cotangent),
        [((HEADS, MAP_ROWS, C), F32)] + [(heads, F32)] * 4 + [(square, F32)] * 2 + [((16, C), F32)],
        [
            pltpu.SMEM((2,), F32),
            pltpu.SMEM((2,), F32),
            pltpu.VMEM(square, BF16),
            pltpu.VMEM((C, D), BF16),
            pltpu.VMEM((2, D), BF16),
            pltpu.VMEM((2, D), BF16),
            pltpu.VMEM(square, BF16),
            pltpu.VMEM(wide, BF16),
            pltpu.VMEM(wide, BF16),
            pltpu.SemaphoreType.DMA((9,)),
        ],
        HBM,
    )
    maps = exchange(maps, "core")
    (packed,) = call(pair_kernel, (), (maps,), [((MAP_ROWS, C), F32)])
    ring = spread(packed, NZ, "z")
    packed, near = call(
        ring_kernel, (at_z,), (ring,), [((MAP_ROWS, C), F32), ((4 * C, C), F32)]
    )
    groups = spread(packed, NX, "x")
    (ends,) = call(
        entry_kernel,
        (at_x,),
        (groups, near, maps),
        [((NC, 2 * C, C), F32)],
        [pltpu.VMEM(square, F32), pltpu.VMEM(square, F32)],
    )
    ends = exchange(ends, "core")
    dv, e, f, query_side, key_side, share, own = call(
        grad_kernel,
        (at_z, at_y),
        (ends, hidden, keys, queries, cotangent, wd, wb, uhat, what, z0, y, gram, qk, rows),
        [(wide, BF16)] + [(square, F32)] * 4 + [((NZ * NY, 8, C), F32), ((8, C), F32)],
        [pltpu.VMEM((8, C), F32)],
    )
    share = exchange(share, ("z", "dp"))
    dq, dk = call(
        vector_kernel,
        (),
        (keys, queries, e, f, query_side, key_side),
        [(square, BF16), (square, BF16)],
        flops=1 << 28,
    )
    (sums,) = call(sum_kernel, (at_y,), (share, own), [((16, C), F32)])
    parts = spread(sums, NX * NZ * NC, CTX)
    (hidden_grad,) = call(
        hidden_kernel,
        (at_z, at_y),
        (share, own, wd, wb),
        [(wide, BF16)],
        [pltpu.VMEM((4 * NY, C), F32), pltpu.VMEM((4 * NY, 2 * C), F32)],
        flops=1 << 28,
    )
    wd_grad, wb_grad, rate_grad, bias_grad = call(
        finish_kernel,
        (),
        (parts,),
        [((2, D), F32), ((2, D), F32), ((HEADS,), F32), ((HEADS,), F32)],
        small=2,
    )
    return (dq, dk, dv, hidden_grad, wd_grad.T, wb_grad.T, rate_grad, bias_grad)


def solution(mesh):
    fine = Mesh(mesh.devices.reshape(NX, NZ, NC, NY), ("x", "z", "core", "dp"))
    rows, both, cols = P(CTX, None), P(CTX, "dp"), P(None, "dp")
    return jax.shard_map(
        on_device,
        mesh=fine,
        in_specs=(rows, both, both, both, both, cols, cols, P("dp"), P("dp"), P()),
        out_specs=(both, both, both, both, cols, cols, P("dp"), P("dp")),
        check_vma=False,
    )
```

```python
import functools

import jax
import jax.numpy as jnp
from jax import lax
from jax.experimental import pallas as pl
from jax.experimental.pallas import tpu as pltpu
from jax.sharding import Mesh
from jax.sharding import PartitionSpec as P

F32 = jnp.float32
BF16 = jnp.bfloat16
F16 = jnp.float16
C = 128
HEADS = 2
D = 2048
NX, NZ, NC, NY = 4, 8, 2, 8
PARTS = D // NX // C
CTX = ("x", "z", "core")
norm_epsilon = 1e-06
SCALE = C**-0.5
MAP_ROWS = 3 * C


def split(a):
    high = a.astype(BF16)
    return (high, (a - high.astype(F32)).astype(BF16))


def split3(a):
    high = a.astype(BF16)
    rest = a - high.astype(F32)
    middle = rest.astype(BF16)
    return (high, middle, (rest - middle.astype(F32)).astype(BF16))


def dot(a, b, ca, cb):
    return lax.dot_general(a, b, (((ca,), (cb,)), ((), ())), preferred_element_type=F32)


def mm(a, b, ca=1, cb=0):
    if len(a) == len(b) == 2 and (ca, cb) != (0, 1):
        return dot(jnp.concatenate([a[0], a[0], a[1]], axis=ca), jnp.concatenate([b[0], b[1], b[0]], axis=cb), ca, cb)
    total = dot(a[0], b[0], ca, cb)
    for i in range(len(a)):
        for j in range(len(b)):
            if 0 < i + j < max(len(a), len(b)):
                total = total + dot(a[i], b[j], ca, cb)
    return total


def iotas():
    return (
        lax.broadcasted_iota(jnp.int32, (C, C), 0),
        lax.broadcasted_iota(jnp.int32, (C, C), 1),
    )


def pair_column(first, second):
    row = lax.broadcasted_iota(jnp.int32, (HEADS, C), 0)
    return jnp.where(row == 0, first, second)


def unit_rows(source):
    root = lax.rsqrt(jnp.sum(source * source, axis=-1, keepdims=True) + norm_epsilon)
    return source * root, root


def gate_matrices(rows_ref, cols, h, ii, jj, reset):
    keep = jnp.logical_and(ii >= jj, jnp.logical_or(jj >= reset, ii < reset))
    ii_col = ii[:, 0:1]
    c_col, c_row = cols[:, h : h + 1], rows_ref[h : h + 1, :]
    decay = jnp.where(keep, jnp.exp(jnp.where(keep, c_col - c_row, 0.0)), 0.0)
    carry = jnp.where(ii_col < reset, jnp.exp(c_col), 0.0)
    c_last = c_col[C - 1 : C, :]
    late = jnp.logical_or(ii_col >= reset, reset > C - 1)
    weight = jnp.where(late, jnp.exp(jnp.where(late, c_last - c_col, 0.0)), 0.0)
    return keep, decay, carry, weight, cols[:, 2 + h : 3 + h], c_last


def local_kernel(
    at_ref, _x_ref, _y_ref, _z_ref, doc_ref, rate_hbm, bias_hbm, k_hbm, hid_hbm, wd_hbm, wb_hbm, q_hbm, v_hbm, do_hbm,
    map_ref, uhat_ref, what_ref, z0_ref, y_ref, gram_ref, qk_ref, rows_ref,
    rate_ref, bias_ref, k_ref, hid_ref, wd_ref, wb_ref, q_ref, v_ref, do_ref, sems,
):
    pairs = (
        (hid_hbm, hid_ref), (wd_hbm, wd_ref), (wb_hbm, wb_ref), (rate_hbm, rate_ref), (bias_hbm, bias_ref),
        (k_hbm, k_ref), (q_hbm, q_ref), (v_hbm, v_ref), (do_hbm, do_ref),
    )
    copies = [pltpu.make_async_copy(a, b, sems.at[i]) for i, (a, b) in enumerate(pairs)]
    for copy in copies:
        copy.start()
    ii, jj = iotas()
    copies[5].wait()
    copies[6].wait()
    keys, _ = unit_rows(k_ref[...].astype(F32))
    queries, _ = unit_rows(q_ref[...].astype(F32))
    queries = queries * SCALE
    ks, qs = split(keys), split(queries)
    gram = mm(ks, ks, 1, 1)
    qk = mm(qs, ks, 1, 1)
    gram_ref[...] = gram
    qk_ref[...] = qk
    for copy in copies[:5]:
        copy.wait()
    reset = doc_ref[0] - at_ref[0]
    reset = jnp.where(reset < 0, C, jnp.minimum(reset, C))
    zd = dot(wd_ref[...], hid_ref[...], 1, 1)
    zb = dot(wb_ref[...], hid_ref[...], 1, 1)
    x = zd + pair_column(bias_ref[0], bias_ref[1])
    soft = jnp.maximum(x, 0.0) + jnp.log1p(jnp.exp(-jnp.abs(x)))
    slope = -jnp.exp(pair_column(rate_ref[0], rate_ref[1]))
    log_decay = slope * soft
    upper = (ii <= jj).astype(BF16)
    rows_ref[0:2, :] = sum(dot(t, upper, 1, 0) for t in split3(log_decay))
    rows_ref[2:4, :] = jax.nn.sigmoid(zb)
    rows_ref[4:6, :] = log_decay
    rows_ref[6:8, :] = x
    rows_ref[8:10, :] = slope
    rows_ref[10:16, :] = jnp.broadcast_to(reset.astype(F32), (6, C))
    cols = rows_ref[0:8, :].T
    copies[7].wait()
    copies[8].wait()
    eye = jnp.where(ii == jj, 1.0, 0.0).astype(F32)
    both_heads = range(HEADS)
    gates = [gate_matrices(rows_ref, cols, h, ii, jj, reset) for h in both_heads]
    inner = [jnp.where(ii > jj, g[1] * gram, 0.0) for g in gates]
    coupling = [g[4] * i for g, i in zip(gates, inner)]
    inverse = [eye - jnp.where((ii & 1) * (ii - jj) == 1, c, 0.0) for c in coupling]
    for level in (1, 3, 5):
        same = (ii >> (level + 2)) == (jj >> (level + 2))
        between = jnp.logical_and(same, (ii >> level) > (jj >> level))
        part = [split(jnp.where(between, c, 0.0)) for c in coupling]
        xs = [split(x) for x in inverse]
        links = [split(mm(xs[h], part[h])) for h in both_heads]
        twice = [split(mm(p, p)) for p in links]
        inverse = [inverse[h] - mm(links[h], xs[h]) for h in both_heads]
        inverse = [inverse[h] + mm(twice[h], split(inverse[h])) for h in both_heads]
    xs = [split(x) for x in inverse]
    cotangent = [(do_ref[:, h * C : (h + 1) * C],) for h in both_heads]
    ps = [split(qk * g[1]) for g in gates]
    both = [
        jnp.concatenate([g[2] * keys, v_ref[:, h * C : (h + 1) * C].astype(F32)], axis=1)
        for h, g in enumerate(gates)
    ]
    right = [split(g[4] * b) for g, b in zip(gates, both)]
    wu = [split(mm(xs[h], right[h])) for h in both_heads]
    pdo = [mm(ps[h], cotangent[h], 0, 0) for h in both_heads]
    keys_out = [g[3] * keys for g in gates]
    ml = [mm(split(keys_out[h]), wu[h], 0, 0) for h in both_heads]
    reach = [mm(ps[h], tuple(t[:, :C] for t in wu[h])) for h in both_heads]
    sides = [split(jnp.concatenate([pdo[h], keys_out[h]], axis=1)) for h in both_heads]
    zy = [mm(xs[h], sides[h], 0, 0) for h in both_heads]
    hats = [both[h] - mm(split(inner[h]), wu[h]) for h in both_heads]
    effective = [split(gates[h][2] * queries - reach[h]) for h in both_heads]
    adjoint = [mm(effective[h], cotangent[h], 0, 0) for h in both_heads]
    for h in both_heads:
        left = jnp.where(reset > C - 1, 1.0 - jnp.exp(gates[h][5]), 1.0)
        map_ref[h, 0:C, :] = ml[h][:, :C] + eye * left
        map_ref[h, C : 2 * C, :] = ml[h][:, C:]
        map_ref[h, 2 * C : 3 * C, :] = adjoint[h]
        what_ref[h], uhat_ref[h] = hats[h][:, :C], hats[h][:, C:]
        z0_ref[h], y_ref[h] = zy[h][:, :C], zy[h][:, C:]


def read_map(ref, *at):
    return tuple(ref[(*at, slice(i * C, (i + 1) * C), slice(None))] for i in range(3))


def scaled(part):
    largest = jnp.max(jnp.max(jnp.abs(part), axis=0, keepdims=True), axis=1, keepdims=True)
    power = jnp.floor(jnp.log2(jnp.maximum(largest, 1e-30)))
    return part * jnp.exp2(13.0 - power), power


def coded(n, powers):
    ii, jj = iotas()
    bits = jnp.zeros((C, C), jnp.int32)
    for at, power in enumerate(powers):
        code = power.astype(jnp.int32) + 256
        bits = jnp.where((jj >> 4) == at, (code >> (jj & 15)) & 1, bits)
    n = n * 8192.0
    return jnp.where(ii == jj, jnp.maximum(n, 2.0**-13) * (1 - 2 * bits).astype(F32), n)


def unpack(ref, at, count):
    ii, jj = iotas()
    n = ref[at, 0:C, :]
    head = jnp.logical_and(ii == jj, n < 0.0)[0:32, :]
    place = jj[0:32, :]
    weight = jnp.where(head, 1 << (place & 15), 0)
    parts = []
    for i in range(count):
        code = jnp.where((place >> 4) == i, weight, 0).astype(F32)
        code = jnp.sum(jnp.sum(code, axis=0, keepdims=True), axis=1, keepdims=True)
        parts.append(ref[at, (i + 1) * C : (i + 2) * C, :] * jnp.exp2(code - (256.0 + 13.0)))
    return jnp.where(ii == jj, jnp.abs(n), n) * (1.0 / 8192.0), *parts


def pair_kernel(maps_ref, out_ref):
    n0, l0, a0 = read_map(maps_ref, 0)
    n1, l1, a1 = read_map(maps_ref, 1)
    n0s = split(n0)
    forward = mm(split(n1), tuple(jnp.concatenate([a, b], axis=1) for a, b in zip(n0s, split(l0))))
    backward = mm(n0s, split(a1), 0, 0)
    out_ref[C : 2 * C, :], state_power = scaled(l0 + l1 - forward[:, C:])
    out_ref[2 * C : 3 * C, :], adjoint_power = scaled(a0 + a1 - backward)
    out_ref[0:C, :] = coded(n0 + n1 - forward[:, :C], (state_power, adjoint_power))


def ring_kernel(at_x_ref, at_ref, maps_ref, out_ref, near_ref):
    here = at_ref[0]
    zero = jnp.zeros((C, C), F32)

    @pl.when(here == 0)
    def _():
        near_ref[0:C, :] = zero
        near_ref[C : 2 * C, :] = zero

    @pl.when(here == NZ - 1)
    def _():
        near_ref[2 * C : 3 * C, :] = zero
        near_ref[3 * C : 4 * C, :] = zero

    maps = [unpack(maps_ref, z, 2) for z in range(NZ)]
    n, state, _ = maps[0]
    n_back, _, adjoint = maps[NZ - 1]
    n_back = n_back.T
    for step in range(1, NZ):
        back = NZ - 1 - step

        @pl.when(here == step)
        def _():
            near_ref[0:C, :] = n
            near_ref[C : 2 * C, :] = state

        @pl.when(here == back)
        def _():
            near_ref[2 * C : 3 * C, :] = n_back
            near_ref[3 * C : 4 * C, :] = adjoint

        nz, lz, _ = maps[step]
        ahead = jnp.concatenate([n, state], axis=1)
        nb, _, az = maps[back]
        nb = nb.T
        behind = jnp.concatenate([n_back, adjoint], axis=1)
        ahead = ahead - mm(split(nz), split(ahead))
        behind = behind - mm(split(nb), split(behind))
        n, state = ahead[:, :C] + nz, ahead[:, C:] + lz
        n_back, adjoint = behind[:, :C] + nb, behind[:, C:] + az
    state, state_power = scaled(state)
    adjoint, adjoint_power = scaled(adjoint)
    onward, backward = coded(n, (state_power,)), coded(n, (adjoint_power,))
    for x in range(NX):

        @pl.when(x > at_x_ref[0])
        def _():
            out_ref[x, 0:C, :] = onward
            out_ref[x, C : 2 * C, :] = state

        @pl.when(x <= at_x_ref[0])
        def _():
            out_ref[x, 0:C, :] = backward
            out_ref[x, C : 2 * C, :] = adjoint


def entry_kernel(at_ref, groups_ref, near_ref, maps_ref, out_ref, s_ref, a_ref):
    here = at_ref[0]
    s_ref[...] = jnp.where(here > 0, unpack(groups_ref, 0, 1)[1], 0.0)
    a_ref[...] = jnp.where(here < NX - 1, unpack(groups_ref, NX - 1, 1)[1], 0.0)
    for step in range(1, NX - 1):
        back = NX - 1 - step

        @pl.when(here > step)
        def _():
            n, state = unpack(groups_ref, step, 1)
            s = s_ref[...]
            s_ref[...] = s - mm(split(n), split(s)) + state

        @pl.when(here < back)
        def _():
            n, adjoint = unpack(groups_ref, back, 1)
            a = a_ref[...]
            a_ref[...] = a - mm(split(n), split(a), 0, 0) + adjoint

    s, a = s_ref[...], a_ref[...]
    s = s - mm(split(near_ref[0:C, :]), split(s)) + near_ref[C : 2 * C, :]
    a = a - mm(split(near_ref[2 * C : 3 * C, :]), split(a)) + near_ref[3 * C : 4 * C, :]
    out_ref[0, 0:C, :] = s
    out_ref[1, C : 2 * C, :] = a
    n, state, _ = read_map(maps_ref, 0)
    out_ref[1, 0:C, :] = s - mm(split(n), split(s)) + state
    n, _, adjoint = read_map(maps_ref, 1)
    out_ref[0, C : 2 * C, :] = a - mm(split(n), split(a), 0, 0) + adjoint


def grad_kernel(
    at_x_ref, at_y_ref,
    ends_ref, hid_ref, k_ref, q_ref, do_ref, wd_ref, wb_ref,
    uhat_ref, what_ref, z0_ref, y_ref, gram_ref, qk_ref, rows_ref,
    dv_ref, e_ref, f_ref, query_side_ref, key_side_ref, share_ref, own_ref,
    sums_ref, terms_ref,
):
    here, mine = at_x_ref[0], at_y_ref[0]
    ii, jj = iotas()
    reset = rows_ref[10:11, 0:1].astype(jnp.int32)
    cols = rows_ref[0:8, :].T
    keys, _ = unit_rows(k_ref[...].astype(F32))
    queries = unit_rows(q_ref[...].astype(F32))[0] * SCALE
    gram, qk = gram_ref[...], qk_ref[...]
    lower = (ii >= jj).astype(BF16)
    both_heads = range(HEADS)
    gates = [gate_matrices(rows_ref, cols, h, ii, jj, reset) for h in both_heads]
    states = [ends_ref[h, 0:C, :] for h in both_heads]
    adjoints = [ends_ref[h, C : 2 * C, :] for h in both_heads]
    ss, as_ = [split(s) for s in states], [split(a) for a in adjoints]
    cotangent = [(do_ref[:, h * C : (h + 1) * C],) for h in both_heads]
    uhat = [uhat_ref[h] - mm(split(what_ref[h]), ss[h]) for h in both_heads]
    z = [z0_ref[h] + mm(split(y_ref[h]), as_[h]) for h in both_heads]
    from_out = [gates[h][2] * mm(cotangent[h], ss[h], 1, 1) for h in both_heads]
    bz = [gates[h][4] * z[h] for h in both_heads]
    us = [split(gates[h][4] * uhat[h]) for h in both_heads]
    zs, bzs = [split(a) for a in z], [split(a) for a in bz]
    from_keys = [gates[h][3] * mm(us[h], as_[h], 1, 1) for h in both_heads]
    through = [mm(bzs[h], ss[h], 1, 1) for h in both_heads]
    e = [mm(cotangent[h], us[h], 1, 1) for h in both_heads]
    f = [mm(zs[h], us[h], 1, 1) for h in both_heads]
    e = [jnp.where(gates[h][0], e[h] * gates[h][1], 0.0) for h in both_heads]
    f = [jnp.where(ii > jj, f[h] * gates[h][1] * -gates[h][4], 0.0) for h in both_heads]
    key_side = [from_keys[h] - gates[h][2] * through[h] for h in both_heads]
    h_mat = [e[h] * qk + f[h] * gram for h in both_heads]
    by_row = [
        h_mat[h] + queries * from_out[h] + keys * (key_side[h] - 2.0 * from_keys[h])
        for h in both_heads
    ]
    zu = [z[h] * uhat[h] for h in both_heads]
    by_lane = jnp.zeros((C, C), F32)
    for i, t in enumerate((*by_row, *zu)):
        by_lane = jnp.where(jj == i, jnp.sum(t, axis=1, keepdims=True), by_lane)
    by_lane = by_lane.T
    dc, db = by_lane[0:2, :], by_lane[2:4, :]
    for h in both_heads:
        carry = gates[h][2]
        ends = keys * from_keys[h] + carry[C - 1 : C, :] * states[h] * adjoints[h]
        tail = jnp.sum(jnp.sum(ends, axis=0, keepdims=True), axis=1, keepdims=True)
        sums_ref[h : h + 1, :] = dc[h : h + 1, :] - jnp.sum(h_mat[h], axis=0, keepdims=True)
        sums_ref[2 + h : 3 + h, :] = db[h : h + 1, :]
        sums_ref[4 + h : 5 + h, :] = jnp.broadcast_to(tail, (1, C))
        dv_ref[:, h * C : (h + 1) * C] = bz[h].astype(BF16)
    e_ref[...] = e[0] + e[1]
    f_ref[...] = f[0] + f[1]
    query_side_ref[...] = from_out[0] + from_out[1]
    key_side_ref[...] = key_side[0] + key_side[1]
    dc, db, tail = sums_ref[0:2, :], sums_ref[2:4, :], sums_ref[4:6, :]
    dg = sum(dot(t, lower, 1, 0) for t in split3(dc)) + tail
    beta, log_decay = rows_ref[2:4, :], rows_ref[4:6, :]
    dz = dg * rows_ref[8:10, :] * jax.nn.sigmoid(rows_ref[6:8, :])
    own_ref[0:2, :] = dz
    own_ref[2:4, :] = db * beta * (1.0 - beta)
    own_ref[4:6, :] = jnp.broadcast_to(jnp.sum(dg * log_decay, axis=1, keepdims=True), (2, C))
    own_ref[6:8, :] = jnp.broadcast_to(jnp.sum(dz, axis=1, keepdims=True), (2, C))
    for i, t in enumerate(split3(own_ref[0:4, :])):
        terms_ref[4 * i : 4 * i + 4, :] = t.astype(F32)
    terms_ref[12:16, :] = jnp.zeros((4, C), F32)
    grad = dot(terms_ref[...].astype(BF16), hid_ref[...], 1, 0)
    grad = grad[0:4, :] + grad[4:8, :] + grad[8:12, :]
    share_ref[...] = jnp.zeros_like(share_ref)
    for other in range(NY):
        share_ref[here * NY + other, 0:4, :] = own_ref[0:4, :]
        for half in range(2):
            at = slice((2 * other + half) * C, (2 * other + half + 1) * C)
            share_ref[here * NY + other, 4 * half + 4 : 4 * half + 6, :] = wd_ref[:, at].astype(F32)
            share_ref[here * NY + other, 4 * half + 6 : 4 * half + 8, :] = wb_ref[:, at].astype(F32)
    for x in range(NX):
        for i in range(PARTS):
            at = slice((PARTS * x + i) * C, (PARTS * x + i + 1) * C)
            share_ref[x * NY + mine, 4 * i : 4 * i + 4, :] = grad[:, at]


def vector_kernel(k_ref, q_ref, e_ref, f_ref, query_side_ref, key_side_ref, dq_ref, dk_ref):
    keys, key_root = unit_rows(k_ref[...].astype(F32))
    unit_queries, query_root = unit_rows(q_ref[...].astype(F32))
    ks, qs = split(keys), split(unit_queries * SCALE)
    es, f = split(e_ref[...]), f_ref[...]
    dq = query_side_ref[...] + mm(es, ks)
    dk = key_side_ref[...] + mm(es, qs, 0, 0) + mm(split(f + f.T), ks)
    dq = dq - unit_queries * jnp.sum(unit_queries * dq, axis=-1, keepdims=True)
    dk = dk - keys * jnp.sum(keys * dk, axis=-1, keepdims=True)
    dq_ref[...] = (dq * (query_root * SCALE)).astype(BF16)
    dk_ref[...] = (dk * key_root).astype(BF16)


def sum_kernel(at_y_ref, share_ref, own_ref, out_ref):
    mine = at_y_ref[0]
    total = share_ref[mine]
    for x in range(1, NX):
        total = total + share_ref[x * NY + mine]
    total, power = scaled(total)
    lane = lax.broadcasted_iota(jnp.int32, (1, C), 1) >> 5
    sums = own_ref[4:5, :]
    for i in range(1, 4):
        sums = jnp.where(lane == i, own_ref[4 + i : 5 + i, :], sums)
    powers = jnp.floor(jnp.log2(jnp.maximum(jnp.abs(sums), 1e-30)))
    fractions = sums * jnp.exp2(-powers)
    high = jnp.floor(fractions * 256.0) * (1.0 / 256.0)
    for i in range(PARTS):
        out_ref[:, i * C : (i + 1) * C] = total[4 * i : 4 * i + 4, :]
    out_ref[0:1, PARTS * C :] = jnp.broadcast_to(power, (1, C))
    out_ref[1:2, PARTS * C :] = powers
    out_ref[2:3, PARTS * C :] = high
    out_ref[3:4, PARTS * C :] = (fractions - high) * 256.0


def hidden_kernel(at_x_ref, at_y_ref, share_ref, own_ref, wd_ref, wb_ref, hidden_ref, lg_ref, w_ref):
    here, mine = at_x_ref[0], at_y_ref[0]
    for y in range(NY):
        rows = slice(4 * y, 4 * y + 4)

        @pl.when(mine == y)
        def _():
            lg_ref[rows, :] = own_ref[0:4, :]
            w_ref[4 * y : 4 * y + 2, :] = wd_ref[:, 2 * y * C : 2 * (y + 1) * C].astype(F32)
            w_ref[4 * y + 2 : 4 * y + 4, :] = wb_ref[:, 2 * y * C : 2 * (y + 1) * C].astype(F32)

        @pl.when(mine != y)
        def _():
            lg_ref[rows, :] = share_ref[here * NY + y, 0:4, :]
            w_ref[rows, 0:C] = share_ref[here * NY + y, 4:8, :]
            w_ref[rows, C : 2 * C] = share_ref[here * NY + y, 8:12, :]

    weights = w_ref[...].astype(BF16)
    hidden = sum(dot(t, weights, 0, 0) for t in split3(lg_ref[...]))
    hidden_ref[...] = hidden.astype(BF16)


def finish_kernel(parts_ref, wd_ref, wb_ref, rate_ref, bias_ref):
    per = NZ * NC
    sums = jnp.zeros((1, C), F32)
    for x in range(NX):
        totals = [jnp.zeros((4, C), F32)] * PARTS
        for at in range(x * per, (x + 1) * per):
            meta = parts_ref[at, :, PARTS * C :]
            scale = jnp.exp2(meta[0:1, :] - 13.0)
            totals = [t + parts_ref[at, :, i * C : (i + 1) * C] * scale for i, t in enumerate(totals)]
            sums = sums + (meta[2:3, :] + meta[3:4, :] * (1.0 / 256.0)) * jnp.exp2(meta[1:2, :])
        for i, total in enumerate(totals):
            at = slice((PARTS * x + i) * C, (PARTS * x + i + 1) * C)
            wd_ref[:, at] = total[0:2, :]
            wb_ref[:, at] = total[2:4, :]
    lane = lax.broadcasted_iota(jnp.int32, (1, C), 1)
    for i in range(2):
        rate_ref[i] = jnp.sum(jnp.where(lane == 32 * i, sums, 0.0))
        bias_ref[i] = jnp.sum(jnp.where(lane == 64 + 32 * i, sums, 0.0))


VMEM = pl.BlockSpec(memory_space=pltpu.VMEM)
SMEM = pl.BlockSpec(memory_space=pltpu.SMEM)
HBM = pl.BlockSpec(memory_space=pltpu.HBM)


def call(kernel, scalars, arrays, outs, scratch=(), space=VMEM, small=0, flops=0):
    if space is HBM:
        arrays = tuple(pltpu.with_memory_space_constraint(a, pltpu.HBM) for a in arrays)
    return pl.pallas_call(
        kernel,
        out_shape=tuple(jax.ShapeDtypeStruct(s, t) for s, t in outs),
        in_specs=[SMEM] * len(scalars) + [space] * len(arrays),
        out_specs=tuple([VMEM] * (len(outs) - small) + [SMEM] * small),
        scratch_shapes=list(scratch),
        compiler_params=pltpu.CompilerParams(vmem_limit_bytes=40 << 20),
        cost_estimate=pl.CostEstimate(flops=flops, bytes_accessed=1 << 20, transcendentals=0) if flops else None,
    )(*scalars, *arrays)


def exchange(a, axes):
    return lax.all_to_all(a, axes, 0, 0, tiled=True)


def spread(a, count, axes):
    a = jnp.broadcast_to(a.astype(F16), (count, *a.shape))
    return exchange(a, axes).astype(F32)


def on_device(hidden, queries, keys, values, cotangent, w_decay, w_beta, rate, bias, doc_start):
    at_x = lax.axis_index("x").astype(jnp.int32)
    at_z = lax.axis_index("z").astype(jnp.int32)
    at_core = lax.axis_index("core").astype(jnp.int32)
    at_y = lax.axis_index("dp").astype(jnp.int32)
    first = ((at_x * NZ + at_z) * NC + at_core) * C
    at_x, at_y, at_z, first = (a[None] for a in (at_x, at_y, at_z, first))
    wd, wb = w_decay.T, w_beta.T
    square, heads, wide = (C, C), (HEADS, C, C), (C, HEADS * C)
    maps, uhat, what, z0, y, gram, qk, rows = call(
        local_kernel,
        (first, at_x, at_y, at_z, doc_start),
        (rate, bias, keys, hidden, wd, wb, queries, values, cotangent),
        [((HEADS, MAP_ROWS, C), F32)] + [(heads, F32)] * 4 + [(square, F32)] * 2 + [((16, C), F32)],
        [
            pltpu.SMEM((2,), F32),
            pltpu.SMEM((2,), F32),
            pltpu.VMEM(square, BF16),
            pltpu.VMEM((C, D), BF16),
            pltpu.VMEM((2, D), BF16),
            pltpu.VMEM((2, D), BF16),
            pltpu.VMEM(square, BF16),
            pltpu.VMEM(wide, BF16),
            pltpu.VMEM(wide, BF16),
            pltpu.SemaphoreType.DMA((9,)),
        ],
        HBM,
    )
    maps = exchange(maps, "core")
    (packed,) = call(pair_kernel, (), (maps,), [((MAP_ROWS, C), F32)])
    ring = spread(packed, NZ, "z")
    groups, near = call(
        ring_kernel, (at_x, at_z), (ring,), [((NX, 2 * C, C), F32), ((4 * C, C), F32)]
    )
    groups = exchange(groups.astype(F16), "x").astype(F32)
    (ends,) = call(
        entry_kernel,
        (at_x,),
        (groups, near, maps),
        [((NC, 2 * C, C), F32)],
        [pltpu.VMEM(square, F32), pltpu.VMEM(square, F32)],
    )
    ends = exchange(ends, "core")
    dv, e, f, query_side, key_side, share, own = call(
        grad_kernel,
        (at_x, at_y),
        (ends, hidden, keys, queries, cotangent, wd, wb, uhat, what, z0, y, gram, qk, rows),
        [(wide, BF16)] + [(square, F32)] * 4 + [((NX * NY, 4 * PARTS, C), F32), ((8, C), F32)],
        [pltpu.VMEM((8, C), F32), pltpu.VMEM((16, C), F32)],
    )
    share = exchange(share, ("x", "dp"))
    dq, dk = call(
        vector_kernel,
        (),
        (keys, queries, e, f, query_side, key_side),
        [(square, BF16), (square, BF16)],
        flops=1 << 28,
    )
    (sums,) = call(sum_kernel, (at_y,), (share, own), [((4, (PARTS + 1) * C), F32)])
    parts = spread(sums, NX * NZ * NC, CTX)
    (hidden_grad,) = call(
        hidden_kernel,
        (at_x, at_y),
        (share, own, wd, wb),
        [(wide, BF16)],
        [pltpu.VMEM((4 * NY, C), F32), pltpu.VMEM((4 * NY, 2 * C), F32)],
        flops=1 << 28,
    )
    wd_grad, wb_grad, rate_grad, bias_grad = call(
        finish_kernel,
        (),
        (parts,),
        [((2, D), F32), ((2, D), F32), ((HEADS,), F32), ((HEADS,), F32)],
        small=2,
    )
    return (dq, dk, dv, hidden_grad, wd_grad.T, wb_grad.T, rate_grad, bias_grad)


def solution(mesh):
    fine = Mesh(mesh.devices.reshape(NX, NZ, NC, NY), ("x", "z", "core", "dp"))
    rows, both, cols = P(CTX, None), P(CTX, "dp"), P(None, "dp")
    return jax.shard_map(
        on_device,
        mesh=fine,
        in_specs=(rows, both, both, both, both, cols, cols, P("dp"), P("dp"), P()),
        out_specs=(both, both, both, both, cols, cols, P("dp"), P("dp")),
        check_vma=False,
    )
```

```python
import functools

import jax
import jax.numpy as jnp
from jax import lax
from jax.experimental import pallas as pl
from jax.experimental.pallas import tpu as pltpu
from jax.sharding import Mesh
from jax.sharding import PartitionSpec as P

F32 = jnp.float32
BF16 = jnp.bfloat16
F16 = jnp.float16
C = 128
HEADS = 2
D = 2048
NX, NZ, NC, NY = 4, 8, 2, 8
PARTS = D // NX // C
CTX = ("x", "z", "core")
norm_epsilon = 1e-06
SCALE = C**-0.5
MAP_ROWS = 3 * C


def split(a):
    high = a.astype(BF16)
    return (high, (a - high.astype(F32)).astype(BF16))


def split3(a):
    high = a.astype(BF16)
    rest = a - high.astype(F32)
    middle = rest.astype(BF16)
    return (high, middle, (rest - middle.astype(F32)).astype(BF16))


def dot(a, b, ca, cb):
    return lax.dot_general(a, b, (((ca,), (cb,)), ((), ())), preferred_element_type=F32)


def mm(a, b, ca=1, cb=0):
    if len(a) == len(b) == 2 and (ca, cb) != (0, 1):
        return dot(jnp.concatenate([a[0], a[0], a[1]], axis=ca), jnp.concatenate([b[0], b[1], b[0]], axis=cb), ca, cb)
    total = dot(a[0], b[0], ca, cb)
    for i in range(len(a)):
        for j in range(len(b)):
            if 0 < i + j < max(len(a), len(b)):
                total = total + dot(a[i], b[j], ca, cb)
    return total


def iotas():
    return (
        lax.broadcasted_iota(jnp.int32, (C, C), 0),
        lax.broadcasted_iota(jnp.int32, (C, C), 1),
    )


def pair_column(first, second):
    row = lax.broadcasted_iota(jnp.int32, (HEADS, C), 0)
    return jnp.where(row == 0, first, second)


def unit_rows(source):
    root = lax.rsqrt(jnp.sum(source * source, axis=-1, keepdims=True) + norm_epsilon)
    return source * root, root


def gate_matrices(rows_ref, cols, h, ii, jj, reset):
    keep = jnp.logical_and(ii >= jj, jnp.logical_or(jj >= reset, ii < reset))
    ii_col = ii[:, 0:1]
    c_col, c_row = cols[:, h : h + 1], rows_ref[h : h + 1, :]
    decay = jnp.where(keep, jnp.exp(jnp.where(keep, c_col - c_row, 0.0)), 0.0)
    carry = jnp.where(ii_col < reset, jnp.exp(c_col), 0.0)
    c_last = c_col[C - 1 : C, :]
    late = jnp.logical_or(ii_col >= reset, reset > C - 1)
    weight = jnp.where(late, jnp.exp(jnp.where(late, c_last - c_col, 0.0)), 0.0)
    return keep, decay, carry, weight, cols[:, 2 + h : 3 + h], c_last


def local_kernel(
    at_ref, _x_ref, _y_ref, _z_ref, doc_ref, rate_hbm, bias_hbm, k_hbm, hid_hbm, wd_hbm, wb_hbm, q_hbm, v_hbm, do_hbm,
    map_ref, uhat_ref, what_ref, z0_ref, y_ref, gram_ref, qk_ref, rows_ref,
    rate_ref, bias_ref, k_ref, hid_ref, wd_ref, wb_ref, q_ref, v_ref, do_ref, sems,
):
    pairs = (
        (hid_hbm, hid_ref), (wd_hbm, wd_ref), (wb_hbm, wb_ref), (rate_hbm, rate_ref), (bias_hbm, bias_ref),
        (k_hbm, k_ref), (q_hbm, q_ref), (v_hbm, v_ref), (do_hbm, do_ref),
    )
    copies = [pltpu.make_async_copy(a, b, sems.at[i]) for i, (a, b) in enumerate(pairs)]
    for copy in copies:
        copy.start()
    ii, jj = iotas()
    copies[5].wait()
    copies[6].wait()
    keys, _ = unit_rows(k_ref[...].astype(F32))
    queries, _ = unit_rows(q_ref[...].astype(F32))
    queries = queries * SCALE
    ks, qs = split(keys), split(queries)
    gram = mm(ks, ks, 1, 1)
    qk = mm(qs, ks, 1, 1)
    gram_ref[...] = gram
    qk_ref[...] = qk
    for copy in copies[:5]:
        copy.wait()
    reset = doc_ref[0] - at_ref[0]
    reset = jnp.where(reset < 0, C, jnp.minimum(reset, C))
    zd = dot(wd_ref[...], hid_ref[...], 1, 1)
    zb = dot(wb_ref[...], hid_ref[...], 1, 1)
    x = zd + pair_column(bias_ref[0], bias_ref[1])
    soft = jnp.maximum(x, 0.0) + jnp.log1p(jnp.exp(-jnp.abs(x)))
    slope = -jnp.exp(pair_column(rate_ref[0], rate_ref[1]))
    log_decay = slope * soft
    upper = (ii <= jj).astype(BF16)
    rows_ref[0:2, :] = sum(dot(t, upper, 1, 0) for t in split3(log_decay))
    rows_ref[2:4, :] = jax.nn.sigmoid(zb)
    rows_ref[4:6, :] = log_decay
    rows_ref[6:8, :] = x
    rows_ref[8:10, :] = slope
    rows_ref[10:16, :] = jnp.broadcast_to(reset.astype(F32), (6, C))
    cols = rows_ref[0:8, :].T
    copies[7].wait()
    copies[8].wait()
    eye = jnp.where(ii == jj, 1.0, 0.0).astype(F32)
    both_heads = range(HEADS)
    gates = [gate_matrices(rows_ref, cols, h, ii, jj, reset) for h in both_heads]
    inner = [jnp.where(ii > jj, g[1] * gram, 0.0) for g in gates]
    coupling = [g[4] * i for g, i in zip(gates, inner)]
    inverse = [eye - jnp.where((ii & 1) * (ii - jj) == 1, c, 0.0) for c in coupling]
    for level in (1, 3, 5):
        same = (ii >> (level + 2)) == (jj >> (level + 2))
        between = jnp.logical_and(same, (ii >> level) > (jj >> level))
        part = [split(jnp.where(between, c, 0.0)) for c in coupling]
        xs = [split(x) for x in inverse]
        links = [split(mm(xs[h], part[h])) for h in both_heads]
        twice = [split(mm(p, p)) for p in links]
        inverse = [inverse[h] - mm(links[h], xs[h]) for h in both_heads]
        inverse = [inverse[h] + mm(twice[h], split(inverse[h])) for h in both_heads]
    xs = [split(x) for x in inverse]
    cotangent = [(do_ref[:, h * C : (h + 1) * C],) for h in both_heads]
    ps = [split(qk * g[1]) for g in gates]
    both = [
        jnp.concatenate([g[2] * keys, v_ref[:, h * C : (h + 1) * C].astype(F32)], axis=1)
        for h, g in enumerate(gates)
    ]
    right = [split(g[4] * b) for g, b in zip(gates, both)]
    wu = [split(mm(xs[h], right[h])) for h in both_heads]
    pdo = [mm(ps[h], cotangent[h], 0, 0) for h in both_heads]
    keys_out = [g[3] * keys for g in gates]
    ml = [mm(split(keys_out[h]), wu[h], 0, 0) for h in both_heads]
    reach = [mm(ps[h], tuple(t[:, :C] for t in wu[h])) for h in both_heads]
    sides = [split(jnp.concatenate([pdo[h], keys_out[h]], axis=1)) for h in both_heads]
    zy = [mm(xs[h], sides[h], 0, 0) for h in both_heads]
    hats = [both[h] - mm(split(inner[h]), wu[h]) for h in both_heads]
    effective = [split(gates[h][2] * queries - reach[h]) for h in both_heads]
    adjoint = [mm(effective[h], cotangent[h], 0, 0) for h in both_heads]
    for h in both_heads:
        left = jnp.where(reset > C - 1, 1.0 - jnp.exp(gates[h][5]), 1.0)
        map_ref[h, 0:C, :] = ml[h][:, :C] + eye * left
        map_ref[h, C : 2 * C, :] = ml[h][:, C:]
        map_ref[h, 2 * C : 3 * C, :] = adjoint[h]
        what_ref[h], uhat_ref[h] = hats[h][:, :C], hats[h][:, C:]
        z0_ref[h], y_ref[h] = zy[h][:, :C], zy[h][:, C:]


def read_map(ref, *at):
    return tuple(ref[(*at, slice(i * C, (i + 1) * C), slice(None))] for i in range(3))


def scaled(part):
    largest = jnp.max(jnp.max(jnp.abs(part), axis=0, keepdims=True), axis=1, keepdims=True)
    power = jnp.floor(jnp.log2(jnp.maximum(largest, 1e-30)))
    return part * jnp.exp2(13.0 - power), power


def coded(n, powers):
    ii, jj = iotas()
    bits = jnp.zeros((C, C), jnp.int32)
    for at, power in enumerate(powers):
        code = power.astype(jnp.int32) + 256
        bits = jnp.where((jj >> 4) == at, (code >> (jj & 15)) & 1, bits)
    n = n * 8192.0
    return jnp.where(ii == jj, jnp.maximum(n, 2.0**-13) * (1 - 2 * bits).astype(F32), n)


def unpack(ref, at, count):
    ii, jj = iotas()
    n = ref[at, 0:C, :]
    head = jnp.logical_and(ii == jj, n < 0.0)[0:32, :]
    place = jj[0:32, :]
    weight = jnp.where(head, 1 << (place & 15), 0)
    parts = []
    for i in range(count):
        code = jnp.where((place >> 4) == i, weight, 0).astype(F32)
        code = jnp.sum(jnp.sum(code, axis=0, keepdims=True), axis=1, keepdims=True)
        parts.append(ref[at, (i + 1) * C : (i + 2) * C, :] * jnp.exp2(code - (256.0 + 13.0)))
    return jnp.where(ii == jj, jnp.abs(n), n) * (1.0 / 8192.0), *parts


def pair_kernel(maps_ref, out_ref):
    n0, l0, a0 = read_map(maps_ref, 0)
    n1, l1, a1 = read_map(maps_ref, 1)
    n0s = split(n0)
    forward = mm(split(n1), tuple(jnp.concatenate([a, b], axis=1) for a, b in zip(n0s, split(l0))))
    backward = mm(n0s, split(a1), 0, 0)
    out_ref[C : 2 * C, :], state_power = scaled(l0 + l1 - forward[:, C:])
    out_ref[2 * C : 3 * C, :], adjoint_power = scaled(a0 + a1 - backward)
    out_ref[0:C, :] = coded(n0 + n1 - forward[:, :C], (state_power, adjoint_power))


def ring_kernel(at_x_ref, at_ref, maps_ref, out_ref, near_ref):
    here = at_ref[0]
    zero = jnp.zeros((C, C), F32)

    @pl.when(here == 0)
    def _():
        near_ref[0:C, :] = zero
        near_ref[C : 2 * C, :] = zero

    @pl.when(here == NZ - 1)
    def _():
        near_ref[2 * C : 3 * C, :] = zero
        near_ref[3 * C : 4 * C, :] = zero

    maps = [unpack(maps_ref, z, 2) for z in range(NZ)]
    n, state, _ = maps[0]
    n_back, _, adjoint = maps[NZ - 1]
    n_back = n_back.T
    for step in range(1, NZ):
        back = NZ - 1 - step

        @pl.when(here == step)
        def _():
            near_ref[0:C, :] = n
            near_ref[C : 2 * C, :] = state

        @pl.when(here == back)
        def _():
            near_ref[2 * C : 3 * C, :] = n_back
            near_ref[3 * C : 4 * C, :] = adjoint

        nz, lz, _ = maps[step]
        ahead = jnp.concatenate([n, state], axis=1)
        nb, _, az = maps[back]
        nb = nb.T
        behind = jnp.concatenate([n_back, adjoint], axis=1)
        ahead = ahead - mm(split(nz), split(ahead))
        behind = behind - mm(split(nb), split(behind))
        n, state = ahead[:, :C] + nz, ahead[:, C:] + lz
        n_back, adjoint = behind[:, :C] + nb, behind[:, C:] + az
    state, state_power = scaled(state)
    adjoint, adjoint_power = scaled(adjoint)
    onward, backward = coded(n, (state_power,)), coded(n, (adjoint_power,))
    for x in range(NX):

        @pl.when(x > at_x_ref[0])
        def _():
            out_ref[x, 0:C, :] = onward
            out_ref[x, C : 2 * C, :] = state

        @pl.when(x <= at_x_ref[0])
        def _():
            out_ref[x, 0:C, :] = backward
            out_ref[x, C : 2 * C, :] = adjoint


def entry_kernel(at_ref, groups_ref, near_ref, maps_ref, out_ref, s_ref, a_ref):
    here = at_ref[0]
    s_ref[...] = jnp.where(here > 0, unpack(groups_ref, 0, 1)[1], 0.0)
    a_ref[...] = jnp.where(here < NX - 1, unpack(groups_ref, NX - 1, 1)[1], 0.0)
    for step in range(1, NX - 1):
        back = NX - 1 - step

        @pl.when(here > step)
        def _():
            n, state = unpack(groups_ref, step, 1)
            s = s_ref[...]
            s_ref[...] = s - mm(split(n), split(s)) + state

        @pl.when(here < back)
        def _():
            n, adjoint = unpack(groups_ref, back, 1)
            a = a_ref[...]
            a_ref[...] = a - mm(split(n), split(a), 0, 0) + adjoint

    s, a = s_ref[...], a_ref[...]
    s = s - mm(split(near_ref[0:C, :]), split(s)) + near_ref[C : 2 * C, :]
    a = a - mm(split(near_ref[2 * C : 3 * C, :]), split(a)) + near_ref[3 * C : 4 * C, :]
    out_ref[0, 0:C, :] = s
    out_ref[1, C : 2 * C, :] = a
    n, state, _ = read_map(maps_ref, 0)
    out_ref[1, 0:C, :] = s - mm(split(n), split(s)) + state
    n, _, adjoint = read_map(maps_ref, 1)
    out_ref[0, C : 2 * C, :] = a - mm(split(n), split(a), 0, 0) + adjoint


def grad_kernel(
    at_y_ref,
    ends_ref, hid_ref, k_ref, q_ref, do_ref, wd_ref, wb_ref,
    uhat_ref, what_ref, z0_ref, y_ref, gram_ref, qk_ref, rows_ref,
    dv_ref, e_ref, f_ref, query_side_ref, key_side_ref, share_ref, own_ref, send_ref, keep_ref,
    sums_ref, terms_ref,
):
    mine = at_y_ref[0]
    ii, jj = iotas()
    reset = rows_ref[10:11, 0:1].astype(jnp.int32)
    cols = rows_ref[0:8, :].T
    keys, _ = unit_rows(k_ref[...].astype(F32))
    queries = unit_rows(q_ref[...].astype(F32))[0] * SCALE
    gram, qk = gram_ref[...], qk_ref[...]
    lower = (ii >= jj).astype(BF16)
    both_heads = range(HEADS)
    gates = [gate_matrices(rows_ref, cols, h, ii, jj, reset) for h in both_heads]
    states = [ends_ref[h, 0:C, :] for h in both_heads]
    adjoints = [ends_ref[h, C : 2 * C, :] for h in both_heads]
    ss, as_ = [split(s) for s in states], [split(a) for a in adjoints]
    cotangent = [(do_ref[:, h * C : (h + 1) * C],) for h in both_heads]
    uhat = [uhat_ref[h] - mm(split(what_ref[h]), ss[h]) for h in both_heads]
    z = [z0_ref[h] + mm(split(y_ref[h]), as_[h]) for h in both_heads]
    from_out = [gates[h][2] * mm(cotangent[h], ss[h], 1, 1) for h in both_heads]
    bz = [gates[h][4] * z[h] for h in both_heads]
    us = [split(gates[h][4] * uhat[h]) for h in both_heads]
    zs, bzs = [split(a) for a in z], [split(a) for a in bz]
    from_keys = [gates[h][3] * mm(us[h], as_[h], 1, 1) for h in both_heads]
    through = [mm(bzs[h], ss[h], 1, 1) for h in both_heads]
    e = [mm(cotangent[h], us[h], 1, 1) for h in both_heads]
    f = [mm(zs[h], us[h], 1, 1) for h in both_heads]
    e = [jnp.where(gates[h][0], e[h] * gates[h][1], 0.0) for h in both_heads]
    f = [jnp.where(ii > jj, f[h] * gates[h][1] * -gates[h][4], 0.0) for h in both_heads]
    key_side = [from_keys[h] - gates[h][2] * through[h] for h in both_heads]
    h_mat = [e[h] * qk + f[h] * gram for h in both_heads]
    by_row = [
        h_mat[h] + queries * from_out[h] + keys * (key_side[h] - 2.0 * from_keys[h])
        for h in both_heads
    ]
    zu = [z[h] * uhat[h] for h in both_heads]
    by_lane = jnp.zeros((C, C), F32)
    for i, t in enumerate((*by_row, *zu)):
        by_lane = jnp.where(jj == i, jnp.sum(t, axis=1, keepdims=True), by_lane)
    by_lane = by_lane.T
    dc, db = by_lane[0:2, :], by_lane[2:4, :]
    for h in both_heads:
        carry = gates[h][2]
        ends = keys * from_keys[h] + carry[C - 1 : C, :] * states[h] * adjoints[h]
        tail = jnp.sum(jnp.sum(ends, axis=0, keepdims=True), axis=1, keepdims=True)
        sums_ref[h : h + 1, :] = dc[h : h + 1, :] - jnp.sum(h_mat[h], axis=0, keepdims=True)
        sums_ref[2 + h : 3 + h, :] = db[h : h + 1, :]
        sums_ref[4 + h : 5 + h, :] = jnp.broadcast_to(tail, (1, C))
        dv_ref[:, h * C : (h + 1) * C] = bz[h].astype(BF16)
    e_ref[...] = e[0] + e[1]
    f_ref[...] = f[0] + f[1]
    query_side_ref[...] = from_out[0] + from_out[1]
    key_side_ref[...] = key_side[0] + key_side[1]
    dc, db, tail = sums_ref[0:2, :], sums_ref[2:4, :], sums_ref[4:6, :]
    dg = sum(dot(t, lower, 1, 0) for t in split3(dc)) + tail
    beta, log_decay = rows_ref[2:4, :], rows_ref[4:6, :]
    dz = dg * rows_ref[8:10, :] * jax.nn.sigmoid(rows_ref[6:8, :])
    own_ref[0:2, :] = dz
    own_ref[2:4, :] = db * beta * (1.0 - beta)
    own_ref[4:6, :] = jnp.broadcast_to(jnp.sum(dg * log_decay, axis=1, keepdims=True), (2, C))
    own_ref[6:8, :] = jnp.broadcast_to(jnp.sum(dz, axis=1, keepdims=True), (2, C))
    for i, t in enumerate(split3(own_ref[0:4, :])):
        terms_ref[4 * i : 4 * i + 4, :] = t.astype(F32)
    terms_ref[12:16, :] = jnp.zeros((4, C), F32)
    grad = dot(terms_ref[...].astype(BF16), hid_ref[...], 1, 0)
    grad = grad[0:4, :] + grad[4:8, :] + grad[8:12, :]
    for x in range(NX):
        for i in range(PARTS):
            at = slice((PARTS * x + i) * C, (PARTS * x + i + 1) * C)
            share_ref[x, 4 * i : 4 * i + 4, :] = grad[:, at]
    send_ref[0:4, :] = own_ref[0:4, :]
    send_ref[4:8, :] = own_ref[0:4, :]
    for other in range(NY):

        at = other % 4

        @pl.when(mine // 4 == other // 4)
        def _():
            keep_ref[at] = weight_rows(wd_ref, wb_ref, other)

        @pl.when(mine // 4 != other // 4)
        def _():
            send_ref[8 + 8 * at : 16 + 8 * at, :] = weight_rows(wd_ref, wb_ref, other)


def weight_rows(wd_ref, wb_ref, place):
    return jnp.concatenate(
        [
            jnp.concatenate([ref[:, (2 * place + half) * C : (2 * place + half + 1) * C] for ref in (wd_ref, wb_ref)], axis=0)
            for half in range(2)
        ],
        axis=0,
    ).astype(F32)


def second_kernel(at_y_ref, got_ref, sent_ref, keep_ref, send_ref, kept_ref):
    bit = (at_y_ref[0] >> 1) & 1
    send_ref[0:4, :] = sent_ref[0:4, :]
    send_ref[4:8, :] = got_ref[0:4, :]
    for high in range(2):
        for low in range(2):
            place = 2 * high + low
            pair = (keep_ref[place], got_ref[8 + 8 * place : 16 + 8 * place, :])
            for source, rows in enumerate(pair):

                at = 2 * source + low

                @pl.when(bit == high)
                def _():
                    kept_ref[at] = rows

                @pl.when(bit != high)
                def _():
                    send_ref[8 + 8 * at : 16 + 8 * at, :] = rows


def third_kernel(at_y_ref, got_ref, sent_ref, keep_ref, send_ref, kept_ref):
    bit = at_y_ref[0] & 1
    send_ref[0:8, :] = sent_ref[0:8, :]
    send_ref[8:16, :] = got_ref[0:8, :]
    for source in range(4):
        for low in range(2):
            at = 2 * (source % 2) + low
            rows = keep_ref[at] if source < 2 else got_ref[8 + 8 * at : 16 + 8 * at, :]

            @pl.when(bit == low)
            def _():
                kept_ref[source] = rows

            @pl.when(bit != low)
            def _():
                send_ref[16 + 8 * source : 24 + 8 * source, :] = rows


def hidden_kernel(got_ref, sent_ref, keep_ref, hidden_ref, w_ref):
    for source in range(NY):
        for half in range(2):
            lanes, at = slice(half * C, (half + 1) * C), slice(4 * half, 4 * half + 4)
            if source < 4:
                rows = keep_ref[source, at, :]
            else:
                rows = got_ref[16 + 8 * (source - 4) + 4 * half : 20 + 8 * (source - 4) + 4 * half, :]
            w_ref[4 * source : 4 * source + 4, lanes] = rows
    logit_rows = jnp.concatenate([sent_ref[0:16, :], got_ref[0:16, :]], axis=0)
    weights = w_ref[...].astype(BF16)
    hidden = sum(dot(t, weights, 0, 0) for t in split3(logit_rows))
    hidden_ref[...] = hidden.astype(BF16)


def vector_kernel(k_ref, q_ref, e_ref, f_ref, query_side_ref, key_side_ref, dq_ref, dk_ref):
    keys, key_root = unit_rows(k_ref[...].astype(F32))
    unit_queries, query_root = unit_rows(q_ref[...].astype(F32))
    ks, qs = split(keys), split(unit_queries * SCALE)
    es, f = split(e_ref[...]), f_ref[...]
    dq = query_side_ref[...] + mm(es, ks)
    dk = key_side_ref[...] + mm(es, qs, 0, 0) + mm(split(f + f.T), ks)
    dq = dq - unit_queries * jnp.sum(unit_queries * dq, axis=-1, keepdims=True)
    dk = dk - keys * jnp.sum(keys * dk, axis=-1, keepdims=True)
    dq_ref[...] = (dq * (query_root * SCALE)).astype(BF16)
    dk_ref[...] = (dk * key_root).astype(BF16)


def sum_kernel(share_ref, own_ref, _send_ref, out_ref):
    total = share_ref[0]
    for x in range(1, NX):
        total = total + share_ref[x]
    total, power = scaled(total)
    lane = lax.broadcasted_iota(jnp.int32, (1, C), 1) >> 5
    sums = own_ref[4:5, :]
    for i in range(1, 4):
        sums = jnp.where(lane == i, own_ref[4 + i : 5 + i, :], sums)
    powers = jnp.floor(jnp.log2(jnp.maximum(jnp.abs(sums), 1e-30)))
    fractions = sums * jnp.exp2(-powers)
    high = jnp.floor(fractions * 256.0) * (1.0 / 256.0)
    for i in range(PARTS):
        out_ref[:, i * C : (i + 1) * C] = total[4 * i : 4 * i + 4, :]
    out_ref[0:1, PARTS * C :] = jnp.broadcast_to(power, (1, C))
    out_ref[1:2, PARTS * C :] = powers
    out_ref[2:3, PARTS * C :] = high
    out_ref[3:4, PARTS * C :] = (fractions - high) * 256.0


def finish_kernel(parts_ref, wd_ref, wb_ref, rate_ref, bias_ref):
    per = NZ * NC
    sums = jnp.zeros((1, C), F32)
    for x in range(NX):
        totals = [jnp.zeros((4, C), F32)] * PARTS
        for at in range(x * per, (x + 1) * per):
            meta = parts_ref[at, :, PARTS * C :]
            scale = jnp.exp2(meta[0:1, :] - 13.0)
            totals = [t + parts_ref[at, :, i * C : (i + 1) * C] * scale for i, t in enumerate(totals)]
            sums = sums + (meta[2:3, :] + meta[3:4, :] * (1.0 / 256.0)) * jnp.exp2(meta[1:2, :])
        for i, total in enumerate(totals):
            at = slice((PARTS * x + i) * C, (PARTS * x + i + 1) * C)
            wd_ref[:, at] = total[0:2, :]
            wb_ref[:, at] = total[2:4, :]
    lane = lax.broadcasted_iota(jnp.int32, (1, C), 1)
    for i in range(2):
        rate_ref[i] = jnp.sum(jnp.where(lane == 32 * i, sums, 0.0))
        bias_ref[i] = jnp.sum(jnp.where(lane == 64 + 32 * i, sums, 0.0))


VMEM = pl.BlockSpec(memory_space=pltpu.VMEM)
SMEM = pl.BlockSpec(memory_space=pltpu.SMEM)
HBM = pl.BlockSpec(memory_space=pltpu.HBM)


def call(kernel, scalars, arrays, outs, scratch=(), space=VMEM, small=0, flops=0):
    if space is HBM:
        arrays = tuple(pltpu.with_memory_space_constraint(a, pltpu.HBM) for a in arrays)
    return pl.pallas_call(
        kernel,
        out_shape=tuple(jax.ShapeDtypeStruct(s, t) for s, t in outs),
        in_specs=[SMEM] * len(scalars) + [space] * len(arrays),
        out_specs=tuple([VMEM] * (len(outs) - small) + [SMEM] * small),
        scratch_shapes=list(scratch),
        compiler_params=pltpu.CompilerParams(vmem_limit_bytes=40 << 20),
        cost_estimate=pl.CostEstimate(flops=flops, bytes_accessed=1 << 20, transcendentals=0) if flops else None,
    )(*scalars, *arrays)


def exchange(a, axes):
    return lax.all_to_all(a, axes, 0, 0, tiled=True)


def spread(a, count, axes):
    a = jnp.broadcast_to(a.astype(F16), (count, *a.shape))
    return exchange(a, axes).astype(F32)


def swap(a, bit):
    return lax.ppermute(a, "dp", [(i, i ^ bit) for i in range(NY)])


def on_device(hidden, queries, keys, values, cotangent, w_decay, w_beta, rate, bias, doc_start):
    at_x = lax.axis_index("x").astype(jnp.int32)
    at_z = lax.axis_index("z").astype(jnp.int32)
    at_core = lax.axis_index("core").astype(jnp.int32)
    at_y = lax.axis_index("dp").astype(jnp.int32)
    first = ((at_x * NZ + at_z) * NC + at_core) * C
    at_x, at_y, at_z, first = (a[None] for a in (at_x, at_y, at_z, first))
    wd, wb = w_decay.T, w_beta.T
    square, heads, wide = (C, C), (HEADS, C, C), (C, HEADS * C)
    maps, uhat, what, z0, y, gram, qk, rows = call(
        local_kernel,
        (first, at_x, at_y, at_z, doc_start),
        (rate, bias, keys, hidden, wd, wb, queries, values, cotangent),
        [((HEADS, MAP_ROWS, C), F32)] + [(heads, F32)] * 4 + [(square, F32)] * 2 + [((16, C), F32)],
        [
            pltpu.SMEM((2,), F32),
            pltpu.SMEM((2,), F32),
            pltpu.VMEM(square, BF16),
            pltpu.VMEM((C, D), BF16),
            pltpu.VMEM((2, D), BF16),
            pltpu.VMEM((2, D), BF16),
            pltpu.VMEM(square, BF16),
            pltpu.VMEM(wide, BF16),
            pltpu.VMEM(wide, BF16),
            pltpu.SemaphoreType.DMA((9,)),
        ],
        HBM,
    )
    maps = exchange(maps, "core")
    (packed,) = call(pair_kernel, (), (maps,), [((MAP_ROWS, C), F32)])
    ring = spread(packed, NZ, "z")
    groups, near = call(
        ring_kernel, (at_x, at_z), (ring,), [((NX, 2 * C, C), F32), ((4 * C, C), F32)]
    )
    groups = exchange(groups.astype(F16), "x").astype(F32)
    (ends,) = call(
        entry_kernel,
        (at_x,),
        (groups, near, maps),
        [((NC, 2 * C, C), F32)],
        [pltpu.VMEM(square, F32), pltpu.VMEM(square, F32)],
    )
    ends = exchange(ends, "core")
    dv, e, f, query_side, key_side, share, own, send, keep = call(
        grad_kernel,
        (at_y,),
        (ends, hidden, keys, queries, cotangent, wd, wb, uhat, what, z0, y, gram, qk, rows),
        [(wide, BF16)]
        + [(square, F32)] * 4
        + [((NX, 4 * PARTS, C), F32), ((8, C), F32), ((40, C), F32), ((4, 8, C), F32)],
        [pltpu.VMEM((8, C), F32), pltpu.VMEM((16, C), F32)],
    )
    got = swap(send, 4)
    share = exchange(share, "x")
    send, keep = call(second_kernel, (at_y,), (got, send, keep), [((40, C), F32), ((4, 8, C), F32)])
    got = swap(send, 2)
    (sums,) = call(sum_kernel, (), (share, own, send), [((4, (PARTS + 1) * C), F32)])
    parts = spread(sums, NX * NZ * NC, CTX)
    dq, dk = call(
        vector_kernel,
        (),
        (keys, queries, e, f, query_side, key_side),
        [(square, BF16), (square, BF16)],
        flops=1 << 28,
    )
    send, keep = call(third_kernel, (at_y,), (got, send, keep), [((48, C), F32), ((4, 8, C), F32)])
    got = swap(send, 1)
    (hidden_grad,) = call(
        hidden_kernel,
        (),
        (got, send, keep),
        [(wide, BF16)],
        [pltpu.VMEM((4 * NY, 2 * C), F32)],
        flops=1 << 28,
    )
    wd_grad, wb_grad, rate_grad, bias_grad = call(
        finish_kernel,
        (),
        (parts,),
        [((2, D), F32), ((2, D), F32), ((HEADS,), F32), ((HEADS,), F32)],
        small=2,
    )
    return (dq, dk, dv, hidden_grad, wd_grad.T, wb_grad.T, rate_grad, bias_grad)


def solution(mesh):
    fine = Mesh(mesh.devices.reshape(NX, NZ, NC, NY), ("x", "z", "core", "dp"))
    rows, both, cols = P(CTX, None), P(CTX, "dp"), P(None, "dp")
    return jax.shard_map(
        on_device,
        mesh=fine,
        in_specs=(rows, both, both, both, both, cols, cols, P("dp"), P("dp"), P()),
        out_specs=(both, both, both, both, cols, cols, P("dp"), P("dp")),
        check_vma=False,
    )
```

```python
import functools

import jax
import jax.numpy as jnp
from jax import lax
from jax.experimental import pallas as pl
from jax.experimental.pallas import tpu as pltpu
from jax.sharding import Mesh
from jax.sharding import PartitionSpec as P

F32 = jnp.float32
BF16 = jnp.bfloat16
F16 = jnp.float16
C = 128
HEADS = 2
D = 2048
NX, NZ, NC, NY = 4, 8, 2, 8
PARTS = D // NX // C
CTX = ("x", "z", "core")
norm_epsilon = 1e-06
SCALE = C**-0.5
MAP_ROWS = 3 * C


def split(a):
    high = a.astype(BF16)
    return (high, (a - high.astype(F32)).astype(BF16))


def split3(a):
    high = a.astype(BF16)
    rest = a - high.astype(F32)
    middle = rest.astype(BF16)
    return (high, middle, (rest - middle.astype(F32)).astype(BF16))


def dot(a, b, ca, cb):
    return lax.dot_general(a, b, (((ca,), (cb,)), ((), ())), preferred_element_type=F32)


def mm(a, b, ca=1, cb=0):
    if len(a) == len(b) == 2 and (ca, cb) != (0, 1):
        return dot(jnp.concatenate([a[0], a[0], a[1]], axis=ca), jnp.concatenate([b[0], b[1], b[0]], axis=cb), ca, cb)
    total = dot(a[0], b[0], ca, cb)
    for i in range(len(a)):
        for j in range(len(b)):
            if 0 < i + j < max(len(a), len(b)):
                total = total + dot(a[i], b[j], ca, cb)
    return total


def iotas():
    return (
        lax.broadcasted_iota(jnp.int32, (C, C), 0),
        lax.broadcasted_iota(jnp.int32, (C, C), 1),
    )


def pair_column(first, second):
    row = lax.broadcasted_iota(jnp.int32, (HEADS, C), 0)
    return jnp.where(row == 0, first, second)


def unit_rows(source):
    root = lax.rsqrt(jnp.sum(source * source, axis=-1, keepdims=True) + norm_epsilon)
    return source * root, root


def gate_matrices(rows_ref, cols, h, ii, jj, reset):
    keep = jnp.logical_and(ii >= jj, jnp.logical_or(jj >= reset, ii < reset))
    ii_col = ii[:, 0:1]
    c_col, c_row = cols[:, h : h + 1], rows_ref[h : h + 1, :]
    decay = jnp.where(keep, jnp.exp(jnp.where(keep, c_col - c_row, 0.0)), 0.0)
    carry = jnp.where(ii_col < reset, jnp.exp(c_col), 0.0)
    c_last = c_col[C - 1 : C, :]
    late = jnp.logical_or(ii_col >= reset, reset > C - 1)
    weight = jnp.where(late, jnp.exp(jnp.where(late, c_last - c_col, 0.0)), 0.0)
    return keep, decay, carry, weight, cols[:, 2 + h : 3 + h], c_last


def local_kernel(
    at_ref, _x_ref, _y_ref, _z_ref, doc_ref, rate_hbm, bias_hbm, k_hbm, hid_hbm, wd_hbm, wb_hbm, q_hbm, v_hbm, do_hbm,
    map_ref, uhat_ref, what_ref, z0_ref, y_ref, gram_ref, qk_ref, rows_ref, weights_ref,
    rate_ref, bias_ref, k_ref, hid_ref, wd_ref, wb_ref, q_ref, v_ref, do_ref, sems,
):
    pairs = (
        (hid_hbm, hid_ref), (wd_hbm, wd_ref), (wb_hbm, wb_ref), (rate_hbm, rate_ref), (bias_hbm, bias_ref),
        (k_hbm, k_ref), (q_hbm, q_ref), (v_hbm, v_ref), (do_hbm, do_ref),
    )
    copies = [pltpu.make_async_copy(a, b, sems.at[i]) for i, (a, b) in enumerate(pairs)]
    for copy in copies:
        copy.start()
    ii, jj = iotas()
    copies[5].wait()
    copies[6].wait()
    keys, _ = unit_rows(k_ref[...].astype(F32))
    queries, _ = unit_rows(q_ref[...].astype(F32))
    queries = queries * SCALE
    ks, qs = split(keys), split(queries)
    gram = mm(ks, ks, 1, 1)
    qk = mm(qs, ks, 1, 1)
    gram_ref[...] = gram
    qk_ref[...] = qk
    for copy in copies[:5]:
        copy.wait()
    reset = doc_ref[0] - at_ref[0]
    reset = jnp.where(reset < 0, C, jnp.minimum(reset, C))
    zd = dot(wd_ref[...], hid_ref[...], 1, 1)
    zb = dot(wb_ref[...], hid_ref[...], 1, 1)
    x = zd + pair_column(bias_ref[0], bias_ref[1])
    soft = jnp.maximum(x, 0.0) + jnp.log1p(jnp.exp(-jnp.abs(x)))
    slope = -jnp.exp(pair_column(rate_ref[0], rate_ref[1]))
    log_decay = slope * soft
    upper = (ii <= jj).astype(BF16)
    rows_ref[0:2, :] = sum(dot(t, upper, 1, 0) for t in split3(log_decay))
    rows_ref[2:4, :] = jax.nn.sigmoid(zb)
    rows_ref[4:6, :] = log_decay
    rows_ref[6:8, :] = x
    rows_ref[8:10, :] = slope
    rows_ref[10:16, :] = jnp.broadcast_to(reset.astype(F32), (6, C))
    for i, ref in enumerate((wd_ref, wb_ref)):
        weights = ref[...].astype(F32)
        for at in range(2 * NY):
            first = 4 * (at % 2) + 2 * i
            weights_ref[at // 2, first : first + 2, :] = weights[:, at * C : (at + 1) * C]
    cols = rows_ref[0:8, :].T
    copies[7].wait()
    copies[8].wait()
    eye = jnp.where(ii == jj, 1.0, 0.0).astype(F32)
    both_heads = range(HEADS)
    gates = [gate_matrices(rows_ref, cols, h, ii, jj, reset) for h in both_heads]
    inner = [jnp.where(ii > jj, g[1] * gram, 0.0) for g in gates]
    coupling = [g[4] * i for g, i in zip(gates, inner)]
    inverse = [eye - jnp.where((ii & 1) * (ii - jj) == 1, c, 0.0) for c in coupling]
    for level in (1, 3, 5):
        same = (ii >> (level + 2)) == (jj >> (level + 2))
        between = jnp.logical_and(same, (ii >> level) > (jj >> level))
        part = [split(jnp.where(between, c, 0.0)) for c in coupling]
        xs = [split(x) for x in inverse]
        links = [split(mm(xs[h], part[h])) for h in both_heads]
        twice = [split(mm(p, p)) for p in links]
        inverse = [inverse[h] - mm(links[h], xs[h]) for h in both_heads]
        inverse = [inverse[h] + mm(twice[h], split(inverse[h])) for h in both_heads]
    xs = [split(x) for x in inverse]
    cotangent = [(do_ref[:, h * C : (h + 1) * C],) for h in both_heads]
    ps = [split(qk * g[1]) for g in gates]
    both = [
        jnp.concatenate([g[2] * keys, v_ref[:, h * C : (h + 1) * C].astype(F32)], axis=1)
        for h, g in enumerate(gates)
    ]
    right = [split(g[4] * b) for g, b in zip(gates, both)]
    wu = [split(mm(xs[h], right[h])) for h in both_heads]
    pdo = [mm(ps[h], cotangent[h], 0, 0) for h in both_heads]
    keys_out = [g[3] * keys for g in gates]
    ml = [mm(split(keys_out[h]), wu[h], 0, 0) for h in both_heads]
    reach = [mm(ps[h], tuple(t[:, :C] for t in wu[h])) for h in both_heads]
    sides = [split(jnp.concatenate([pdo[h], keys_out[h]], axis=1)) for h in both_heads]
    zy = [mm(xs[h], sides[h], 0, 0) for h in both_heads]
    hats = [both[h] - mm(split(inner[h]), wu[h]) for h in both_heads]
    effective = [split(gates[h][2] * queries - reach[h]) for h in both_heads]
    adjoint = [mm(effective[h], cotangent[h], 0, 0) for h in both_heads]
    for h in both_heads:
        left = jnp.where(reset > C - 1, 1.0 - jnp.exp(gates[h][5]), 1.0)
        map_ref[h, 0:C, :] = ml[h][:, :C] + eye * left
        map_ref[h, C : 2 * C, :] = ml[h][:, C:]
        map_ref[h, 2 * C : 3 * C, :] = adjoint[h]
        what_ref[h], uhat_ref[h] = hats[h][:, :C], hats[h][:, C:]
        z0_ref[h], y_ref[h] = zy[h][:, :C], zy[h][:, C:]


def read_map(ref, *at):
    return tuple(ref[(*at, slice(i * C, (i + 1) * C), slice(None))] for i in range(3))


def scaled(part):
    largest = jnp.max(jnp.max(jnp.abs(part), axis=0, keepdims=True), axis=1, keepdims=True)
    power = jnp.floor(jnp.log2(jnp.maximum(largest, 1e-30)))
    return part * jnp.exp2(13.0 - power), power


def coded(n, powers):
    ii, jj = iotas()
    bits = jnp.zeros((C, C), jnp.int32)
    for at, power in enumerate(powers):
        code = power.astype(jnp.int32) + 256
        bits = jnp.where((jj >> 4) == at, (code >> (jj & 15)) & 1, bits)
    n = n * 8192.0
    return jnp.where(ii == jj, jnp.maximum(n, 2.0**-13) * (1 - 2 * bits).astype(F32), n)


def unpack(ref, at, count):
    ii, jj = iotas()
    n = ref[at, 0:C, :]
    head = jnp.logical_and(ii == jj, n < 0.0)[0:32, :]
    place = jj[0:32, :]
    weight = jnp.where(head, 1 << (place & 15), 0)
    parts = []
    for i in range(count):
        code = jnp.where((place >> 4) == i, weight, 0).astype(F32)
        code = jnp.sum(jnp.sum(code, axis=0, keepdims=True), axis=1, keepdims=True)
        parts.append(ref[at, (i + 1) * C : (i + 2) * C, :] * jnp.exp2(code - (256.0 + 13.0)))
    return jnp.where(ii == jj, jnp.abs(n), n) * (1.0 / 8192.0), *parts


def pair_kernel(maps_ref, out_ref):
    n0, l0, a0 = read_map(maps_ref, 0)
    n1, l1, a1 = read_map(maps_ref, 1)
    n0s = split(n0)
    forward = mm(split(n1), tuple(jnp.concatenate([a, b], axis=1) for a, b in zip(n0s, split(l0))))
    backward = mm(n0s, split(a1), 0, 0)
    out_ref[C : 2 * C, :], state_power = scaled(l0 + l1 - forward[:, C:])
    out_ref[2 * C : 3 * C, :], adjoint_power = scaled(a0 + a1 - backward)
    out_ref[0:C, :] = coded(n0 + n1 - forward[:, :C], (state_power, adjoint_power))


def ring_kernel(at_x_ref, at_ref, maps_ref, out_ref, near_ref):
    here = at_ref[0]
    zero = jnp.zeros((C, C), F32)

    @pl.when(here == 0)
    def _():
        near_ref[0:C, :] = zero
        near_ref[C : 2 * C, :] = zero

    @pl.when(here == NZ - 1)
    def _():
        near_ref[2 * C : 3 * C, :] = zero
        near_ref[3 * C : 4 * C, :] = zero

    maps = [unpack(maps_ref, z, 2) for z in range(NZ)]
    n, state, _ = maps[0]
    n_back, _, adjoint = maps[NZ - 1]
    n_back = n_back.T
    for step in range(1, NZ):
        back = NZ - 1 - step

        @pl.when(here == step)
        def _():
            near_ref[0:C, :] = n
            near_ref[C : 2 * C, :] = state

        @pl.when(here == back)
        def _():
            near_ref[2 * C : 3 * C, :] = n_back
            near_ref[3 * C : 4 * C, :] = adjoint

        nz, lz, _ = maps[step]
        ahead = jnp.concatenate([n, state], axis=1)
        nb, _, az = maps[back]
        nb = nb.T
        behind = jnp.concatenate([n_back, adjoint], axis=1)
        ahead = ahead - mm(split(nz), split(ahead))
        behind = behind - mm(split(nb), split(behind))
        n, state = ahead[:, :C] + nz, ahead[:, C:] + lz
        n_back, adjoint = behind[:, :C] + nb, behind[:, C:] + az
    state, state_power = scaled(state)
    adjoint, adjoint_power = scaled(adjoint)
    onward, backward = coded(n, (state_power,)), coded(n, (adjoint_power,))
    for x in range(NX):

        @pl.when(x > at_x_ref[0])
        def _():
            out_ref[x, 0:C, :] = onward
            out_ref[x, C : 2 * C, :] = state

        @pl.when(x <= at_x_ref[0])
        def _():
            out_ref[x, 0:C, :] = backward
            out_ref[x, C : 2 * C, :] = adjoint


def entry_kernel(at_ref, groups_ref, near_ref, maps_ref, out_ref, s_ref, a_ref):
    here = at_ref[0]
    s_ref[...] = jnp.where(here > 0, unpack(groups_ref, 0, 1)[1], 0.0)
    a_ref[...] = jnp.where(here < NX - 1, unpack(groups_ref, NX - 1, 1)[1], 0.0)
    for step in range(1, NX - 1):
        back = NX - 1 - step

        @pl.when(here > step)
        def _():
            n, state = unpack(groups_ref, step, 1)
            s = s_ref[...]
            s_ref[...] = s - mm(split(n), split(s)) + state

        @pl.when(here < back)
        def _():
            n, adjoint = unpack(groups_ref, back, 1)
            a = a_ref[...]
            a_ref[...] = a - mm(split(n), split(a), 0, 0) + adjoint

    s, a = s_ref[...], a_ref[...]
    s = s - mm(split(near_ref[0:C, :]), split(s)) + near_ref[C : 2 * C, :]
    a = a - mm(split(near_ref[2 * C : 3 * C, :]), split(a)) + near_ref[3 * C : 4 * C, :]
    out_ref[0, 0:C, :] = s
    out_ref[1, C : 2 * C, :] = a
    n, state, _ = read_map(maps_ref, 0)
    out_ref[1, 0:C, :] = s - mm(split(n), split(s)) + state
    n, _, adjoint = read_map(maps_ref, 1)
    out_ref[0, C : 2 * C, :] = a - mm(split(n), split(a), 0, 0) + adjoint


def grad_kernel(
    at_y_ref,
    ends_ref, hid_ref, k_ref, q_ref, do_ref, weights_ref,
    uhat_ref, what_ref, z0_ref, y_ref, gram_ref, qk_ref, rows_ref,
    dv_ref, e_ref, f_ref, query_side_ref, key_side_ref, share_ref, own_ref, send_ref, keep_ref,
    sums_ref, terms_ref,
):
    mine = at_y_ref[0]
    ii, jj = iotas()
    reset = rows_ref[10:11, 0:1].astype(jnp.int32)
    cols = rows_ref[0:8, :].T
    keys, _ = unit_rows(k_ref[...].astype(F32))
    queries = unit_rows(q_ref[...].astype(F32))[0] * SCALE
    gram, qk = gram_ref[...], qk_ref[...]
    lower = (ii >= jj).astype(BF16)
    both_heads = range(HEADS)
    gates = [gate_matrices(rows_ref, cols, h, ii, jj, reset) for h in both_heads]
    states = [ends_ref[h, 0:C, :] for h in both_heads]
    adjoints = [ends_ref[h, C : 2 * C, :] for h in both_heads]
    ss, as_ = [split(s) for s in states], [split(a) for a in adjoints]
    cotangent = [(do_ref[:, h * C : (h + 1) * C],) for h in both_heads]
    uhat = [uhat_ref[h] - mm(split(what_ref[h]), ss[h]) for h in both_heads]
    z = [z0_ref[h] + mm(split(y_ref[h]), as_[h]) for h in both_heads]
    from_out = [gates[h][2] * mm(cotangent[h], ss[h], 1, 1) for h in both_heads]
    bz = [gates[h][4] * z[h] for h in both_heads]
    us = [split(gates[h][4] * uhat[h]) for h in both_heads]
    zs, bzs = [split(a) for a in z], [split(a) for a in bz]
    from_keys = [gates[h][3] * mm(us[h], as_[h], 1, 1) for h in both_heads]
    through = [mm(bzs[h], ss[h], 1, 1) for h in both_heads]
    e = [mm(cotangent[h], us[h], 1, 1) for h in both_heads]
    f = [mm(zs[h], us[h], 1, 1) for h in both_heads]
    e = [jnp.where(gates[h][0], e[h] * gates[h][1], 0.0) for h in both_heads]
    f = [jnp.where(ii > jj, f[h] * gates[h][1] * -gates[h][4], 0.0) for h in both_heads]
    key_side = [from_keys[h] - gates[h][2] * through[h] for h in both_heads]
    h_mat = [e[h] * qk + f[h] * gram for h in both_heads]
    by_row = [
        h_mat[h] + queries * from_out[h] + keys * (key_side[h] - 2.0 * from_keys[h])
        for h in both_heads
    ]
    zu = [z[h] * uhat[h] for h in both_heads]
    by_lane = jnp.zeros((C, C), F32)
    for i, t in enumerate((*by_row, *zu)):
        by_lane = jnp.where(jj == i, jnp.sum(t, axis=1, keepdims=True), by_lane)
    by_lane = by_lane.T
    dc, db = by_lane[0:2, :], by_lane[2:4, :]
    for h in both_heads:
        carry = gates[h][2]
        ends = keys * from_keys[h] + carry[C - 1 : C, :] * states[h] * adjoints[h]
        tail = jnp.sum(jnp.sum(ends, axis=0, keepdims=True), axis=1, keepdims=True)
        sums_ref[h : h + 1, :] = dc[h : h + 1, :] - jnp.sum(h_mat[h], axis=0, keepdims=True)
        sums_ref[2 + h : 3 + h, :] = db[h : h + 1, :]
        sums_ref[4 + h : 5 + h, :] = jnp.broadcast_to(tail, (1, C))
        dv_ref[:, h * C : (h + 1) * C] = bz[h].astype(BF16)
    e_ref[...] = e[0] + e[1]
    f_ref[...] = f[0] + f[1]
    query_side_ref[...] = from_out[0] + from_out[1]
    key_side_ref[...] = key_side[0] + key_side[1]
    dc, db, tail = sums_ref[0:2, :], sums_ref[2:4, :], sums_ref[4:6, :]
    dg = sum(dot(t, lower, 1, 0) for t in split3(dc)) + tail
    beta, log_decay = rows_ref[2:4, :], rows_ref[4:6, :]
    dz = dg * rows_ref[8:10, :] * jax.nn.sigmoid(rows_ref[6:8, :])
    own_ref[0:2, :] = dz
    own_ref[2:4, :] = db * beta * (1.0 - beta)
    own_ref[4:6, :] = jnp.broadcast_to(jnp.sum(dg * log_decay, axis=1, keepdims=True), (2, C))
    own_ref[6:8, :] = jnp.broadcast_to(jnp.sum(dz, axis=1, keepdims=True), (2, C))
    for i, t in enumerate(split3(own_ref[0:4, :])):
        terms_ref[4 * i : 4 * i + 4, :] = t.astype(F32)
    terms_ref[12:16, :] = jnp.zeros((4, C), F32)
    grad = dot(terms_ref[...].astype(BF16), hid_ref[...], 1, 0)
    grad = grad[0:4, :] + grad[4:8, :] + grad[8:12, :]
    for x in range(NX):
        for i in range(PARTS):
            at = slice((PARTS * x + i) * C, (PARTS * x + i + 1) * C)
            share_ref[x, 4 * i : 4 * i + 4, :] = grad[:, at]
    send_ref[0:4, :] = own_ref[0:4, :]
    send_ref[4:8, :] = own_ref[0:4, :]
    bit = mine & 1
    for at in range(4):
        pair = weights_ref[2 * at], weights_ref[2 * at + 1]
        keep_ref[at] = jnp.where(bit == 0, pair[0], pair[1])
        send_ref[8 + 8 * at : 16 + 8 * at, :] = jnp.where(bit == 0, pair[1], pair[0])


def second_kernel(at_y_ref, got_ref, sent_ref, keep_ref, send_ref, kept_ref):
    bit = (at_y_ref[0] >> 2) & 1
    send_ref[0:4, :] = sent_ref[0:4, :]
    send_ref[4:8, :] = got_ref[0:4, :]
    for high in range(2):
        for low in range(2):
            place = 2 * high + low
            pair = (keep_ref[place], got_ref[8 + 8 * place : 16 + 8 * place, :])
            for source, rows in enumerate(pair):

                at = 2 * source + low

                @pl.when(bit == high)
                def _():
                    kept_ref[at] = rows

                @pl.when(bit != high)
                def _():
                    send_ref[8 + 8 * at : 16 + 8 * at, :] = rows


def third_kernel(at_y_ref, got_ref, sent_ref, keep_ref, send_ref, kept_ref):
    bit = (at_y_ref[0] >> 1) & 1
    send_ref[0:8, :] = sent_ref[0:8, :]
    send_ref[8:16, :] = got_ref[0:8, :]
    for source in range(4):
        for low in range(2):
            at = 2 * (source % 2) + low
            rows = keep_ref[at] if source < 2 else got_ref[8 + 8 * at : 16 + 8 * at, :]

            @pl.when(bit == low)
            def _():
                kept_ref[source] = rows

            @pl.when(bit != low)
            def _():
                send_ref[16 + 8 * source : 24 + 8 * source, :] = rows


def hidden_kernel(got_ref, sent_ref, keep_ref, _after_ref, hidden_ref, w_ref):
    for source in range(NY):
        for half in range(2):
            lanes, at = slice(half * C, (half + 1) * C), slice(4 * half, 4 * half + 4)
            if source < 4:
                rows = keep_ref[source, at, :]
            else:
                rows = got_ref[16 + 8 * (source - 4) + 4 * half : 20 + 8 * (source - 4) + 4 * half, :]
            w_ref[4 * source : 4 * source + 4, lanes] = rows
    logit_rows = jnp.concatenate([sent_ref[0:16, :], got_ref[0:16, :]], axis=0)
    weights = w_ref[...].astype(BF16)
    hidden = sum(dot(t, weights, 0, 0) for t in split3(logit_rows))
    hidden_ref[...] = hidden.astype(BF16)


def vector_kernel(k_ref, q_ref, e_ref, f_ref, query_side_ref, key_side_ref, dq_ref, dk_ref):
    keys, key_root = unit_rows(k_ref[...].astype(F32))
    unit_queries, query_root = unit_rows(q_ref[...].astype(F32))
    ks, qs = split(keys), split(unit_queries * SCALE)
    es, f = split(e_ref[...]), f_ref[...]
    dq = query_side_ref[...] + mm(es, ks)
    dk = key_side_ref[...] + mm(es, qs, 0, 0) + mm(split(f + f.T), ks)
    dq = dq - unit_queries * jnp.sum(unit_queries * dq, axis=-1, keepdims=True)
    dk = dk - keys * jnp.sum(keys * dk, axis=-1, keepdims=True)
    dq_ref[...] = (dq * (query_root * SCALE)).astype(BF16)
    dk_ref[...] = (dk * key_root).astype(BF16)


def sum_kernel(share_ref, own_ref, _send_ref, out_ref):
    total = share_ref[0]
    for x in range(1, NX):
        total = total + share_ref[x]
    total, power = scaled(total)
    lane = lax.broadcasted_iota(jnp.int32, (1, C), 1) >> 5
    sums = own_ref[4:5, :]
    for i in range(1, 4):
        sums = jnp.where(lane == i, own_ref[4 + i : 5 + i, :], sums)
    powers = jnp.floor(jnp.log2(jnp.maximum(jnp.abs(sums), 1e-30)))
    fractions = sums * jnp.exp2(-powers)
    high = jnp.floor(fractions * 256.0) * (1.0 / 256.0)
    for i in range(PARTS):
        out_ref[:, i * C : (i + 1) * C] = total[4 * i : 4 * i + 4, :]
    out_ref[0:1, PARTS * C :] = jnp.broadcast_to(power, (1, C))
    out_ref[1:2, PARTS * C :] = powers
    out_ref[2:3, PARTS * C :] = high
    out_ref[3:4, PARTS * C :] = (fractions - high) * 256.0


def finish_kernel(parts_ref, wd_ref, wb_ref, after_ref, rate_ref, bias_ref):
    after_ref[...] = jnp.zeros_like(after_ref)
    per = NZ * NC
    sums = jnp.zeros((1, C), F32)
    for x in range(NX):
        totals = [jnp.zeros((4, C), F32)] * PARTS
        for at in range(x * per, (x + 1) * per):
            meta = parts_ref[at, :, PARTS * C :]
            scale = jnp.exp2(meta[0:1, :] - 13.0)
            totals = [t + parts_ref[at, :, i * C : (i + 1) * C] * scale for i, t in enumerate(totals)]
            sums = sums + (meta[2:3, :] + meta[3:4, :] * (1.0 / 256.0)) * jnp.exp2(meta[1:2, :])
        for i, total in enumerate(totals):
            at = slice((PARTS * x + i) * C, (PARTS * x + i + 1) * C)
            wd_ref[:, at] = total[0:2, :]
            wb_ref[:, at] = total[2:4, :]
    lane = lax.broadcasted_iota(jnp.int32, (1, C), 1)
    for i in range(2):
        rate_ref[i] = jnp.sum(jnp.where(lane == 32 * i, sums, 0.0))
        bias_ref[i] = jnp.sum(jnp.where(lane == 64 + 32 * i, sums, 0.0))


VMEM = pl.BlockSpec(memory_space=pltpu.VMEM)
SMEM = pl.BlockSpec(memory_space=pltpu.SMEM)
HBM = pl.BlockSpec(memory_space=pltpu.HBM)


def call(kernel, scalars, arrays, outs, scratch=(), space=VMEM, small=0, flops=0):
    if space is HBM:
        arrays = tuple(pltpu.with_memory_space_constraint(a, pltpu.HBM) for a in arrays)
    return pl.pallas_call(
        kernel,
        out_shape=tuple(jax.ShapeDtypeStruct(s, t) for s, t in outs),
        in_specs=[SMEM] * len(scalars) + [space] * len(arrays),
        out_specs=tuple([VMEM] * (len(outs) - small) + [SMEM] * small),
        scratch_shapes=list(scratch),
        compiler_params=pltpu.CompilerParams(vmem_limit_bytes=40 << 20),
        cost_estimate=pl.CostEstimate(flops=flops, bytes_accessed=1 << 20, transcendentals=0) if flops else None,
    )(*scalars, *arrays)


def exchange(a, axes):
    return lax.all_to_all(a, axes, 0, 0, tiled=True)


def spread(a, count, axes):
    a = jnp.broadcast_to(a.astype(F16), (count, *a.shape))
    return exchange(a, axes).astype(F32)


def swap(a, bit):
    return lax.ppermute(a, "dp", [(i, i ^ bit) for i in range(NY)])


def on_device(hidden, queries, keys, values, cotangent, w_decay, w_beta, rate, bias, doc_start):
    at_x = lax.axis_index("x").astype(jnp.int32)
    at_z = lax.axis_index("z").astype(jnp.int32)
    at_core = lax.axis_index("core").astype(jnp.int32)
    at_y = lax.axis_index("dp").astype(jnp.int32)
    first = ((at_x * NZ + at_z) * NC + at_core) * C
    at_x, at_y, at_z, first = (a[None] for a in (at_x, at_y, at_z, first))
    wd, wb = w_decay.T, w_beta.T
    square, heads, wide = (C, C), (HEADS, C, C), (C, HEADS * C)
    maps, uhat, what, z0, y, gram, qk, rows, weights = call(
        local_kernel,
        (first, at_x, at_y, at_z, doc_start),
        (rate, bias, keys, hidden, wd, wb, queries, values, cotangent),
        [((HEADS, MAP_ROWS, C), F32)] + [(heads, F32)] * 4 + [(square, F32)] * 2 + [((16, C), F32), ((NY, 8, C), F32)],
        [
            pltpu.SMEM((2,), F32),
            pltpu.SMEM((2,), F32),
            pltpu.VMEM(square, BF16),
            pltpu.VMEM((C, D), BF16),
            pltpu.VMEM((2, D), BF16),
            pltpu.VMEM((2, D), BF16),
            pltpu.VMEM(square, BF16),
            pltpu.VMEM(wide, BF16),
            pltpu.VMEM(wide, BF16),
            pltpu.SemaphoreType.DMA((9,)),
        ],
        HBM,
    )
    maps = exchange(maps, "core")
    (packed,) = call(pair_kernel, (), (maps,), [((MAP_ROWS, C), F32)])
    ring = spread(packed, NZ, "z")
    groups, near = call(
        ring_kernel, (at_x, at_z), (ring,), [((NX, 2 * C, C), F32), ((4 * C, C), F32)]
    )
    groups = exchange(groups.astype(F16), "x").astype(F32)
    (ends,) = call(
        entry_kernel,
        (at_x,),
        (groups, near, maps),
        [((NC, 2 * C, C), F32)],
        [pltpu.VMEM(square, F32), pltpu.VMEM(square, F32)],
    )
    ends = exchange(ends, "core")
    dv, e, f, query_side, key_side, share, own, send, keep = call(
        grad_kernel,
        (at_y,),
        (ends, hidden, keys, queries, cotangent, weights, uhat, what, z0, y, gram, qk, rows),
        [(wide, BF16)]
        + [(square, F32)] * 4
        + [((NX, 4 * PARTS, C), F32), ((8, C), F32), ((40, C), F32), ((4, 8, C), F32)],
        [pltpu.VMEM((8, C), F32), pltpu.VMEM((16, C), F32)],
    )
    got = swap(send, 1)
    share = exchange(share, "x")
    send, keep = call(second_kernel, (at_y,), (got, send, keep), [((40, C), F32), ((4, 8, C), F32)])
    got = swap(send, 4)
    (sums,) = call(sum_kernel, (), (share, own, send), [((4, (PARTS + 1) * C), F32)])
    parts = spread(sums, NX * NZ * NC, CTX)
    dq, dk = call(
        vector_kernel,
        (),
        (keys, queries, e, f, query_side, key_side),
        [(square, BF16), (square, BF16)],
        flops=1 << 28,
    )
    send, keep = call(third_kernel, (at_y,), (got, send, keep), [((48, C), F32), ((4, 8, C), F32)])
    got = swap(send, 2)
    wd_grad, wb_grad, after, rate_grad, bias_grad = call(
        finish_kernel,
        (),
        (parts,),
        [((2, D), F32), ((2, D), F32), ((8, C), F32), ((HEADS,), F32), ((HEADS,), F32)],
        small=2,
    )
    (hidden_grad,) = call(
        hidden_kernel,
        (),
        (got, send, keep, after),
        [(wide, BF16)],
        [pltpu.VMEM((4 * NY, 2 * C), F32)],
        flops=1 << 28,
    )
    return (dq, dk, dv, hidden_grad, wd_grad.T, wb_grad.T, rate_grad, bias_grad)


def solution(mesh):
    fine = Mesh(mesh.devices.reshape(NX, NZ, NC, NY), ("x", "z", "core", "dp"))
    rows, both, cols = P(CTX, None), P(CTX, "dp"), P(None, "dp")
    return jax.shard_map(
        on_device,
        mesh=fine,
        in_specs=(rows, both, both, both, both, cols, cols, P("dp"), P("dp"), P()),
        out_specs=(both, both, both, both, cols, cols, P("dp"), P("dp")),
        check_vma=False,
    )
```

```python
import functools

import jax
import jax.numpy as jnp
from jax import lax
from jax.experimental import pallas as pl
from jax.experimental.pallas import tpu as pltpu
from jax.sharding import Mesh
from jax.sharding import PartitionSpec as P

F32 = jnp.float32
BF16 = jnp.bfloat16
F16 = jnp.float16
C = 128
HEADS = 2
D = 2048
NX, NZ, NC, NY = 4, 8, 2, 8
NQ, NP = 4, 2
PARTS = D // NX // C
CTX = ("x", "zq", "zp", "core")
norm_epsilon = 1e-06
SCALE = C**-0.5
MAP_ROWS = 3 * C


def split(a):
    high = a.astype(BF16)
    return (high, (a - high.astype(F32)).astype(BF16))


def split3(a):
    high = a.astype(BF16)
    rest = a - high.astype(F32)
    middle = rest.astype(BF16)
    return (high, middle, (rest - middle.astype(F32)).astype(BF16))


def dot(a, b, ca, cb):
    return lax.dot_general(a, b, (((ca,), (cb,)), ((), ())), preferred_element_type=F32)


def mm(a, b, ca=1, cb=0):
    if len(a) == len(b) == 2 and (ca, cb) != (0, 1):
        return dot(jnp.concatenate([a[0], a[0], a[1]], axis=ca), jnp.concatenate([b[0], b[1], b[0]], axis=cb), ca, cb)
    total = dot(a[0], b[0], ca, cb)
    for i in range(len(a)):
        for j in range(len(b)):
            if 0 < i + j < max(len(a), len(b)):
                total = total + dot(a[i], b[j], ca, cb)
    return total


def iotas():
    return (
        lax.broadcasted_iota(jnp.int32, (C, C), 0),
        lax.broadcasted_iota(jnp.int32, (C, C), 1),
    )


def pair_column(first, second):
    row = lax.broadcasted_iota(jnp.int32, (HEADS, C), 0)
    return jnp.where(row == 0, first, second)


def unit_rows(source):
    root = lax.rsqrt(jnp.sum(source * source, axis=-1, keepdims=True) + norm_epsilon)
    return source * root, root


def gate_matrices(rows_ref, cols, h, ii, jj, reset):
    keep = jnp.logical_and(ii >= jj, jnp.logical_or(jj >= reset, ii < reset))
    ii_col = ii[:, 0:1]
    c_col, c_row = cols[:, h : h + 1], rows_ref[h : h + 1, :]
    decay = jnp.where(keep, jnp.exp(jnp.where(keep, c_col - c_row, 0.0)), 0.0)
    carry = jnp.where(ii_col < reset, jnp.exp(c_col), 0.0)
    c_last = c_col[C - 1 : C, :]
    late = jnp.logical_or(ii_col >= reset, reset > C - 1)
    weight = jnp.where(late, jnp.exp(jnp.where(late, c_last - c_col, 0.0)), 0.0)
    return keep, decay, carry, weight, cols[:, 2 + h : 3 + h], c_last


def local_kernel(
    at_ref, _x_ref, _y_ref, _q_ref, _p_ref, doc_ref, rate_hbm, bias_hbm, k_hbm, hid_hbm, wd_hbm, wb_hbm, q_hbm, v_hbm, do_hbm,
    map_ref, uhat_ref, what_ref, z0_ref, y_ref, gram_ref, qk_ref, rows_ref, weights_ref,
    rate_ref, bias_ref, k_ref, hid_ref, wd_ref, wb_ref, q_ref, v_ref, do_ref, sems,
):
    pairs = (
        (hid_hbm, hid_ref), (wd_hbm, wd_ref), (wb_hbm, wb_ref), (rate_hbm, rate_ref), (bias_hbm, bias_ref),
        (k_hbm, k_ref), (q_hbm, q_ref), (v_hbm, v_ref), (do_hbm, do_ref),
    )
    copies = [pltpu.make_async_copy(a, b, sems.at[i]) for i, (a, b) in enumerate(pairs)]
    for copy in copies:
        copy.start()
    ii, jj = iotas()
    copies[5].wait()
    copies[6].wait()
    keys, _ = unit_rows(k_ref[...].astype(F32))
    queries, _ = unit_rows(q_ref[...].astype(F32))
    queries = queries * SCALE
    ks, qs = split(keys), split(queries)
    gram = mm(ks, ks, 1, 1)
    qk = mm(qs, ks, 1, 1)
    gram_ref[...] = gram
    qk_ref[...] = qk
    for copy in copies[:5]:
        copy.wait()
    reset = doc_ref[0] - at_ref[0]
    reset = jnp.where(reset < 0, C, jnp.minimum(reset, C))
    zd = dot(wd_ref[...], hid_ref[...], 1, 1)
    zb = dot(wb_ref[...], hid_ref[...], 1, 1)
    x = zd + pair_column(bias_ref[0], bias_ref[1])
    soft = jnp.maximum(x, 0.0) + jnp.log1p(jnp.exp(-jnp.abs(x)))
    slope = -jnp.exp(pair_column(rate_ref[0], rate_ref[1]))
    log_decay = slope * soft
    upper = (ii <= jj).astype(BF16)
    rows_ref[0:2, :] = sum(dot(t, upper, 1, 0) for t in split3(log_decay))
    rows_ref[2:4, :] = jax.nn.sigmoid(zb)
    rows_ref[4:6, :] = log_decay
    rows_ref[6:8, :] = x
    rows_ref[8:10, :] = slope
    rows_ref[10:16, :] = jnp.broadcast_to(reset.astype(F32), (6, C))
    for i, ref in enumerate((wd_ref, wb_ref)):
        weights = ref[...].astype(F32)
        for at in range(2 * NY):
            first = 4 * (at % 2) + 2 * i
            weights_ref[at // 2, first : first + 2, :] = weights[:, at * C : (at + 1) * C]
    cols = rows_ref[0:8, :].T
    copies[7].wait()
    copies[8].wait()
    eye = jnp.where(ii == jj, 1.0, 0.0).astype(F32)
    both_heads = range(HEADS)
    gates = [gate_matrices(rows_ref, cols, h, ii, jj, reset) for h in both_heads]
    inner = [jnp.where(ii > jj, g[1] * gram, 0.0) for g in gates]
    coupling = [g[4] * i for g, i in zip(gates, inner)]
    inverse = [eye - jnp.where((ii & 1) * (ii - jj) == 1, c, 0.0) for c in coupling]
    for level in (1, 3, 5):
        same = (ii >> (level + 2)) == (jj >> (level + 2))
        between = jnp.logical_and(same, (ii >> level) > (jj >> level))
        part = [split(jnp.where(between, c, 0.0)) for c in coupling]
        xs = [split(x) for x in inverse]
        links = [split(mm(xs[h], part[h])) for h in both_heads]
        twice = [split(mm(p, p)) for p in links]
        inverse = [inverse[h] - mm(links[h], xs[h]) for h in both_heads]
        inverse = [inverse[h] + mm(twice[h], split(inverse[h])) for h in both_heads]
    xs = [split(x) for x in inverse]
    cotangent = [(do_ref[:, h * C : (h + 1) * C],) for h in both_heads]
    ps = [split(qk * g[1]) for g in gates]
    both = [
        jnp.concatenate([g[2] * keys, v_ref[:, h * C : (h + 1) * C].astype(F32)], axis=1)
        for h, g in enumerate(gates)
    ]
    right = [split(g[4] * b) for g, b in zip(gates, both)]
    wu = [split(mm(xs[h], right[h])) for h in both_heads]
    pdo = [mm(ps[h], cotangent[h], 0, 0) for h in both_heads]
    keys_out = [g[3] * keys for g in gates]
    ml = [mm(split(keys_out[h]), wu[h], 0, 0) for h in both_heads]
    reach = [mm(ps[h], tuple(t[:, :C] for t in wu[h])) for h in both_heads]
    sides = [split(jnp.concatenate([pdo[h], keys_out[h]], axis=1)) for h in both_heads]
    zy = [mm(xs[h], sides[h], 0, 0) for h in both_heads]
    hats = [both[h] - mm(split(inner[h]), wu[h]) for h in both_heads]
    effective = [split(gates[h][2] * queries - reach[h]) for h in both_heads]
    adjoint = [mm(effective[h], cotangent[h], 0, 0) for h in both_heads]
    for h in both_heads:
        left = jnp.where(reset > C - 1, 1.0 - jnp.exp(gates[h][5]), 1.0)
        map_ref[h, 0:C, :] = ml[h][:, :C] + eye * left
        map_ref[h, C : 2 * C, :] = ml[h][:, C:]
        map_ref[h, 2 * C : 3 * C, :] = adjoint[h]
        what_ref[h], uhat_ref[h] = hats[h][:, :C], hats[h][:, C:]
        z0_ref[h], y_ref[h] = zy[h][:, :C], zy[h][:, C:]


def read_map(ref, *at):
    return tuple(ref[(*at, slice(i * C, (i + 1) * C), slice(None))] for i in range(3))


def scaled(part):
    largest = jnp.max(jnp.max(jnp.abs(part), axis=0, keepdims=True), axis=1, keepdims=True)
    power = jnp.floor(jnp.log2(jnp.maximum(largest, 1e-30)))
    return part * jnp.exp2(13.0 - power), power


def coded(n, powers):
    ii, jj = iotas()
    bits = jnp.zeros((C, C), jnp.int32)
    for at, power in enumerate(powers):
        code = power.astype(jnp.int32) + 256
        bits = jnp.where((jj >> 4) == at, (code >> (jj & 15)) & 1, bits)
    n = n * 8192.0
    return jnp.where(ii == jj, jnp.maximum(n, 2.0**-13) * (1 - 2 * bits).astype(F32), n)


def unpack(ref, at, count):
    ii, jj = iotas()
    n = ref[at, 0:C, :]
    head = jnp.logical_and(ii == jj, n < 0.0)[0:32, :]
    place = jj[0:32, :]
    weight = jnp.where(head, 1 << (place & 15), 0)
    parts = []
    for i in range(count):
        code = jnp.where((place >> 4) == i, weight, 0).astype(F32)
        code = jnp.sum(jnp.sum(code, axis=0, keepdims=True), axis=1, keepdims=True)
        parts.append(ref[at, (i + 1) * C : (i + 2) * C, :] * jnp.exp2(code - (256.0 + 13.0)))
    return jnp.where(ii == jj, jnp.abs(n), n) * (1.0 / 8192.0), *parts


def pair_kernel(maps_ref, out_ref):
    n0, l0, a0 = read_map(maps_ref, 0)
    n1, l1, a1 = read_map(maps_ref, 1)
    n0s = split(n0)
    forward = mm(split(n1), tuple(jnp.concatenate([a, b], axis=1) for a, b in zip(n0s, split(l0))))
    backward = mm(n0s, split(a1), 0, 0)
    out_ref[C : 2 * C, :], state_power = scaled(l0 + l1 - forward[:, C:])
    out_ref[2 * C : 3 * C, :], adjoint_power = scaled(a0 + a1 - backward)
    out_ref[0:C, :] = coded(n0 + n1 - forward[:, :C], (state_power, adjoint_power))


def duo_kernel(maps_ref, out_ref):
    n0, l0, a0 = unpack(maps_ref, 0, 2)
    n1, l1, a1 = unpack(maps_ref, 1, 2)
    n0s = split(n0)
    forward = mm(split(n1), tuple(jnp.concatenate([a, b], axis=1) for a, b in zip(n0s, split(l0))))
    backward = mm(n0s, split(a1), 0, 0)
    out_ref[C : 2 * C, :], state_power = scaled(l0 + l1 - forward[:, C:])
    out_ref[2 * C : 3 * C, :], adjoint_power = scaled(a0 + a1 - backward)
    out_ref[0:C, :] = coded(n0 + n1 - forward[:, :C], (state_power, adjoint_power))


def ring_kernel(at_x_ref, at_ref, maps_ref, out_ref, near_ref):
    here = at_ref[0]
    zero = jnp.zeros((C, C), F32)

    @pl.when(here == 0)
    def _():
        near_ref[0:C, :] = zero
        near_ref[C : 2 * C, :] = zero

    @pl.when(here == NQ - 1)
    def _():
        near_ref[2 * C : 3 * C, :] = zero
        near_ref[3 * C : 4 * C, :] = zero

    maps = [unpack(maps_ref, z, 2) for z in range(NQ)]
    n, state, _ = maps[0]
    n_back, _, adjoint = maps[NQ - 1]
    n_back = n_back.T
    for step in range(1, NQ):
        back = NQ - 1 - step

        @pl.when(here == step)
        def _():
            near_ref[0:C, :] = n
            near_ref[C : 2 * C, :] = state

        @pl.when(here == back)
        def _():
            near_ref[2 * C : 3 * C, :] = n_back
            near_ref[3 * C : 4 * C, :] = adjoint

        nz, lz, _ = maps[step]
        ahead = jnp.concatenate([n, state], axis=1)
        nb, _, az = maps[back]
        nb = nb.T
        behind = jnp.concatenate([n_back, adjoint], axis=1)
        ahead = ahead - mm(split(nz), split(ahead))
        behind = behind - mm(split(nb), split(behind))
        n, state = ahead[:, :C] + nz, ahead[:, C:] + lz
        n_back, adjoint = behind[:, :C] + nb, behind[:, C:] + az
    state, state_power = scaled(state)
    adjoint, adjoint_power = scaled(adjoint)
    onward, backward = coded(n, (state_power,)), coded(n, (adjoint_power,))
    for x in range(NX):

        @pl.when(x > at_x_ref[0])
        def _():
            out_ref[x, 0:C, :] = onward
            out_ref[x, C : 2 * C, :] = state

        @pl.when(x <= at_x_ref[0])
        def _():
            out_ref[x, 0:C, :] = backward
            out_ref[x, C : 2 * C, :] = adjoint


def entry_kernel(at_ref, at_pair_ref, groups_ref, near_ref, chips_ref, maps_ref, out_ref, s_ref, a_ref):
    here = at_ref[0]
    s_ref[...] = jnp.where(here > 0, unpack(groups_ref, 0, 1)[1], 0.0)
    a_ref[...] = jnp.where(here < NX - 1, unpack(groups_ref, NX - 1, 1)[1], 0.0)
    for step in range(1, NX - 1):
        back = NX - 1 - step

        @pl.when(here > step)
        def _():
            n, state = unpack(groups_ref, step, 1)
            s = s_ref[...]
            s_ref[...] = s - mm(split(n), split(s)) + state

        @pl.when(here < back)
        def _():
            n, adjoint = unpack(groups_ref, back, 1)
            a = a_ref[...]
            a_ref[...] = a - mm(split(n), split(a), 0, 0) + adjoint

    s, a = s_ref[...], a_ref[...]
    s = s - mm(split(near_ref[0:C, :]), split(s)) + near_ref[C : 2 * C, :]
    a = a - mm(split(near_ref[2 * C : 3 * C, :]), split(a)) + near_ref[3 * C : 4 * C, :]
    n, state, _ = unpack(chips_ref, 0, 2)
    second = s - mm(split(n), split(s)) + state
    n, _, adjoint = unpack(chips_ref, 1, 2)
    first = a - mm(split(n), split(a), 0, 0) + adjoint
    s = jnp.where(at_pair_ref[0] == 0, s, second)
    a = jnp.where(at_pair_ref[0] == 0, first, a)
    out_ref[0, 0:C, :] = s
    out_ref[1, C : 2 * C, :] = a
    n, state, _ = read_map(maps_ref, 0)
    out_ref[1, 0:C, :] = s - mm(split(n), split(s)) + state
    n, _, adjoint = read_map(maps_ref, 1)
    out_ref[0, C : 2 * C, :] = a - mm(split(n), split(a), 0, 0) + adjoint


def grad_kernel(
    at_y_ref,
    ends_ref, hid_ref, k_ref, q_ref, do_ref, weights_ref,
    uhat_ref, what_ref, z0_ref, y_ref, gram_ref, qk_ref, rows_ref,
    dv_ref, e_ref, f_ref, query_side_ref, key_side_ref, share_ref, own_ref, send_ref, keep_ref,
    sums_ref, terms_ref,
):
    mine = at_y_ref[0]
    ii, jj = iotas()
    reset = rows_ref[10:11, 0:1].astype(jnp.int32)
    cols = rows_ref[0:8, :].T
    keys, _ = unit_rows(k_ref[...].astype(F32))
    queries = unit_rows(q_ref[...].astype(F32))[0] * SCALE
    gram, qk = gram_ref[...], qk_ref[...]
    lower = (ii >= jj).astype(BF16)
    both_heads = range(HEADS)
    gates = [gate_matrices(rows_ref, cols, h, ii, jj, reset) for h in both_heads]
    states = [ends_ref[h, 0:C, :] for h in both_heads]
    adjoints = [ends_ref[h, C : 2 * C, :] for h in both_heads]
    ss, as_ = [split(s) for s in states], [split(a) for a in adjoints]
    cotangent = [(do_ref[:, h * C : (h + 1) * C],) for h in both_heads]
    uhat = [uhat_ref[h] - mm(split(what_ref[h]), ss[h]) for h in both_heads]
    z = [z0_ref[h] + mm(split(y_ref[h]), as_[h]) for h in both_heads]
    from_out = [gates[h][2] * mm(cotangent[h], ss[h], 1, 1) for h in both_heads]
    bz = [gates[h][4] * z[h] for h in both_heads]
    us = [split(gates[h][4] * uhat[h]) for h in both_heads]
    zs, bzs = [split(a) for a in z], [split(a) for a in bz]
    from_keys = [gates[h][3] * mm(us[h], as_[h], 1, 1) for h in both_heads]
    through = [mm(bzs[h], ss[h], 1, 1) for h in both_heads]
    e = [mm(cotangent[h], us[h], 1, 1) for h in both_heads]
    f = [mm(zs[h], us[h], 1, 1) for h in both_heads]
    e = [jnp.where(gates[h][0], e[h] * gates[h][1], 0.0) for h in both_heads]
    f = [jnp.where(ii > jj, f[h] * gates[h][1] * -gates[h][4], 0.0) for h in both_heads]
    key_side = [from_keys[h] - gates[h][2] * through[h] for h in both_heads]
    h_mat = [e[h] * qk + f[h] * gram for h in both_heads]
    by_row = [
        h_mat[h] + queries * from_out[h] + keys * (key_side[h] - 2.0 * from_keys[h])
        for h in both_heads
    ]
    zu = [z[h] * uhat[h] for h in both_heads]
    by_lane = jnp.zeros((C, C), F32)
    for i, t in enumerate((*by_row, *zu)):
        by_lane = jnp.where(jj == i, jnp.sum(t, axis=1, keepdims=True), by_lane)
    by_lane = by_lane.T
    dc, db = by_lane[0:2, :], by_lane[2:4, :]
    for h in both_heads:
        carry = gates[h][2]
        ends = keys * from_keys[h] + carry[C - 1 : C, :] * states[h] * adjoints[h]
        tail = jnp.sum(jnp.sum(ends, axis=0, keepdims=True), axis=1, keepdims=True)
        sums_ref[h : h + 1, :] = dc[h : h + 1, :] - jnp.sum(h_mat[h], axis=0, keepdims=True)
        sums_ref[2 + h : 3 + h, :] = db[h : h + 1, :]
        sums_ref[4 + h : 5 + h, :] = jnp.broadcast_to(tail, (1, C))
        dv_ref[:, h * C : (h + 1) * C] = bz[h].astype(BF16)
    e_ref[...] = e[0] + e[1]
    f_ref[...] = f[0] + f[1]
    query_side_ref[...] = from_out[0] + from_out[1]
    key_side_ref[...] = key_side[0] + key_side[1]
    dc, db, tail = sums_ref[0:2, :], sums_ref[2:4, :], sums_ref[4:6, :]
    dg = sum(dot(t, lower, 1, 0) for t in split3(dc)) + tail
    beta, log_decay = rows_ref[2:4, :], rows_ref[4:6, :]
    dz = dg * rows_ref[8:10, :] * jax.nn.sigmoid(rows_ref[6:8, :])
    own_ref[0:2, :] = dz
    own_ref[2:4, :] = db * beta * (1.0 - beta)
    own_ref[4:6, :] = jnp.broadcast_to(jnp.sum(dg * log_decay, axis=1, keepdims=True), (2, C))
    own_ref[6:8, :] = jnp.broadcast_to(jnp.sum(dz, axis=1, keepdims=True), (2, C))
    for i, t in enumerate(split3(own_ref[0:4, :])):
        terms_ref[4 * i : 4 * i + 4, :] = t.astype(F32)
    terms_ref[12:16, :] = jnp.zeros((4, C), F32)
    grad = dot(terms_ref[...].astype(BF16), hid_ref[...], 1, 0)
    grad = grad[0:4, :] + grad[4:8, :] + grad[8:12, :]
    for x in range(NX):
        for i in range(PARTS):
            at = slice((PARTS * x + i) * C, (PARTS * x + i + 1) * C)
            share_ref[x, 4 * i : 4 * i + 4, :] = grad[:, at]
    send_ref[0:4, :] = own_ref[0:4, :]
    send_ref[4:8, :] = own_ref[0:4, :]
    bit = mine & 1
    for at in range(4):
        pair = weights_ref[2 * at], weights_ref[2 * at + 1]
        keep_ref[at] = jnp.where(bit == 0, pair[0], pair[1])
        send_ref[8 + 8 * at : 16 + 8 * at, :] = jnp.where(bit == 0, pair[1], pair[0])


def second_kernel(at_y_ref, got_ref, sent_ref, keep_ref, send_ref, kept_ref):
    bit = (at_y_ref[0] >> 2) & 1
    send_ref[0:4, :] = sent_ref[0:4, :]
    send_ref[4:8, :] = got_ref[0:4, :]
    for high in range(2):
        for low in range(2):
            place = 2 * high + low
            pair = (keep_ref[place], got_ref[8 + 8 * place : 16 + 8 * place, :])
            for source, rows in enumerate(pair):

                at = 2 * source + low

                @pl.when(bit == high)
                def _():
                    kept_ref[at] = rows

                @pl.when(bit != high)
                def _():
                    send_ref[8 + 8 * at : 16 + 8 * at, :] = rows


def third_kernel(at_y_ref, got_ref, sent_ref, keep_ref, send_ref, kept_ref):
    bit = (at_y_ref[0] >> 1) & 1
    send_ref[0:8, :] = sent_ref[0:8, :]
    send_ref[8:16, :] = got_ref[0:8, :]
    for source in range(4):
        for low in range(2):
            at = 2 * (source % 2) + low
            rows = keep_ref[at] if source < 2 else got_ref[8 + 8 * at : 16 + 8 * at, :]

            @pl.when(bit == low)
            def _():
                kept_ref[source] = rows

            @pl.when(bit != low)
            def _():
                send_ref[16 + 8 * source : 24 + 8 * source, :] = rows


def hidden_kernel(got_ref, sent_ref, keep_ref, _after_ref, hidden_ref, w_ref):
    for source in range(NY):
        for half in range(2):
            lanes, at = slice(half * C, (half + 1) * C), slice(4 * half, 4 * half + 4)
            if source < 4:
                rows = keep_ref[source, at, :]
            else:
                rows = got_ref[16 + 8 * (source - 4) + 4 * half : 20 + 8 * (source - 4) + 4 * half, :]
            w_ref[4 * source : 4 * source + 4, lanes] = rows
    logit_rows = jnp.concatenate([sent_ref[0:16, :], got_ref[0:16, :]], axis=0)
    weights = w_ref[...].astype(BF16)
    hidden = sum(dot(t, weights, 0, 0) for t in split3(logit_rows))
    hidden_ref[...] = hidden.astype(BF16)


def vector_kernel(k_ref, q_ref, e_ref, f_ref, query_side_ref, key_side_ref, dq_ref, dk_ref):
    keys, key_root = unit_rows(k_ref[...].astype(F32))
    unit_queries, query_root = unit_rows(q_ref[...].astype(F32))
    ks, qs = split(keys), split(unit_queries * SCALE)
    es, f = split(e_ref[...]), f_ref[...]
    dq = query_side_ref[...] + mm(es, ks)
    dk = key_side_ref[...] + mm(es, qs, 0, 0) + mm(split(f + f.T), ks)
    dq = dq - unit_queries * jnp.sum(unit_queries * dq, axis=-1, keepdims=True)
    dk = dk - keys * jnp.sum(keys * dk, axis=-1, keepdims=True)
    dq_ref[...] = (dq * (query_root * SCALE)).astype(BF16)
    dk_ref[...] = (dk * key_root).astype(BF16)


def sum_kernel(share_ref, own_ref, _send_ref, out_ref):
    total = share_ref[0]
    for x in range(1, NX):
        total = total + share_ref[x]
    total, power = scaled(total)
    lane = lax.broadcasted_iota(jnp.int32, (1, C), 1) >> 5
    sums = own_ref[4:5, :]
    for i in range(1, 4):
        sums = jnp.where(lane == i, own_ref[4 + i : 5 + i, :], sums)
    powers = jnp.floor(jnp.log2(jnp.maximum(jnp.abs(sums), 1e-30)))
    fractions = sums * jnp.exp2(-powers)
    high = jnp.floor(fractions * 256.0) * (1.0 / 256.0)
    for i in range(PARTS):
        out_ref[:, i * C : (i + 1) * C] = total[4 * i : 4 * i + 4, :]
    out_ref[0:1, PARTS * C :] = jnp.broadcast_to(power, (1, C))
    out_ref[1:2, PARTS * C :] = powers
    out_ref[2:3, PARTS * C :] = high
    out_ref[3:4, PARTS * C :] = (fractions - high) * 256.0


def finish_kernel(parts_ref, wd_ref, wb_ref, after_ref, rate_ref, bias_ref):
    after_ref[...] = jnp.zeros_like(after_ref)
    per = NZ * NC
    sums = jnp.zeros((1, C), F32)
    for x in range(NX):
        totals = [jnp.zeros((4, C), F32)] * PARTS
        for at in range(x * per, (x + 1) * per):
            meta = parts_ref[at, :, PARTS * C :]
            scale = jnp.exp2(meta[0:1, :] - 13.0)
            totals = [t + parts_ref[at, :, i * C : (i + 1) * C] * scale for i, t in enumerate(totals)]
            sums = sums + (meta[2:3, :] + meta[3:4, :] * (1.0 / 256.0)) * jnp.exp2(meta[1:2, :])
        for i, total in enumerate(totals):
            at = slice((PARTS * x + i) * C, (PARTS * x + i + 1) * C)
            wd_ref[:, at] = total[0:2, :]
            wb_ref[:, at] = total[2:4, :]
    lane = lax.broadcasted_iota(jnp.int32, (1, C), 1)
    for i in range(2):
        rate_ref[i] = jnp.sum(jnp.where(lane == 32 * i, sums, 0.0))
        bias_ref[i] = jnp.sum(jnp.where(lane == 64 + 32 * i, sums, 0.0))


VMEM = pl.BlockSpec(memory_space=pltpu.VMEM)
SMEM = pl.BlockSpec(memory_space=pltpu.SMEM)
HBM = pl.BlockSpec(memory_space=pltpu.HBM)


def call(kernel, scalars, arrays, outs, scratch=(), space=VMEM, small=0, flops=0):
    if space is HBM:
        arrays = tuple(pltpu.with_memory_space_constraint(a, pltpu.HBM) for a in arrays)
    return pl.pallas_call(
        kernel,
        out_shape=tuple(jax.ShapeDtypeStruct(s, t) for s, t in outs),
        in_specs=[SMEM] * len(scalars) + [space] * len(arrays),
        out_specs=tuple([VMEM] * (len(outs) - small) + [SMEM] * small),
        scratch_shapes=list(scratch),
        compiler_params=pltpu.CompilerParams(vmem_limit_bytes=40 << 20),
        cost_estimate=pl.CostEstimate(flops=flops, bytes_accessed=1 << 20, transcendentals=0) if flops else None,
    )(*scalars, *arrays)


def exchange(a, axes):
    return lax.all_to_all(a, axes, 0, 0, tiled=True)


def spread(a, count, axes):
    a = jnp.broadcast_to(a.astype(F16), (count, *a.shape))
    return exchange(a, axes).astype(F32)


def swap(a, bit):
    return lax.ppermute(a, "dp", [(i, i ^ bit) for i in range(NY)])


def on_device(hidden, queries, keys, values, cotangent, w_decay, w_beta, rate, bias, doc_start):
    at_x = lax.axis_index("x").astype(jnp.int32)
    at_q = lax.axis_index("zq").astype(jnp.int32)
    at_p = lax.axis_index("zp").astype(jnp.int32)
    at_core = lax.axis_index("core").astype(jnp.int32)
    at_y = lax.axis_index("dp").astype(jnp.int32)
    first = (((at_x * NQ + at_q) * NP + at_p) * NC + at_core) * C
    at_x, at_y, at_q, at_p, first = (a[None] for a in (at_x, at_y, at_q, at_p, first))
    wd, wb = w_decay.T, w_beta.T
    square, heads, wide = (C, C), (HEADS, C, C), (C, HEADS * C)
    maps, uhat, what, z0, y, gram, qk, rows, weights = call(
        local_kernel,
        (first, at_x, at_y, at_q, at_p, doc_start),
        (rate, bias, keys, hidden, wd, wb, queries, values, cotangent),
        [((HEADS, MAP_ROWS, C), F32)] + [(heads, F32)] * 4 + [(square, F32)] * 2 + [((16, C), F32), ((NY, 8, C), F32)],
        [
            pltpu.SMEM((2,), F32),
            pltpu.SMEM((2,), F32),
            pltpu.VMEM(square, BF16),
            pltpu.VMEM((C, D), BF16),
            pltpu.VMEM((2, D), BF16),
            pltpu.VMEM((2, D), BF16),
            pltpu.VMEM(square, BF16),
            pltpu.VMEM(wide, BF16),
            pltpu.VMEM(wide, BF16),
            pltpu.SemaphoreType.DMA((9,)),
        ],
        HBM,
    )
    maps = exchange(maps, "core")
    (packed,) = call(pair_kernel, (), (maps,), [((MAP_ROWS, C), F32)])
    chips = spread(packed, NP, "zp")
    (packed,) = call(duo_kernel, (), (chips,), [((MAP_ROWS, C), F32)])
    ring = spread(packed, NQ, "zq")
    groups, near = call(
        ring_kernel, (at_x, at_q), (ring,), [((NX, 2 * C, C), F32), ((4 * C, C), F32)]
    )
    groups = exchange(groups.astype(F16), "x").astype(F32)
    (ends,) = call(
        entry_kernel,
        (at_x, at_p),
        (groups, near, chips, maps),
        [((NC, 2 * C, C), F32)],
        [pltpu.VMEM(square, F32), pltpu.VMEM(square, F32)],
    )
    ends = exchange(ends, "core")
    dv, e, f, query_side, key_side, share, own, send, keep = call(
        grad_kernel,
        (at_y,),
        (ends, hidden, keys, queries, cotangent, weights, uhat, what, z0, y, gram, qk, rows),
        [(wide, BF16)]
        + [(square, F32)] * 4
        + [((NX, 4 * PARTS, C), F32), ((8, C), F32), ((40, C), F32), ((4, 8, C), F32)],
        [pltpu.VMEM((8, C), F32), pltpu.VMEM((16, C), F32)],
    )
    got = swap(send, 1)
    share = exchange(share, "x")
    send, keep = call(second_kernel, (at_y,), (got, send, keep), [((40, C), F32), ((4, 8, C), F32)])
    got = swap(send, 4)
    (sums,) = call(sum_kernel, (), (share, own, send), [((4, (PARTS + 1) * C), F32)])
    parts = spread(sums, NX * NZ * NC, CTX)
    dq, dk = call(
        vector_kernel,
        (),
        (keys, queries, e, f, query_side, key_side),
        [(square, BF16), (square, BF16)],
        flops=1 << 28,
    )
    send, keep = call(third_kernel, (at_y,), (got, send, keep), [((48, C), F32), ((4, 8, C), F32)])
    got = swap(send, 2)
    wd_grad, wb_grad, after, rate_grad, bias_grad = call(
        finish_kernel,
        (),
        (parts,),
        [((2, D), F32), ((2, D), F32), ((8, C), F32), ((HEADS,), F32), ((HEADS,), F32)],
        small=2,
    )
    (hidden_grad,) = call(
        hidden_kernel,
        (),
        (got, send, keep, after),
        [(wide, BF16)],
        [pltpu.VMEM((4 * NY, 2 * C), F32)],
        flops=1 << 28,
    )
    return (dq, dk, dv, hidden_grad, wd_grad.T, wb_grad.T, rate_grad, bias_grad)


def solution(mesh):
    fine = Mesh(mesh.devices.reshape(NX, NQ, NP, NC, NY), (*CTX, "dp"))
    rows, both, cols = P(CTX, None), P(CTX, "dp"), P(None, "dp")
    return jax.shard_map(
        on_device,
        mesh=fine,
        in_specs=(rows, both, both, both, both, cols, cols, P("dp"), P("dp"), P()),
        out_specs=(both, both, both, both, cols, cols, P("dp"), P("dp")),
        check_vma=False,
    )
```

```python
import functools

import jax
import jax.numpy as jnp
from jax import lax
from jax.experimental import pallas as pl
from jax.experimental.pallas import tpu as pltpu
from jax.sharding import Mesh
from jax.sharding import PartitionSpec as P

F32 = jnp.float32
BF16 = jnp.bfloat16
F16 = jnp.float16
C = 128
HEADS = 2
D = 2048
NX, NZ, NC, NY = 4, 8, 2, 8
NQ, NP = 4, 2
PARTS = D // (NX * NC) // C
CTX = ("x", "zq", "zp", "core")
norm_epsilon = 1e-06
SCALE = C**-0.5
MAP_ROWS = 3 * C


def split(a):
    high = a.astype(BF16)
    return (high, (a - high.astype(F32)).astype(BF16))


def split3(a):
    high = a.astype(BF16)
    rest = a - high.astype(F32)
    middle = rest.astype(BF16)
    return (high, middle, (rest - middle.astype(F32)).astype(BF16))


def dot(a, b, ca, cb):
    return lax.dot_general(a, b, (((ca,), (cb,)), ((), ())), preferred_element_type=F32)


def mm(a, b, ca=1, cb=0):
    if len(a) == len(b) == 2 and (ca, cb) != (0, 1):
        return dot(jnp.concatenate([a[0], a[0], a[1]], axis=ca), jnp.concatenate([b[0], b[1], b[0]], axis=cb), ca, cb)
    total = dot(a[0], b[0], ca, cb)
    for i in range(len(a)):
        for j in range(len(b)):
            if 0 < i + j < max(len(a), len(b)):
                total = total + dot(a[i], b[j], ca, cb)
    return total


def iotas():
    return (
        lax.broadcasted_iota(jnp.int32, (C, C), 0),
        lax.broadcasted_iota(jnp.int32, (C, C), 1),
    )


def pair_column(first, second):
    row = lax.broadcasted_iota(jnp.int32, (HEADS, C), 0)
    return jnp.where(row == 0, first, second)


def unit_rows(source):
    root = lax.rsqrt(jnp.sum(source * source, axis=-1, keepdims=True) + norm_epsilon)
    return source * root, root


def gate_matrices(rows_ref, cols, h, ii, jj, reset):
    keep = jnp.logical_and(ii >= jj, jnp.logical_or(jj >= reset, ii < reset))
    ii_col = ii[:, 0:1]
    c_col, c_row = cols[:, h : h + 1], rows_ref[h : h + 1, :]
    decay = jnp.where(keep, jnp.exp(jnp.where(keep, c_col - c_row, 0.0)), 0.0)
    carry = jnp.where(ii_col < reset, jnp.exp(c_col), 0.0)
    c_last = c_col[C - 1 : C, :]
    late = jnp.logical_or(ii_col >= reset, reset > C - 1)
    weight = jnp.where(late, jnp.exp(jnp.where(late, c_last - c_col, 0.0)), 0.0)
    return keep, decay, carry, weight, cols[:, 2 + h : 3 + h], c_last


def local_kernel(
    at_ref, _x_ref, _y_ref, _q_ref, _p_ref, doc_ref, rate_hbm, bias_hbm, k_hbm, hid_hbm, wd_hbm, wb_hbm, q_hbm, v_hbm, do_hbm,
    map_ref, uhat_ref, what_ref, z0_ref, y_ref, gram_ref, qk_ref, rows_ref, weights_ref,
    rate_ref, bias_ref, k_ref, hid_ref, wd_ref, wb_ref, q_ref, v_ref, do_ref, sems,
):
    pairs = (
        (hid_hbm, hid_ref), (wd_hbm, wd_ref), (wb_hbm, wb_ref), (rate_hbm, rate_ref), (bias_hbm, bias_ref),
        (k_hbm, k_ref), (q_hbm, q_ref), (v_hbm, v_ref), (do_hbm, do_ref),
    )
    copies = [pltpu.make_async_copy(a, b, sems.at[i]) for i, (a, b) in enumerate(pairs)]
    for copy in copies:
        copy.start()
    ii, jj = iotas()
    copies[5].wait()
    copies[6].wait()
    keys, _ = unit_rows(k_ref[...].astype(F32))
    queries, _ = unit_rows(q_ref[...].astype(F32))
    queries = queries * SCALE
    ks, qs = split(keys), split(queries)
    gram = mm(ks, ks, 1, 1)
    qk = mm(qs, ks, 1, 1)
    gram_ref[...] = gram
    qk_ref[...] = qk
    for copy in copies[:5]:
        copy.wait()
    reset = doc_ref[0] - at_ref[0]
    reset = jnp.where(reset < 0, C, jnp.minimum(reset, C))
    zd = dot(wd_ref[...], hid_ref[...], 1, 1)
    zb = dot(wb_ref[...], hid_ref[...], 1, 1)
    x = zd + pair_column(bias_ref[0], bias_ref[1])
    soft = jnp.maximum(x, 0.0) + jnp.log1p(jnp.exp(-jnp.abs(x)))
    slope = -jnp.exp(pair_column(rate_ref[0], rate_ref[1]))
    log_decay = slope * soft
    upper = (ii <= jj).astype(BF16)
    rows_ref[0:2, :] = sum(dot(t, upper, 1, 0) for t in split3(log_decay))
    rows_ref[2:4, :] = jax.nn.sigmoid(zb)
    rows_ref[4:6, :] = log_decay
    rows_ref[6:8, :] = x
    rows_ref[8:10, :] = slope
    rows_ref[10:16, :] = jnp.broadcast_to(reset.astype(F32), (6, C))
    for i, ref in enumerate((wd_ref, wb_ref)):
        weights = ref[...].astype(F32)
        for at in range(2 * NY):
            first = 4 * (at % 2) + 2 * i
            weights_ref[at // 2, first : first + 2, :] = weights[:, at * C : (at + 1) * C]
    cols = rows_ref[0:8, :].T
    copies[7].wait()
    copies[8].wait()
    eye = jnp.where(ii == jj, 1.0, 0.0).astype(F32)
    both_heads = range(HEADS)
    gates = [gate_matrices(rows_ref, cols, h, ii, jj, reset) for h in both_heads]
    inner = [jnp.where(ii > jj, g[1] * gram, 0.0) for g in gates]
    coupling = [g[4] * i for g, i in zip(gates, inner)]
    inverse = [eye - jnp.where((ii & 1) * (ii - jj) == 1, c, 0.0) for c in coupling]
    for level in (1, 3, 5):
        same = (ii >> (level + 2)) == (jj >> (level + 2))
        between = jnp.logical_and(same, (ii >> level) > (jj >> level))
        part = [split(jnp.where(between, c, 0.0)) for c in coupling]
        xs = [split(x) for x in inverse]
        links = [split(mm(xs[h], part[h])) for h in both_heads]
        twice = [split(mm(p, p)) for p in links]
        inverse = [inverse[h] - mm(links[h], xs[h]) for h in both_heads]
        inverse = [inverse[h] + mm(twice[h], split(inverse[h])) for h in both_heads]
    xs = [split(x) for x in inverse]
    cotangent = [(do_ref[:, h * C : (h + 1) * C],) for h in both_heads]
    ps = [split(qk * g[1]) for g in gates]
    both = [
        jnp.concatenate([g[2] * keys, v_ref[:, h * C : (h + 1) * C].astype(F32)], axis=1)
        for h, g in enumerate(gates)
    ]
    right = [split(g[4] * b) for g, b in zip(gates, both)]
    wu = [split(mm(xs[h], right[h])) for h in both_heads]
    pdo = [mm(ps[h], cotangent[h], 0, 0) for h in both_heads]
    keys_out = [g[3] * keys for g in gates]
    ml = [mm(split(keys_out[h]), wu[h], 0, 0) for h in both_heads]
    reach = [mm(ps[h], tuple(t[:, :C] for t in wu[h])) for h in both_heads]
    sides = [split(jnp.concatenate([pdo[h], keys_out[h]], axis=1)) for h in both_heads]
    zy = [mm(xs[h], sides[h], 0, 0) for h in both_heads]
    hats = [both[h] - mm(split(inner[h]), wu[h]) for h in both_heads]
    effective = [split(gates[h][2] * queries - reach[h]) for h in both_heads]
    adjoint = [mm(effective[h], cotangent[h], 0, 0) for h in both_heads]
    for h in both_heads:
        left = jnp.where(reset > C - 1, 1.0 - jnp.exp(gates[h][5]), 1.0)
        map_ref[h, 0:C, :] = ml[h][:, :C] + eye * left
        map_ref[h, C : 2 * C, :] = ml[h][:, C:]
        map_ref[h, 2 * C : 3 * C, :] = adjoint[h]
        what_ref[h], uhat_ref[h] = hats[h][:, :C], hats[h][:, C:]
        z0_ref[h], y_ref[h] = zy[h][:, :C], zy[h][:, C:]


def read_map(ref, *at):
    return tuple(ref[(*at, slice(i * C, (i + 1) * C), slice(None))] for i in range(3))


def scaled(part):
    largest = jnp.max(jnp.max(jnp.abs(part), axis=0, keepdims=True), axis=1, keepdims=True)
    power = jnp.floor(jnp.log2(jnp.maximum(largest, 1e-30)))
    return part * jnp.exp2(13.0 - power), power


def coded(n, powers):
    ii, jj = iotas()
    bits = jnp.zeros((C, C), jnp.int32)
    for at, power in enumerate(powers):
        code = power.astype(jnp.int32) + 256
        bits = jnp.where((jj >> 4) == at, (code >> (jj & 15)) & 1, bits)
    n = n * 8192.0
    return jnp.where(ii == jj, jnp.maximum(n, 2.0**-13) * (1 - 2 * bits).astype(F32), n)


def unpack(ref, at, count):
    ii, jj = iotas()
    n = ref[at, 0:C, :]
    head = jnp.logical_and(ii == jj, n < 0.0)[0:32, :]
    place = jj[0:32, :]
    weight = jnp.where(head, 1 << (place & 15), 0)
    parts = []
    for i in range(count):
        code = jnp.where((place >> 4) == i, weight, 0).astype(F32)
        code = jnp.sum(jnp.sum(code, axis=0, keepdims=True), axis=1, keepdims=True)
        parts.append(ref[at, (i + 1) * C : (i + 2) * C, :] * jnp.exp2(code - (256.0 + 13.0)))
    return jnp.where(ii == jj, jnp.abs(n), n) * (1.0 / 8192.0), *parts


def pair_kernel(maps_ref, out_ref):
    n0, l0, a0 = read_map(maps_ref, 0)
    n1, l1, a1 = read_map(maps_ref, 1)
    n0s = split(n0)
    forward = mm(split(n1), tuple(jnp.concatenate([a, b], axis=1) for a, b in zip(n0s, split(l0))))
    backward = mm(n0s, split(a1), 0, 0)
    out_ref[C : 2 * C, :], state_power = scaled(l0 + l1 - forward[:, C:])
    out_ref[2 * C : 3 * C, :], adjoint_power = scaled(a0 + a1 - backward)
    out_ref[0:C, :] = coded(n0 + n1 - forward[:, :C], (state_power, adjoint_power))


def duo_kernel(maps_ref, out_ref):
    n0, l0, a0 = unpack(maps_ref, 0, 2)
    n1, l1, a1 = unpack(maps_ref, 1, 2)
    n0s = split(n0)
    forward = mm(split(n1), tuple(jnp.concatenate([a, b], axis=1) for a, b in zip(n0s, split(l0))))
    backward = mm(n0s, split(a1), 0, 0)
    out_ref[C : 2 * C, :], state_power = scaled(l0 + l1 - forward[:, C:])
    out_ref[2 * C : 3 * C, :], adjoint_power = scaled(a0 + a1 - backward)
    out_ref[0:C, :] = coded(n0 + n1 - forward[:, :C], (state_power, adjoint_power))


def ring_kernel(at_x_ref, at_ref, maps_ref, out_ref, near_ref):
    here = at_ref[0]
    zero = jnp.zeros((C, C), F32)

    @pl.when(here == 0)
    def _():
        near_ref[0:C, :] = zero
        near_ref[C : 2 * C, :] = zero

    @pl.when(here == NQ - 1)
    def _():
        near_ref[2 * C : 3 * C, :] = zero
        near_ref[3 * C : 4 * C, :] = zero

    maps = [unpack(maps_ref, z, 2) for z in range(NQ)]
    n, state, _ = maps[0]
    n_back, _, adjoint = maps[NQ - 1]
    n_back = n_back.T
    for step in range(1, NQ):
        back = NQ - 1 - step

        @pl.when(here == step)
        def _():
            near_ref[0:C, :] = n
            near_ref[C : 2 * C, :] = state

        @pl.when(here == back)
        def _():
            near_ref[2 * C : 3 * C, :] = n_back
            near_ref[3 * C : 4 * C, :] = adjoint

        nz, lz, _ = maps[step]
        ahead = jnp.concatenate([n, state], axis=1)
        nb, _, az = maps[back]
        nb = nb.T
        behind = jnp.concatenate([n_back, adjoint], axis=1)
        ahead = ahead - mm(split(nz), split(ahead))
        behind = behind - mm(split(nb), split(behind))
        n, state = ahead[:, :C] + nz, ahead[:, C:] + lz
        n_back, adjoint = behind[:, :C] + nb, behind[:, C:] + az
    state, state_power = scaled(state)
    adjoint, adjoint_power = scaled(adjoint)
    onward, backward = coded(n, (state_power,)), coded(n, (adjoint_power,))
    for x in range(NX):

        @pl.when(x > at_x_ref[0])
        def _():
            out_ref[x, 0:C, :] = onward
            out_ref[x, C : 2 * C, :] = state

        @pl.when(x <= at_x_ref[0])
        def _():
            out_ref[x, 0:C, :] = backward
            out_ref[x, C : 2 * C, :] = adjoint


def entry_kernel(at_ref, at_pair_ref, groups_ref, near_ref, chips_ref, maps_ref, out_ref, s_ref, a_ref):
    here = at_ref[0]
    s_ref[...] = jnp.where(here > 0, unpack(groups_ref, 0, 1)[1], 0.0)
    a_ref[...] = jnp.where(here < NX - 1, unpack(groups_ref, NX - 1, 1)[1], 0.0)
    for step in range(1, NX - 1):
        back = NX - 1 - step

        @pl.when(here > step)
        def _():
            n, state = unpack(groups_ref, step, 1)
            s = s_ref[...]
            s_ref[...] = s - mm(split(n), split(s)) + state

        @pl.when(here < back)
        def _():
            n, adjoint = unpack(groups_ref, back, 1)
            a = a_ref[...]
            a_ref[...] = a - mm(split(n), split(a), 0, 0) + adjoint

    s, a = s_ref[...], a_ref[...]
    s = s - mm(split(near_ref[0:C, :]), split(s)) + near_ref[C : 2 * C, :]
    a = a - mm(split(near_ref[2 * C : 3 * C, :]), split(a)) + near_ref[3 * C : 4 * C, :]
    n, state, _ = unpack(chips_ref, 0, 2)
    second = s - mm(split(n), split(s)) + state
    n, _, adjoint = unpack(chips_ref, 1, 2)
    first = a - mm(split(n), split(a), 0, 0) + adjoint
    s = jnp.where(at_pair_ref[0] == 0, s, second)
    a = jnp.where(at_pair_ref[0] == 0, first, a)
    out_ref[0, 0:C, :] = s
    out_ref[1, C : 2 * C, :] = a
    n, state, _ = read_map(maps_ref, 0)
    out_ref[1, 0:C, :] = s - mm(split(n), split(s)) + state
    n, _, adjoint = read_map(maps_ref, 1)
    out_ref[0, C : 2 * C, :] = a - mm(split(n), split(a), 0, 0) + adjoint


def grad_kernel(
    at_y_ref,
    ends_ref, hid_ref, k_ref, q_ref, do_ref, weights_ref,
    uhat_ref, what_ref, z0_ref, y_ref, gram_ref, qk_ref, rows_ref,
    dv_ref, e_ref, f_ref, query_side_ref, key_side_ref, share_ref, own_ref, send_ref, keep_ref,
    sums_ref, terms_ref,
):
    mine = at_y_ref[0]
    ii, jj = iotas()
    reset = rows_ref[10:11, 0:1].astype(jnp.int32)
    cols = rows_ref[0:8, :].T
    keys, _ = unit_rows(k_ref[...].astype(F32))
    queries = unit_rows(q_ref[...].astype(F32))[0] * SCALE
    gram, qk = gram_ref[...], qk_ref[...]
    lower = (ii >= jj).astype(BF16)
    both_heads = range(HEADS)
    gates = [gate_matrices(rows_ref, cols, h, ii, jj, reset) for h in both_heads]
    states = [ends_ref[h, 0:C, :] for h in both_heads]
    adjoints = [ends_ref[h, C : 2 * C, :] for h in both_heads]
    ss, as_ = [split(s) for s in states], [split(a) for a in adjoints]
    cotangent = [(do_ref[:, h * C : (h + 1) * C],) for h in both_heads]
    uhat = [uhat_ref[h] - mm(split(what_ref[h]), ss[h]) for h in both_heads]
    z = [z0_ref[h] + mm(split(y_ref[h]), as_[h]) for h in both_heads]
    from_out = [gates[h][2] * mm(cotangent[h], ss[h], 1, 1) for h in both_heads]
    bz = [gates[h][4] * z[h] for h in both_heads]
    us = [split(gates[h][4] * uhat[h]) for h in both_heads]
    zs, bzs = [split(a) for a in z], [split(a) for a in bz]
    from_keys = [gates[h][3] * mm(us[h], as_[h], 1, 1) for h in both_heads]
    through = [mm(bzs[h], ss[h], 1, 1) for h in both_heads]
    e = [mm(cotangent[h], us[h], 1, 1) for h in both_heads]
    f = [mm(zs[h], us[h], 1, 1) for h in both_heads]
    e = [jnp.where(gates[h][0], e[h] * gates[h][1], 0.0) for h in both_heads]
    f = [jnp.where(ii > jj, f[h] * gates[h][1] * -gates[h][4], 0.0) for h in both_heads]
    key_side = [from_keys[h] - gates[h][2] * through[h] for h in both_heads]
    h_mat = [e[h] * qk + f[h] * gram for h in both_heads]
    by_row = [
        h_mat[h] + queries * from_out[h] + keys * (key_side[h] - 2.0 * from_keys[h])
        for h in both_heads
    ]
    zu = [z[h] * uhat[h] for h in both_heads]
    by_lane = jnp.zeros((C, C), F32)
    for i, t in enumerate((*by_row, *zu)):
        by_lane = jnp.where(jj == i, jnp.sum(t, axis=1, keepdims=True), by_lane)
    by_lane = by_lane.T
    dc, db = by_lane[0:2, :], by_lane[2:4, :]
    for h in both_heads:
        carry = gates[h][2]
        ends = keys * from_keys[h] + carry[C - 1 : C, :] * states[h] * adjoints[h]
        tail = jnp.sum(jnp.sum(ends, axis=0, keepdims=True), axis=1, keepdims=True)
        sums_ref[h : h + 1, :] = dc[h : h + 1, :] - jnp.sum(h_mat[h], axis=0, keepdims=True)
        sums_ref[2 + h : 3 + h, :] = db[h : h + 1, :]
        sums_ref[4 + h : 5 + h, :] = jnp.broadcast_to(tail, (1, C))
        dv_ref[:, h * C : (h + 1) * C] = bz[h].astype(BF16)
    e_ref[...] = e[0] + e[1]
    f_ref[...] = f[0] + f[1]
    query_side_ref[...] = from_out[0] + from_out[1]
    key_side_ref[...] = key_side[0] + key_side[1]
    dc, db, tail = sums_ref[0:2, :], sums_ref[2:4, :], sums_ref[4:6, :]
    dg = sum(dot(t, lower, 1, 0) for t in split3(dc)) + tail
    beta, log_decay = rows_ref[2:4, :], rows_ref[4:6, :]
    dz = dg * rows_ref[8:10, :] * jax.nn.sigmoid(rows_ref[6:8, :])
    own_ref[0:2, :] = dz
    own_ref[2:4, :] = db * beta * (1.0 - beta)
    own_ref[4:6, :] = jnp.broadcast_to(jnp.sum(dg * log_decay, axis=1, keepdims=True), (2, C))
    own_ref[6:8, :] = jnp.broadcast_to(jnp.sum(dz, axis=1, keepdims=True), (2, C))
    for i, t in enumerate(split3(own_ref[0:4, :])):
        terms_ref[4 * i : 4 * i + 4, :] = t.astype(F32)
    terms_ref[12:16, :] = jnp.zeros((4, C), F32)
    grad = dot(terms_ref[...].astype(BF16), hid_ref[...], 1, 0)
    grad = grad[0:4, :] + grad[4:8, :] + grad[8:12, :]
    for x in range(NX * NC):
        for i in range(PARTS):
            at = slice((PARTS * x + i) * C, (PARTS * x + i + 1) * C)
            share_ref[x, 4 * i : 4 * i + 4, :] = grad[:, at]
    send_ref[0:4, :] = own_ref[0:4, :]
    send_ref[4:8, :] = own_ref[0:4, :]
    bit = mine & 1
    for at in range(4):
        pair = weights_ref[2 * at], weights_ref[2 * at + 1]
        keep_ref[at] = jnp.where(bit == 0, pair[0], pair[1])
        send_ref[8 + 8 * at : 16 + 8 * at, :] = jnp.where(bit == 0, pair[1], pair[0])


def second_kernel(at_y_ref, got_ref, sent_ref, keep_ref, send_ref, kept_ref):
    bit = (at_y_ref[0] >> 1) & 1
    send_ref[0:4, :] = sent_ref[0:4, :]
    send_ref[4:8, :] = got_ref[0:4, :]
    for high in range(2):
        for low in range(2):
            place = 2 * high + low
            pair = (keep_ref[place], got_ref[8 + 8 * place : 16 + 8 * place, :])
            for source, rows in enumerate(pair):

                at = 2 * source + high

                @pl.when(bit == low)
                def _():
                    kept_ref[at] = rows

                @pl.when(bit != low)
                def _():
                    send_ref[8 + 8 * at : 16 + 8 * at, :] = rows


def third_kernel(at_y_ref, got_ref, sent_ref, keep_ref, send_ref, kept_ref):
    bit = (at_y_ref[0] >> 2) & 1
    send_ref[0:8, :] = sent_ref[0:8, :]
    send_ref[8:16, :] = got_ref[0:8, :]
    for source in range(4):
        for high in range(2):
            at = 2 * (source % 2) + high
            rows = keep_ref[at] if source < 2 else got_ref[8 + 8 * at : 16 + 8 * at, :]

            @pl.when(bit == high)
            def _():
                kept_ref[source] = rows

            @pl.when(bit != high)
            def _():
                send_ref[16 + 8 * source : 24 + 8 * source, :] = rows


def hidden_kernel(got_ref, sent_ref, keep_ref, _after_ref, hidden_ref, w_ref):
    for source in range(NY):
        for half in range(2):
            lanes, at = slice(half * C, (half + 1) * C), slice(4 * half, 4 * half + 4)
            if source < 4:
                rows = keep_ref[source, at, :]
            else:
                rows = got_ref[16 + 8 * (source - 4) + 4 * half : 20 + 8 * (source - 4) + 4 * half, :]
            w_ref[4 * source : 4 * source + 4, lanes] = rows
    logit_rows = jnp.concatenate([sent_ref[0:16, :], got_ref[0:16, :]], axis=0)
    weights = w_ref[...].astype(BF16)
    hidden = sum(dot(t, weights, 0, 0) for t in split3(logit_rows))
    hidden_ref[...] = hidden.astype(BF16)


def vector_kernel(k_ref, q_ref, e_ref, f_ref, query_side_ref, key_side_ref, dq_ref, dk_ref):
    keys, key_root = unit_rows(k_ref[...].astype(F32))
    unit_queries, query_root = unit_rows(q_ref[...].astype(F32))
    ks, qs = split(keys), split(unit_queries * SCALE)
    es, f = split(e_ref[...]), f_ref[...]
    dq = query_side_ref[...] + mm(es, ks)
    dk = key_side_ref[...] + mm(es, qs, 0, 0) + mm(split(f + f.T), ks)
    dq = dq - unit_queries * jnp.sum(unit_queries * dq, axis=-1, keepdims=True)
    dk = dk - keys * jnp.sum(keys * dk, axis=-1, keepdims=True)
    dq_ref[...] = (dq * (query_root * SCALE)).astype(BF16)
    dk_ref[...] = (dk * key_root).astype(BF16)


def sum_kernel(share_ref, own_ref, _send_ref, out_ref):
    total = share_ref[0]
    for x in range(1, NX * NC):
        total = total + share_ref[x]
    total, power = scaled(total)
    lane = lax.broadcasted_iota(jnp.int32, (1, C), 1) >> 5
    sums = own_ref[4:5, :]
    for i in range(1, 4):
        sums = jnp.where(lane == i, own_ref[4 + i : 5 + i, :], sums)
    powers = jnp.floor(jnp.log2(jnp.maximum(jnp.abs(sums), 1e-30)))
    fractions = sums * jnp.exp2(-powers)
    high = jnp.floor(fractions * 256.0) * (1.0 / 256.0)
    for i in range(PARTS):
        out_ref[:, i * C : (i + 1) * C] = total[4 * i : 4 * i + 4, :]
    out_ref[0:1, PARTS * C :] = jnp.broadcast_to(power, (1, C))
    out_ref[1:2, PARTS * C :] = powers
    out_ref[2:3, PARTS * C :] = high
    out_ref[3:4, PARTS * C :] = (fractions - high) * 256.0


def finish_kernel(parts_ref, wd_ref, wb_ref, after_ref, rate_ref, bias_ref):
    after_ref[...] = jnp.zeros_like(after_ref)
    sums = jnp.zeros((1, C), F32)
    for x in range(NX * NC):
        totals = [jnp.zeros((4, C), F32)] * PARTS
        for z in range(NZ):
            at = (x // NC * NZ + z) * NC + x % NC
            meta = parts_ref[at, :, PARTS * C :]
            scale = jnp.exp2(meta[0:1, :] - 13.0)
            totals = [t + parts_ref[at, :, i * C : (i + 1) * C] * scale for i, t in enumerate(totals)]
            sums = sums + (meta[2:3, :] + meta[3:4, :] * (1.0 / 256.0)) * jnp.exp2(meta[1:2, :])
        for i, total in enumerate(totals):
            at = slice((PARTS * x + i) * C, (PARTS * x + i + 1) * C)
            wd_ref[:, at] = total[0:2, :]
            wb_ref[:, at] = total[2:4, :]
    lane = lax.broadcasted_iota(jnp.int32, (1, C), 1)
    for i in range(2):
        rate_ref[i] = jnp.sum(jnp.where(lane == 32 * i, sums, 0.0))
        bias_ref[i] = jnp.sum(jnp.where(lane == 64 + 32 * i, sums, 0.0))


VMEM = pl.BlockSpec(memory_space=pltpu.VMEM)
SMEM = pl.BlockSpec(memory_space=pltpu.SMEM)
HBM = pl.BlockSpec(memory_space=pltpu.HBM)


def call(kernel, scalars, arrays, outs, scratch=(), space=VMEM, small=0, flops=0):
    if space is HBM:
        arrays = tuple(pltpu.with_memory_space_constraint(a, pltpu.HBM) for a in arrays)
    return pl.pallas_call(
        kernel,
        out_shape=tuple(jax.ShapeDtypeStruct(s, t) for s, t in outs),
        in_specs=[SMEM] * len(scalars) + [space] * len(arrays),
        out_specs=tuple([VMEM] * (len(outs) - small) + [SMEM] * small),
        scratch_shapes=list(scratch),
        compiler_params=pltpu.CompilerParams(vmem_limit_bytes=40 << 20),
        cost_estimate=pl.CostEstimate(flops=flops, bytes_accessed=1 << 20, transcendentals=0) if flops else None,
    )(*scalars, *arrays)


def exchange(a, axes):
    return lax.all_to_all(a, axes, 0, 0, tiled=True)


def spread(a, count, axes):
    a = jnp.broadcast_to(a.astype(F16), (count, *a.shape))
    return exchange(a, axes).astype(F32)


def swap(a, bit):
    return lax.ppermute(a, "dp", [(i, i ^ bit) for i in range(NY)])


def on_device(hidden, queries, keys, values, cotangent, w_decay, w_beta, rate, bias, doc_start):
    at_x = lax.axis_index("x").astype(jnp.int32)
    at_q = lax.axis_index("zq").astype(jnp.int32)
    at_p = lax.axis_index("zp").astype(jnp.int32)
    at_core = lax.axis_index("core").astype(jnp.int32)
    at_y = lax.axis_index("dp").astype(jnp.int32)
    first = (((at_x * NQ + at_q) * NP + at_p) * NC + at_core) * C
    at_x, at_y, at_q, at_p, first = (a[None] for a in (at_x, at_y, at_q, at_p, first))
    wd, wb = w_decay.T, w_beta.T
    square, heads, wide = (C, C), (HEADS, C, C), (C, HEADS * C)
    maps, uhat, what, z0, y, gram, qk, rows, weights = call(
        local_kernel,
        (first, at_x, at_y, at_q, at_p, doc_start),
        (rate, bias, keys, hidden, wd, wb, queries, values, cotangent),
        [((HEADS, MAP_ROWS, C), F32)] + [(heads, F32)] * 4 + [(square, F32)] * 2 + [((16, C), F32), ((NY, 8, C), F32)],
        [
            pltpu.SMEM((2,), F32),
            pltpu.SMEM((2,), F32),
            pltpu.VMEM(square, BF16),
            pltpu.VMEM((C, D), BF16),
            pltpu.VMEM((2, D), BF16),
            pltpu.VMEM((2, D), BF16),
            pltpu.VMEM(square, BF16),
            pltpu.VMEM(wide, BF16),
            pltpu.VMEM(wide, BF16),
            pltpu.SemaphoreType.DMA((9,)),
        ],
        HBM,
    )
    maps = exchange(maps, "core")
    (packed,) = call(pair_kernel, (), (maps,), [((MAP_ROWS, C), F32)])
    chips = spread(packed, NP, "zp")
    (packed,) = call(duo_kernel, (), (chips,), [((MAP_ROWS, C), F32)])
    ring = spread(packed, NQ, "zq")
    groups, near = call(
        ring_kernel, (at_x, at_q), (ring,), [((NX, 2 * C, C), F32), ((4 * C, C), F32)]
    )
    groups = exchange(groups.astype(F16), "x").astype(F32)
    (ends,) = call(
        entry_kernel,
        (at_x, at_p),
        (groups, near, chips, maps),
        [((NC, 2 * C, C), F32)],
        [pltpu.VMEM(square, F32), pltpu.VMEM(square, F32)],
    )
    ends = exchange(ends, "core")
    dv, e, f, query_side, key_side, share, own, send, keep = call(
        grad_kernel,
        (at_y,),
        (ends, hidden, keys, queries, cotangent, weights, uhat, what, z0, y, gram, qk, rows),
        [(wide, BF16)]
        + [(square, F32)] * 4
        + [((NX * NC, 4 * PARTS, C), F32), ((8, C), F32), ((40, C), F32), ((4, 8, C), F32)],
        [pltpu.VMEM((8, C), F32), pltpu.VMEM((16, C), F32)],
    )
    got = swap(send, 1)
    share = exchange(share, ("x", "core"))
    send, keep = call(second_kernel, (at_y,), (got, send, keep), [((40, C), F32), ((4, 8, C), F32)])
    got = swap(send, 2)
    (sums,) = call(sum_kernel, (), (share, own, send), [((4, (PARTS + 1) * C), F32)])
    parts = spread(sums, NX * NZ * NC, CTX)
    dq, dk = call(
        vector_kernel,
        (),
        (keys, queries, e, f, query_side, key_side),
        [(square, BF16), (square, BF16)],
        flops=1 << 28,
    )
    send, keep = call(third_kernel, (at_y,), (got, send, keep), [((48, C), F32), ((4, 8, C), F32)])
    got = swap(send, 4)
    wd_grad, wb_grad, after, rate_grad, bias_grad = call(
        finish_kernel,
        (),
        (parts,),
        [((2, D), F32), ((2, D), F32), ((8, C), F32), ((HEADS,), F32), ((HEADS,), F32)],
        small=2,
    )
    (hidden_grad,) = call(
        hidden_kernel,
        (),
        (got, send, keep, after),
        [(wide, BF16)],
        [pltpu.VMEM((4 * NY, 2 * C), F32)],
        flops=1 << 28,
    )
    return (dq, dk, dv, hidden_grad, wd_grad.T, wb_grad.T, rate_grad, bias_grad)


def solution(mesh):
    fine = Mesh(mesh.devices.reshape(NX, NQ, NP, NC, NY), (*CTX, "dp"))
    rows, both, cols = P(CTX, None), P(CTX, "dp"), P(None, "dp")
    return jax.shard_map(
        on_device,
        mesh=fine,
        in_specs=(rows, both, both, both, both, cols, cols, P("dp"), P("dp"), P()),
        out_specs=(both, both, both, both, cols, cols, P("dp"), P("dp")),
        check_vma=False,
    )
```
